32 devices in a mesh: lat: 8 (over z, x), lev: 4 (over y, core).
Axes of the slice: x: 2, y: 2, z: 4, core: 2. Of those that a mesh axis runs over, the one named last changes fastest.
Arguments:
- grid_field: bfloat16 [8, 1280, 128], P('lev', 'lat'), may hold values from -6 to 6
- send_blocks: int32 [8, 2, 32], P('lat'), may hold values from 0 to 159
- donor_index: int32 [1280, 2], P('lat'), may hold values from 0 to 223
- tile_choice: int32 [1280, 2], P('lat'), may hold values from 0 to 7
- kernel_tiles: bfloat16 [8, 128, 128], replicated, may hold values from -0.375 to 0.375
- circle_len: int32 [32], replicated, may hold values from 20 to 5120, as said below
- slot_wave: int32 [1280], replicated, may hold values from 0 to 1279, each once
- legendre: bfloat16 [1280, 32, 1280], P(('lat', 'lev')), may hold values from -0.01171875 to 0.01171875
Outputs:
- spectra: bfloat16 [8, 2, 1280, 1280], P(None, None, ('lat', 'lev'))
The draws below stay inside these ranges and needn't reach their ends.
Inputs may be any that keep to these rules, and one draw needn't show every extreme that they name: `circle_len`: each circle has 4 i + 16 points for a whole i of 1 or more, and some circle has 5120.
All inputs are finite; a program needn't handle non-finite values.
Results may differ from the reference program's by a relative error of at most 0.007.
Values may be sent and summed in bfloat16 or wider, within the bound.
No kernel may reach another device: no remote copies, remote signals or barrier semaphores. Data moves between devices by JAX's collectives and lax.ppermute only.
A program may use at most 64 MiB of HBM per device.

```python
import math
import jax
import jax.numpy as jnp
from jax import lax

PTS = 5120
NW = 1280
KT = 8
BANDS = 8
LEVELS = 8
CIRCLES_PER_BAND = 4
CAP = 32
CIRCLES = 32
BAND_BLOCKS = 160
MSLOTS = 1280


def draw_circle_len(key, part):
    base_key = jax.random.fold_in(key, 17)
    key_step, key_widest = jax.random.split(base_key)
    top_step = (PTS - 16) // 4
    latitude_step = jax.random.randint(key_step, (CIRCLES,), 1, top_step + 1)
    widest = jax.random.randint(key_widest, (), 0, CIRCLES)
    lengths = 4 * latitude_step + 16
    return jnp.where(jnp.arange(CIRCLES) == widest, 4 * top_step + 16, lengths).astype(jnp.int32)


def touch_ends(values, rng, low, high):
    spot = [jax.random.randint(jax.random.fold_in(rng, axis), (), 0, length) for axis, length in enumerate(values.shape)]
    widest = values.shape.index(max(values.shape))
    beside = spot[:widest] + [(spot[widest] + 1) % values.shape[widest]] + spot[widest + 1:]
    return values.at[tuple(spot)].set(low).at[tuple(beside)].set(high)


def block_scale(rng, shape, cuts, least, high):
    factor_of, own = 1.0, jax.random.fold_in(rng, 6)
    for dim, blocks in cuts:
        steps = jnp.exp(jax.random.uniform(jax.random.fold_in(own, dim), (blocks,), jnp.float32, least / len(cuts), high / len(cuts)))
        factor_of = factor_of * jnp.repeat(steps, shape[dim] // blocks).reshape([-1 if axis == dim else 1 for axis in range(len(shape))])
    return factor_of


def scatter_about(stream_key, shape, deviation, limit, cuts=(), kind=jnp.bfloat16):
    gain = block_scale(stream_key, shape, cuts, -0.22, 0.18) if cuts else 1.0
    array = jax.random.normal(stream_key, shape, jnp.float32) * deviation * gain
    return jnp.minimum(jnp.maximum(array, -limit), limit).astype(kind)


def setup_inputs(seed: int = 0) -> dict:
    key_of = jax.random.split(jax.random.key(seed), 9)
    return {
        "grid_field": scatter_about(key_of[0], (LEVELS, CIRCLES * PTS // 128, 128), 1.0, 6.0, ((0, 4), (1, 8))),
        "send_blocks": touch_ends(jax.random.randint(key_of[1], (BANDS, 2, CAP), 0, BAND_BLOCKS), jax.random.fold_in(key_of[1], 1), 0, BAND_BLOCKS - 1).astype(jnp.int32),
        "donor_index": touch_ends(jax.random.randint(key_of[2], (CIRCLES * PTS // 128, 2), 0, BAND_BLOCKS + 2 * CAP), jax.random.fold_in(key_of[2], 1), 0, (BAND_BLOCKS + 2 * CAP) - 1).astype(jnp.int32),
        "tile_choice": touch_ends(jax.random.randint(key_of[3], (CIRCLES * PTS // 128, 2), 0, KT), jax.random.fold_in(key_of[3], 1), 0, KT - 1).astype(jnp.int32),
        "kernel_tiles": scatter_about(key_of[4], (KT, 128, 128), 256 ** -0.5, 0.375),
        "circle_len": draw_circle_len(jax.random.fold_in(key_of[8], 71), 0),
        "slot_wave": jax.random.permutation(key_of[6], MSLOTS).astype(jnp.int32),
        "legendre": scatter_about(key_of[7], (MSLOTS, CIRCLES, NW), (3 * CIRCLES * PTS // 2) ** -0.5, 0.01171875, ((0, 32),)),
    }


def circle_table(length, waves, points, top_wave):
    live_slot = (waves >= 1) & (waves < top_wave) & (2 * waves < length)
    step_angle = (2.0 * math.pi) / length.astype(jnp.float32)
    phases = (jnp.arange(points, dtype=jnp.int32)[:, None] * waves[None, :]) % length
    angles = phases.astype(jnp.float32) * step_angle
    keep_mask = (jnp.arange(points, dtype=jnp.int32) < length)[:, None] & live_slot[None, :]
    cosine = jnp.where(keep_mask, jnp.cos(angles), 0.0)
    sine_part = jnp.where(keep_mask, -jnp.sin(angles), 0.0)
    return jnp.concatenate([cosine, sine_part], axis=1).astype(jnp.bfloat16)


def reference(grid_field, send_blocks, donor_index, tile_choice, kernel_tiles, circle_len, slot_wave, legendre):
    bands = grid_field.reshape(LEVELS, BANDS, BAND_BLOCKS, 128)
    donor_band = donor_index.reshape(BANDS, BAND_BLOCKS, 2)
    tile_band = tile_choice.reshape(BANDS, BAND_BLOCKS, 2)
    kernels = kernel_tiles.astype(jnp.float32)

    def one_band(band):
        own = lax.dynamic_index_in_dim(bands, band, 1, keepdims=False)
        below = jnp.maximum(band - 1, 0).astype(jnp.int32)
        above = jnp.minimum(band + 1, BANDS - 1).astype(jnp.int32)
        from_below = jnp.take(lax.dynamic_index_in_dim(bands, below, 1, keepdims=False), send_blocks[below, 1], axis=1)
        from_above = jnp.take(lax.dynamic_index_in_dim(bands, above, 1, keepdims=False), send_blocks[above, 0], axis=1)
        from_below = jnp.where(band > 0, from_below, jnp.zeros_like(from_below))
        from_above = jnp.where(band < BANDS - 1, from_above, jnp.zeros_like(from_above))
        donor_pool = jnp.concatenate([own, from_below, from_above], axis=1)
        picked = jnp.take(donor_pool, donor_band[band].reshape(-1), axis=1)
        picked = picked.reshape(LEVELS, BAND_BLOCKS, 2, 128).astype(jnp.float32)
        weights = kernels[tile_band[band]]
        arrival = jnp.einsum("lbkc,bkcd->lbd", picked, weights, precision=lax.Precision.HIGHEST)
        return (arrival * arrival).astype(jnp.bfloat16)

    squared = lax.map(one_band, jnp.arange(BANDS, dtype=jnp.int32))
    squared = squared.reshape(BANDS, LEVELS, CIRCLES_PER_BAND, PTS).transpose(1, 0, 2, 3).reshape(LEVELS, CIRCLES, PTS)

    def one_circle(operands):
        values, length = operands
        factors = circle_table(length, slot_wave, PTS, NW).astype(jnp.float32)
        grand_total = jnp.dot(values.astype(jnp.float32), factors, precision=lax.Precision.HIGHEST, preferred_element_type=jnp.float32)
        return grand_total.astype(jnp.bfloat16)

    coeffs = lax.map(one_circle, (jnp.moveaxis(squared, 1, 0), circle_len))
    coeffs = coeffs.reshape(CIRCLES, LEVELS, 2, MSLOTS).transpose(3, 0, 1, 2)
    wave_all = jnp.arange(NW, dtype=jnp.int32)

    def one_slot(operands):
        block_piece, lookup_table_rows, wave = operands
        grand_total = jnp.einsum("ump,uv->mpv", block_piece.astype(jnp.float32), lookup_table_rows.astype(jnp.float32), precision=lax.Precision.HIGHEST)
        return jnp.where(wave_all[None, None, :] >= wave, grand_total, 0.0).astype(jnp.bfloat16)

    spectra = lax.map(one_slot, (coeffs, legendre, slot_wave))
    return spectra.transpose(1, 2, 0, 3)
```

```python
import functools
import math

import jax
import jax.numpy as jnp
from jax import lax
from jax.experimental import pallas as pl
from jax.experimental.pallas import tpu as pltpu
from jax.sharding import PartitionSpec as P

PTS = 5120
LANES = 128
BF16 = jnp.bfloat16
F32 = jnp.float32
VMEM = pl.BlockSpec(memory_space=pltpu.VMEM)
SMEM = pl.BlockSpec(memory_space=pltpu.SMEM)
CONTRACT_ROWS = (((0,), (0,)), ((), ()))


def params(mebibytes):
    return pltpu.CompilerParams(vmem_limit_bytes=mebibytes << 20)


def one_hot(condition):
    return jnp.where(condition, 1.0, 0.0).astype(BF16)


def side_by_side(field_ref):
    return jnp.concatenate([field_ref[l] for l in range(field_ref.shape[0])], axis=1)


def outgoing_kernel(send_ref, field_ref, first_ref, second_ref):
    even = lax.rem(lax.axis_index("lat"), 2) == 0
    own = side_by_side(field_ref)
    blocks, count = own.shape[0], send_ref.shape[2]
    rows = lax.broadcasted_iota(jnp.int32, (blocks, count), 0)
    below, above = send_ref[0, 0:1, :], send_ref[0, 1:2, :]
    for ref, listed in (
        (first_ref, jnp.where(even, above, below)),
        (second_ref, jnp.where(even, below, above)),
    ):
        picked = lax.dot_general(
            one_hot(rows == listed), own, CONTRACT_ROWS, preferred_element_type=F32
        )
        ref[...] = picked.astype(BF16)


def turn(steps, waves, length, inverse):
    phase = steps * waves
    rest = phase - jnp.round(phase * inverse) * length
    f = rest * inverse
    x = f * f
    s = math.pi ** 11 / -math.factorial(11)
    for k in (9, 7, 5, 3, 1):
        s = s * x + (-1) ** (k // 2) * math.pi**k / math.factorial(k)
    s = s * f
    c = math.pi ** 10 / -math.factorial(10)
    for k in (8, 6, 4, 2, 0):
        c = c * x + (-1) ** (k // 2) * math.pi**k / math.factorial(k)
    return 1.0 - 2.0 * (s * s), 2.0 * (s * c)


def times(a, b):
    return a[0] * b[0] - a[1] * b[1], a[0] * b[1] + a[1] * b[0]


def table_kernel(length_ref, wave_ref, fine_ref, coarse_ref):
    circles, tiles = fine_ref.shape[:2]
    coarse = coarse_ref.shape[2]
    band = lax.axis_index("lat")
    step = lax.broadcasted_iota(jnp.int32, (8, LANES), 0).astype(F32)

    def doubled(base, factor_of, groups):
        out = [base]
        while len(out) < groups:
            out += [times(e, factor_of(len(out))) for e in out[: groups - len(out)]]
        return out

    def one(index, _):
        g, t = index // tiles, lax.rem(index, tiles)
        length = jnp.full((8, LANES), length_ref[band * circles + g], jnp.int32).astype(F32)
        inverse = 1.0 / length
        waves = jnp.broadcast_to(wave_ref[pl.ds(t, 1), :], (8, LANES)).astype(F32)
        hop_steps = jnp.left_shift(8, lax.broadcasted_iota(jnp.int32, (8, LANES), 0)).astype(F32)
        hops = turn(hop_steps, waves, length, inverse)
        far = turn(hop_steps * float(LANES), waves, length, inverse)

        def hop(table):
            def factor(groups):
                k = groups.bit_length() - 1
                return tuple(jnp.broadcast_to(x[k : k + 1], (8, LANES)) for x in table)

            return factor

        fine = doubled(turn(step, waves, length, inverse), hop(hops), LANES // 8)
        fine_ref[g, t] = jnp.concatenate(
            [jnp.concatenate([e[p] for e in fine], axis=0) for p in range(2)], axis=1
        ).astype(BF16)
        wide = doubled(turn(step * float(LANES), waves, length, inverse), hop(far), coarse // 8)
        coarse_ref[g, t] = jnp.concatenate(
            [jnp.concatenate([e[p] for e in wide], axis=0) for p in range(2)], axis=1
        )
        return 0

    lax.fori_loop(0, circles * tiles, one, 0, unroll=2)


def transform_kernel(
    length_ref, donor_ref, tile_ref, field_ref, first_ref, second_ref, kernels_ref, wave_ref,
    fine_ref, coarse_ref, out_ref, points_ref, coeff_ref, *, top_wave,
):
    levels, blocks = field_ref.shape[:2]
    circles, tiles = fine_ref.shape[:2]
    coarse = coarse_ref.shape[2]
    kinds = kernels_ref.shape[0]
    band = lax.axis_index("lat")
    even = lax.rem(band, 2) == 0

    first, second = first_ref[...], second_ref[...]
    below, above = jnp.where(even, second, first), jnp.where(even, first, second)
    pool = jnp.concatenate([side_by_side(field_ref), below, above], axis=0)

    listed = jnp.concatenate(
        [donor_ref[...], tile_ref[...], jnp.zeros((4, blocks), jnp.int32)], axis=0
    )
    columns = jnp.transpose(listed.astype(F32))
    lane = lax.broadcasted_iota(jnp.int32, (blocks, pool.shape[0]), 1).astype(F32)
    stacked = jnp.concatenate([kernels_ref[k] for k in range(kinds)], axis=1)
    arrival = [jnp.zeros((blocks, LANES), F32) for _ in range(levels)]
    for k in range(2):
        picked = jnp.dot(
            one_hot(lane == columns[:, k : k + 1]), pool, preferred_element_type=F32
        ).astype(BF16)
        kind = jnp.broadcast_to(columns[:, 2 + k : 3 + k], (blocks, LANES))
        for l in range(levels):
            every = jnp.dot(
                picked[:, l * LANES : (l + 1) * LANES], stacked, preferred_element_type=F32
            )
            value = every[:, :LANES]
            for q in range(1, kinds):
                value = jnp.where(kind == float(q), every[:, q * LANES : (q + 1) * LANES], value)
            arrival[l] = arrival[l] + value

    position = lax.broadcasted_iota(jnp.int32, (coarse, LANES), 0) * LANES
    position = position + lax.broadcasted_iota(jnp.int32, (coarse, LANES), 1)
    for g in range(circles):
        inside = position < length_ref[band * circles + g]
        for l in range(levels):
            part = arrival[l][g * coarse : (g + 1) * coarse]
            points_ref[g, l * coarse : (l + 1) * coarse] = jnp.where(inside, part * part, 0.0)

    def circle(g, _):
        length = length_ref[band * circles + g]
        points = points_ref[g].astype(BF16)
        for t in range(tiles):
            near = jnp.dot(points, fine_ref[g, t], preferred_element_type=F32)
            c, s = coarse_ref[g, t, :, :LANES], coarse_ref[g, t, :, LANES:]
            waves = wave_ref[t : t + 1, :]
            live = (waves >= 1) & (waves < top_wave) & (2 * waves < length)
            for l in range(levels):
                here = near[l * coarse : (l + 1) * coarse]
                a, b = here[:, :LANES], here[:, LANES:]
                real = jnp.sum(a * c - b * s, axis=0, keepdims=True)
                imag = jnp.sum(a * s + b * c, axis=0, keepdims=True)
                for part, value in ((0, real), (1, -imag)):
                    row = (l * 2 + part) * circles + g
                    coeff_ref[t, pl.ds(row, 1), :LANES] = jnp.where(live, value, 0.0)
        return 0

    lax.fori_loop(0, circles, circle, 0, unroll=circles * tiles <= 64)

    devices, height, _ = out_ref.shape
    width = tiles * LANES // devices
    packs = coeff_ref.shape[1] // height
    step = LANES // packs
    lane = lax.broadcasted_iota(jnp.int32, (height, LANES), 1)
    for d in range(devices):
        t, shift = divmod(d * width, LANES)
        chunk = jnp.zeros((height, LANES), F32)
        for p in range(packs):
            rows = slice(p * height, (p + 1) * height)
            at = p * step
            value = pltpu.roll(coeff_ref[t, rows, :LANES], (at - shift) % LANES, 1)
            if shift + width > LANES:
                after = pltpu.roll(coeff_ref[t + 1, rows, :LANES], (at - shift) % LANES, 1)
                value = jnp.where(lane < at + LANES - shift, value, after)
            chunk = value if p == 0 else jnp.where(lane < at, chunk, value)
        out_ref[d] = chunk.astype(BF16)


def legendre_kernel(wave_ref, arrived_ref, legendre_ref, out_ref, *, lat, lev, packs):
    outputs, slots, top_wave = out_ref.shape
    circles = legendre_ref.shape[0] // slots
    own = circles // lat
    per_tile = LANES // circles
    device = lax.axis_index("lat") * lev + lax.axis_index("lev")

    total = arrived_ref.shape[0]
    row = lax.broadcasted_iota(jnp.int32, (total, total), 0)
    col = lax.broadcasted_iota(jnp.int32, (total, total), 1)
    log = lambda n: n.bit_length() - 1
    inner = row & (own - 1)
    group = (row >> log(own)) & (2 * lev - 1)
    outer = row >> log(own * 2 * lev)
    target = (group << log(circles)) | (outer << log(own)) | inner
    turned = lax.dot_general(
        arrived_ref[...], one_hot(col == target), CONTRACT_ROWS, preferred_element_type=F32
    )

    sub = lax.broadcasted_iota(jnp.int32, (8, LANES), 0)
    block = lax.broadcasted_iota(jnp.int32, (8, LANES), 1) >> log(circles)
    chosen = [(block == b) & ((sub & (per_tile - 1)) == b) for b in range(per_tile)]
    halves = 8 // per_tile
    in_half = [(sub >> log(per_tile)) == h for h in range(halves)]
    step = LANES // packs
    spread, limits = [], []
    for k in range(slots // 8):
        pieces = [None] * outputs
        for l in range(packs):
            for j in range(total // LANES):
                at = l * step + 8 * k
                v = turned[at : at + 8, j * LANES : (j + 1) * LANES]
                rolled = [v] + [pltpu.roll(v, circles * d, 1) for d in range(1, per_tile)]
                for i in range(per_tile):
                    a = jnp.zeros((8, LANES), F32)
                    for b in range(per_tile):
                        a = jnp.where(chosen[b], rolled[(b - i) % per_tile], a)
                    group_lev, part = divmod(j * per_tile + i, 2)
                    pieces[(group_lev * packs + l) * 2 + part] = jnp.concatenate(
                        [jnp.where(in_half[h], a, 0.0) for h in range(halves)], axis=1
                    )
        spread.append(jnp.concatenate(pieces, axis=0).astype(BF16))
        limit = jnp.zeros((8, LANES), jnp.int32)
        for s in range(8):
            limit = jnp.where(sub == s, wave_ref[device * slots + 8 * k + s], limit)
        limits.append(limit)

    wide = 2 * LANES
    lane = lax.broadcasted_iota(jnp.int32, (8, wide), 1)
    for n in range(0, top_wave, wide):
        sums = [
            jnp.dot(
                spread[k],
                legendre_ref[8 * k * circles : 8 * (k + 1) * circles, n : n + wide],
                preferred_element_type=F32,
            )
            for k in range(slots // 8)
        ]
        keep = [lane + n >= jnp.concatenate([m, m], axis=1) for m in limits]
        for o in range(outputs):
            out_ref[o, :, n : n + wide] = jnp.concatenate(
                [jnp.where(keep[k], sums[k][8 * o : 8 * o + 8], 0.0) for k in range(slots // 8)],
                axis=0,
            ).astype(BF16)


def other_neighbours(size):
    pairs = [(i, i + 1) for i in range(1, size - 1, 2)]
    return pairs + [(j, i) for i, j in pairs]


def body(
    grid_field, send_blocks, donor_index, tile_choice, kernel_tiles, circle_len, slot_wave, legendre
):
    levels, blocks, _ = grid_field.shape
    send_count = send_blocks.shape[2]
    slots, circles, top_wave = legendre.shape
    lat, lev = lax.axis_size("lat"), lax.axis_size("lev")
    devices = lat * lev
    coarse = PTS // LANES
    own = blocks // coarse
    tiles = slot_wave.shape[0] // LANES
    waves = slot_wave.reshape(tiles, LANES)

    halo = jax.ShapeDtypeStruct((send_count, levels * LANES), BF16)
    to_first, to_second = pl.pallas_call(
        outgoing_kernel, out_shape=(halo, halo), in_specs=[VMEM] * 2, out_specs=(VMEM, VMEM),
        compiler_params=params(4), name="outgoing",
    )(send_blocks, grid_field)
    first = lax.ppermute(to_first, "lat", [(i, i ^ 1) for i in range(lat)])
    second = lax.ppermute(to_second, "lat", other_neighbours(lat))

    entries = own * tiles * (LANES + coarse) * 2 * LANES
    fine, wide = pl.pallas_call(
        table_kernel,
        out_shape=(
            jax.ShapeDtypeStruct((own, tiles, LANES, 2 * LANES), BF16),
            jax.ShapeDtypeStruct((own, tiles, coarse, 2 * LANES), F32),
        ),
        in_specs=[SMEM, VMEM], out_specs=(VMEM, VMEM), compiler_params=params(26), name="tables",
        cost_estimate=pl.CostEstimate(flops=8 * entries, bytes_accessed=3 * entries, transcendentals=0),
    )(circle_len, waves)

    rows = levels * 2 * own
    packs = 1
    while rows % (16 * packs) == 0 and 2 * packs * slots <= LANES:
        packs *= 2
    coeffs = pl.pallas_call(
        functools.partial(transform_kernel, top_wave=top_wave),
        out_shape=jax.ShapeDtypeStruct((devices, rows // packs, LANES), BF16),
        in_specs=[SMEM] + [VMEM] * 9, out_specs=VMEM,
        scratch_shapes=[
            pltpu.VMEM((own, levels * coarse, LANES), F32),
            pltpu.VMEM((tiles, rows, LANES), F32),
        ],
        compiler_params=params(40), name="transform",
    )(
        circle_len, donor_index.T, tile_choice.T, grid_field, first, second, kernel_tiles, waves,
        fine, wide,
    )
    arrived = lax.all_to_all(coeffs, ("lat", "lev"), 0, 0, tiled=True)

    outputs = lev * levels * 2
    height = rows // packs
    if packs == levels and height == 2 * own == 8 and LANES == 4 * circles and slots % 8 == 0:
        spectra = pl.pallas_call(
            functools.partial(legendre_kernel, lat=lat, lev=lev, packs=packs),
            out_shape=jax.ShapeDtypeStruct((outputs, slots, top_wave), BF16),
            in_specs=[SMEM, VMEM, VMEM], out_specs=VMEM, compiler_params=params(32), name="legendre",
        )(
            slot_wave,
            arrived.reshape(devices * height, LANES),
            legendre.reshape(slots * circles, top_wave),
        )
        return spectra.reshape(outputs // 2, 2, slots, top_wave)

    gathered = arrived.reshape(lat, lev, height, packs, LANES // packs)[..., :slots]
    gathered = gathered.swapaxes(2, 3).reshape(lat, lev, levels, 2, own, slots)
    gathered = gathered.transpose(1, 2, 3, 0, 4, 5).reshape(outputs // 2, 2, circles, slots)
    spectra = jnp.einsum("lcgs,sgn->lcsn", gathered, legendre, preferred_element_type=F32)
    first_slot = (lax.axis_index("lat") * lev + lax.axis_index("lev")) * slots
    mine = lax.dynamic_slice_in_dim(slot_wave, first_slot, slots)
    allowed = jnp.arange(top_wave, dtype=jnp.int32)[None, :] >= mine[:, None]
    return jnp.where(allowed[None, None], spectra, 0.0).astype(BF16)


def solution(mesh):
    return jax.shard_map(
        body,
        mesh=mesh,
        in_specs=(
            P("lev", "lat", None),
            P("lat", None, None),
            P("lat", None),
            P("lat", None),
            P(),
            P(),
            P(),
            P(("lat", "lev"), None, None),
        ),
        out_specs=P(None, None, ("lat", "lev"), None),
        check_vma=False,
    )
```

```python
import functools
import math

import jax
import jax.numpy as jnp
from jax import lax
from jax.experimental import pallas as pl
from jax.experimental.pallas import tpu as pltpu
from jax.sharding import PartitionSpec as P

PTS = 5120
LANES = 128
BF16 = jnp.bfloat16
F32 = jnp.float32
VMEM = pl.BlockSpec(memory_space=pltpu.VMEM)
HBM = pl.BlockSpec(memory_space=pltpu.HBM)
CONTRACT_ROWS = (((0,), (0,)), ((), ()))


def params(mebibytes):
    return pltpu.CompilerParams(vmem_limit_bytes=mebibytes << 20)


def one_hot(condition):
    return jnp.where(condition, 1.0, 0.0).astype(BF16)


def side_by_side(field_ref):
    return jnp.concatenate([field_ref[l] for l in range(field_ref.shape[0])], axis=1)


def outgoing_kernel(
    send_hbm, field_hbm, length_hbm, donor_hbm, tile_hbm, kernels_hbm, wave_hbm,
    first_ref, second_ref, field_ref, lengths_ref, donor_ref, tile_ref, kernels_ref, wave_ref,
    send_ref, length_ref, sems,
):
    copies = [
        pltpu.make_async_copy(source, target, sems.at[i])
        for i, (source, target) in enumerate(
            (
                (send_hbm, send_ref),
                (field_hbm, field_ref),
                (length_hbm, length_ref),
                (donor_hbm, donor_ref),
                (tile_hbm, tile_ref),
                (kernels_hbm, kernels_ref),
                (wave_hbm, wave_ref),
            )
        )
    ]
    for copy in copies:
        copy.start()
    copies[0].wait()
    copies[1].wait()
    band = lax.axis_index("lat")
    even = lax.rem(band, 2) == 0
    own = side_by_side(field_ref)
    blocks, count = own.shape[0], send_ref.shape[2]
    rows = lax.broadcasted_iota(jnp.int32, (blocks, count), 0)
    below, above = send_ref[0, 0:1, :], send_ref[0, 1:2, :]
    for ref, listed in (
        (first_ref, jnp.where(even, above, below)),
        (second_ref, jnp.where(even, below, above)),
    ):
        picked = lax.dot_general(
            one_hot(rows == listed), own, CONTRACT_ROWS, preferred_element_type=F32
        )
        ref[...] = picked.astype(BF16)
    copies[2].wait()
    circles = lengths_ref.shape[0]
    for g in range(circles):
        lengths_ref[g] = jnp.full((8, LANES), length_ref[band * circles + g], jnp.int32)
    for copy in copies[3:]:
        copy.wait()


def turn(steps, waves, length, inverse):
    phase = steps * waves
    rest = phase - jnp.round(phase * inverse) * length
    f = rest * inverse
    x = f * f
    s = math.pi ** 11 / -math.factorial(11)
    for k in (9, 7, 5, 3, 1):
        s = s * x + (-1) ** (k // 2) * math.pi**k / math.factorial(k)
    s = s * f
    c = math.pi ** 10 / -math.factorial(10)
    for k in (8, 6, 4, 2, 0):
        c = c * x + (-1) ** (k // 2) * math.pi**k / math.factorial(k)
    return 1.0 - 2.0 * (s * s), 2.0 * (s * c)


def times(a, b):
    return a[0] * b[0] - a[1] * b[1], a[0] * b[1] + a[1] * b[0]


def table_kernel(lengths_ref, wave_ref, slot_hbm, fine_ref, coarse_ref, limits_ref, slot_ref, sem, *, lev):
    circles, tiles = fine_ref.shape[:2]
    coarse = coarse_ref.shape[2]
    fetch = pltpu.make_async_copy(slot_hbm, slot_ref, sem)
    fetch.start()
    step = lax.broadcasted_iota(jnp.int32, (8, LANES), 0).astype(F32)

    def doubled(base, factor_of, groups):
        out = [base]
        while len(out) < groups:
            out += [times(e, factor_of(len(out))) for e in out[: groups - len(out)]]
        return out

    def one(index, _):
        g, t = index // tiles, lax.rem(index, tiles)
        length = lengths_ref[g].astype(F32)
        inverse = 1.0 / length
        waves = jnp.broadcast_to(wave_ref[pl.ds(t, 1), :], (8, LANES)).astype(F32)
        hop_steps = jnp.left_shift(8, lax.broadcasted_iota(jnp.int32, (8, LANES), 0)).astype(F32)
        hops = turn(hop_steps, waves, length, inverse)
        far = turn(hop_steps * float(LANES), waves, length, inverse)

        def hop(table):
            def factor(groups):
                k = groups.bit_length() - 1
                return tuple(jnp.broadcast_to(x[k : k + 1], (8, LANES)) for x in table)

            return factor

        fine = doubled(turn(step, waves, length, inverse), hop(hops), LANES // 8)
        fine_ref[g, t] = jnp.concatenate(
            [jnp.concatenate([e[p] for e in fine], axis=0) for p in range(2)], axis=1
        ).astype(BF16)
        wide = doubled(turn(step * float(LANES), waves, length, inverse), hop(far), coarse // 8)
        coarse_ref[g, t] = jnp.concatenate(
            [jnp.concatenate([e[p] for e in wide], axis=0) for p in range(2)], axis=1
        )
        return 0

    lax.fori_loop(0, circles * tiles, one, 0, unroll=2)

    fetch.wait()
    slots = limits_ref.shape[0]
    first = (lax.axis_index("lat") * lev + lax.axis_index("lev")) * slots
    for s in range(slots):
        limits_ref[s : s + 1] = jnp.full((1, LANES), slot_ref[first + s], jnp.int32)


def transform_kernel(
    lengths_ref, donor_ref, tile_ref, field_ref, first_ref, second_ref, kernels_ref, wave_ref,
    fine_ref, coarse_ref, out_ref, points_ref, coeff_ref, *, top_wave,
):
    levels, blocks = field_ref.shape[:2]
    circles, tiles = fine_ref.shape[:2]
    coarse = coarse_ref.shape[2]
    kinds = kernels_ref.shape[0]
    even = lax.rem(lax.axis_index("lat"), 2) == 0

    first, second = first_ref[...], second_ref[...]
    below, above = jnp.where(even, second, first), jnp.where(even, first, second)
    pool = jnp.concatenate([side_by_side(field_ref), below, above], axis=0)

    listed = jnp.concatenate(
        [donor_ref[...], tile_ref[...], jnp.zeros((4, blocks), jnp.int32)], axis=0
    )
    columns = jnp.transpose(listed.astype(F32))
    lane = lax.broadcasted_iota(jnp.int32, (blocks, pool.shape[0]), 1).astype(F32)
    stacked = jnp.concatenate([kernels_ref[k] for k in range(kinds)], axis=1)
    arrival = [jnp.zeros((blocks, LANES), F32) for _ in range(levels)]
    for k in range(2):
        picked = jnp.dot(
            one_hot(lane == columns[:, k : k + 1]), pool, preferred_element_type=F32
        ).astype(BF16)
        kind = jnp.broadcast_to(columns[:, 2 + k : 3 + k], (blocks, LANES))
        for l in range(levels):
            every = jnp.dot(
                picked[:, l * LANES : (l + 1) * LANES], stacked, preferred_element_type=F32
            )
            value = every[:, :LANES]
            for q in range(1, kinds):
                value = jnp.where(kind == float(q), every[:, q * LANES : (q + 1) * LANES], value)
            arrival[l] = arrival[l] + value

    position = lax.broadcasted_iota(jnp.int32, (coarse, LANES), 0) * LANES
    position = position + lax.broadcasted_iota(jnp.int32, (coarse, LANES), 1)
    for g in range(circles):
        inside = position < jnp.broadcast_to(lengths_ref[g, 0:1], (coarse, LANES))
        for l in range(levels):
            part = arrival[l][g * coarse : (g + 1) * coarse]
            points_ref[g, l * coarse : (l + 1) * coarse] = jnp.where(inside, part * part, 0.0)

    def circle(g, _):
        length = lengths_ref[g, 0:1]
        points = points_ref[g].astype(BF16)
        for t in range(tiles):
            near = jnp.dot(points, fine_ref[g, t], preferred_element_type=F32)
            c, s = coarse_ref[g, t, :, :LANES], coarse_ref[g, t, :, LANES:]
            waves = wave_ref[t : t + 1, :]
            live = (waves >= 1) & (waves < top_wave) & (2 * waves < length)
            for l in range(levels):
                here = near[l * coarse : (l + 1) * coarse]
                a, b = here[:, :LANES], here[:, LANES:]
                real = jnp.sum(a * c - b * s, axis=0, keepdims=True)
                imag = jnp.sum(a * s + b * c, axis=0, keepdims=True)
                for part, value in ((0, real), (1, -imag)):
                    row = (l * 2 + part) * circles + g
                    coeff_ref[t, pl.ds(row, 1), :LANES] = jnp.where(live, value, 0.0)
        return 0

    lax.fori_loop(0, circles, circle, 0, unroll=circles * tiles <= 64)

    devices, height, _ = out_ref.shape
    width = tiles * LANES // devices
    packs = coeff_ref.shape[1] // height
    step = LANES // packs
    lane = lax.broadcasted_iota(jnp.int32, (height, LANES), 1)
    for d in range(devices):
        t, shift = divmod(d * width, LANES)
        chunk = jnp.zeros((height, LANES), F32)
        for p in range(packs):
            rows = slice(p * height, (p + 1) * height)
            at = p * step
            value = pltpu.roll(coeff_ref[t, rows, :LANES], (at - shift) % LANES, 1)
            if shift + width > LANES:
                after = pltpu.roll(coeff_ref[t + 1, rows, :LANES], (at - shift) % LANES, 1)
                value = jnp.where(lane < at + LANES - shift, value, after)
            chunk = value if p == 0 else jnp.where(lane < at, chunk, value)
        out_ref[d] = chunk.astype(BF16)


def legendre_kernel(limits_ref, arrived_ref, legendre_ref, out_hbm, out_ref, sems, *, lat, lev, packs):
    outputs, slots, top_wave = out_ref.shape
    circles = legendre_ref.shape[0] // slots
    own = circles // lat
    per_tile = LANES // circles

    total = arrived_ref.shape[0]
    row = lax.broadcasted_iota(jnp.int32, (total, total), 0)
    col = lax.broadcasted_iota(jnp.int32, (total, total), 1)
    log = lambda n: n.bit_length() - 1
    inner = row & (own - 1)
    group = (row >> log(own)) & (2 * lev - 1)
    outer = row >> log(own * 2 * lev)
    target = (group << log(circles)) | (outer << log(own)) | inner
    turned = lax.dot_general(
        arrived_ref[...], one_hot(col == target), CONTRACT_ROWS, preferred_element_type=F32
    )

    sub = lax.broadcasted_iota(jnp.int32, (8, LANES), 0)
    block = lax.broadcasted_iota(jnp.int32, (8, LANES), 1) >> log(circles)
    chosen = [(block == b) & ((sub & (per_tile - 1)) == b) for b in range(per_tile)]
    halves = 8 // per_tile
    in_half = [(sub >> log(per_tile)) == h for h in range(halves)]
    step = LANES // packs
    spread = []
    for k in range(slots // 8):
        pieces = [None] * outputs
        for l in range(packs):
            for j in range(total // LANES):
                at = l * step + 8 * k
                v = turned[at : at + 8, j * LANES : (j + 1) * LANES]
                rolled = [v] + [pltpu.roll(v, circles * d, 1) for d in range(1, per_tile)]
                for i in range(per_tile):
                    a = jnp.zeros((8, LANES), F32)
                    for b in range(per_tile):
                        a = jnp.where(chosen[b], rolled[(b - i) % per_tile], a)
                    group_lev, part = divmod(j * per_tile + i, 2)
                    pieces[(group_lev * packs + l) * 2 + part] = jnp.concatenate(
                        [jnp.where(in_half[h], a, 0.0) for h in range(halves)], axis=1
                    )
        spread.append(jnp.concatenate(pieces, axis=0).astype(BF16))

    wide = 2 * LANES
    lane = lax.broadcasted_iota(jnp.int32, (8, wide), 1)
    limits = [limits_ref[8 * k : 8 * k + 8] for k in range(slots // 8)]
    limits = [jnp.concatenate([m, m], axis=1) for m in limits]
    copies = []
    for n in range(0, top_wave, wide):
        sums = [
            jnp.dot(
                spread[k],
                legendre_ref[8 * k * circles : 8 * (k + 1) * circles, n : n + wide],
                preferred_element_type=F32,
            )
            for k in range(slots // 8)
        ]
        keep = [lane + n >= m for m in limits]
        for o in range(outputs):
            out_ref[o, :, n : n + wide] = jnp.concatenate(
                [jnp.where(keep[k], sums[k][8 * o : 8 * o + 8], 0.0) for k in range(slots // 8)],
                axis=0,
            ).astype(BF16)
        columns = (slice(None), slice(None), pl.ds(n, wide))
        copies.append(
            pltpu.make_async_copy(
                out_ref.at[columns], out_hbm.at[columns], sems.at[n // wide]
            )
        )
        copies[-1].start()
    for copy in copies:
        copy.wait()


def other_neighbours(size):
    pairs = [(i, i + 1) for i in range(1, size - 1, 2)]
    return pairs + [(j, i) for i, j in pairs]


def body(
    grid_field, send_blocks, donor_index, tile_choice, kernel_tiles, circle_len, slot_wave, legendre
):
    levels, blocks, _ = grid_field.shape
    send_count = send_blocks.shape[2]
    slots, circles, top_wave = legendre.shape
    lat, lev = lax.axis_size("lat"), lax.axis_size("lev")
    devices = lat * lev
    coarse = PTS // LANES
    own = blocks // coarse
    tiles = slot_wave.shape[0] // LANES
    waves = slot_wave.reshape(tiles, LANES)

    def like(x):
        return jax.ShapeDtypeStruct(x.shape, x.dtype)

    donors, kinds = donor_index.T, tile_choice.T
    halo = jax.ShapeDtypeStruct((send_count, levels * LANES), BF16)
    lengths = jax.ShapeDtypeStruct((own, 8, LANES), jnp.int32)
    small = (send_blocks, grid_field, circle_len, donors, kinds, kernel_tiles, waves)
    to_first, to_second, field, lengths, donors, kinds, kernels, waves = pl.pallas_call(
        outgoing_kernel,
        out_shape=(halo, halo, like(grid_field), lengths, *map(like, small[3:])),
        in_specs=[HBM] * 7, out_specs=(VMEM,) * 8,
        scratch_shapes=[
            pltpu.VMEM(send_blocks.shape, jnp.int32),
            pltpu.SMEM(circle_len.shape, jnp.int32),
            pltpu.SemaphoreType.DMA((7,)),
        ],
        compiler_params=params(4), name="outgoing",
    )(*small)
    first = lax.ppermute(to_first, "lat", [(i, i ^ 1) for i in range(lat)])
    second = lax.ppermute(to_second, "lat", other_neighbours(lat))

    entries = own * tiles * (LANES + coarse) * 2 * LANES
    fine, wide, limits = pl.pallas_call(
        functools.partial(table_kernel, lev=lev),
        out_shape=(
            jax.ShapeDtypeStruct((own, tiles, LANES, 2 * LANES), BF16),
            jax.ShapeDtypeStruct((own, tiles, coarse, 2 * LANES), F32),
            jax.ShapeDtypeStruct((slots, LANES), jnp.int32),
        ),
        in_specs=[VMEM, VMEM, HBM], out_specs=(VMEM,) * 3,
        scratch_shapes=[pltpu.SMEM(slot_wave.shape, jnp.int32), pltpu.SemaphoreType.DMA],
        compiler_params=params(26), name="tables",
        cost_estimate=pl.CostEstimate(flops=8 * entries, bytes_accessed=3 * entries, transcendentals=0),
    )(lengths, waves, slot_wave)

    rows = levels * 2 * own
    packs = 1
    while rows % (16 * packs) == 0 and 2 * packs * slots <= LANES:
        packs *= 2
    coeffs = pl.pallas_call(
        functools.partial(transform_kernel, top_wave=top_wave),
        out_shape=jax.ShapeDtypeStruct((devices, rows // packs, LANES), BF16),
        in_specs=[VMEM] * 10, out_specs=VMEM,
        scratch_shapes=[
            pltpu.VMEM((own, levels * coarse, LANES), F32),
            pltpu.VMEM((tiles, rows, LANES), F32),
        ],
        compiler_params=params(40), name="transform",
    )(
        lengths, donors, kinds, field, first, second, kernels, waves, fine, wide
    )
    arrived = lax.all_to_all(coeffs, ("lat", "lev"), 0, 0, tiled=True)

    outputs = lev * levels * 2
    height = rows // packs
    if packs == levels and height == 2 * own == 8 and LANES == 4 * circles and slots % 8 == 0:
        spectra = pl.pallas_call(
            functools.partial(legendre_kernel, lat=lat, lev=lev, packs=packs),
            out_shape=jax.ShapeDtypeStruct((outputs, slots, top_wave), BF16),
            in_specs=[VMEM] * 3, out_specs=HBM,
            scratch_shapes=[
                pltpu.VMEM((outputs, slots, top_wave), BF16),
                pltpu.SemaphoreType.DMA((top_wave // (2 * LANES),)),
            ],
            compiler_params=params(32), name="legendre",
        )(
            limits,
            arrived.reshape(devices * height, LANES),
            legendre.reshape(slots * circles, top_wave),
        )
        return spectra.reshape(outputs // 2, 2, slots, top_wave)

    gathered = arrived.reshape(lat, lev, height, packs, LANES // packs)[..., :slots]
    gathered = gathered.swapaxes(2, 3).reshape(lat, lev, levels, 2, own, slots)
    gathered = gathered.transpose(1, 2, 3, 0, 4, 5).reshape(outputs // 2, 2, circles, slots)
    spectra = jnp.einsum("lcgs,sgn->lcsn", gathered, legendre, preferred_element_type=F32)
    first_slot = (lax.axis_index("lat") * lev + lax.axis_index("lev")) * slots
    mine = lax.dynamic_slice_in_dim(slot_wave, first_slot, slots)
    allowed = jnp.arange(top_wave, dtype=jnp.int32)[None, :] >= mine[:, None]
    return jnp.where(allowed[None, None], spectra, 0.0).astype(BF16)


def solution(mesh):
    return jax.shard_map(
        body,
        mesh=mesh,
        in_specs=(
            P("lev", "lat", None),
            P("lat", None, None),
            P("lat", None),
            P("lat", None),
            P(),
            P(),
            P(),
            P(("lat", "lev"), None, None),
        ),
        out_specs=P(None, None, ("lat", "lev"), None),
        check_vma=False,
    )
```

```python
import functools
import math

import jax
import jax.numpy as jnp
from jax import lax
from jax.experimental import pallas as pl
from jax.experimental.pallas import tpu as pltpu
from jax.sharding import PartitionSpec as P

PTS = 5120
LANES = 128
BF16 = jnp.bfloat16
F32 = jnp.float32
VMEM = pl.BlockSpec(memory_space=pltpu.VMEM)
HBM = pl.BlockSpec(memory_space=pltpu.HBM)
CONTRACT_ROWS = (((0,), (0,)), ((), ()))


def params(mebibytes):
    return pltpu.CompilerParams(vmem_limit_bytes=mebibytes << 20)


def one_hot(condition):
    return jnp.where(condition, 1.0, 0.0).astype(BF16)


def side_by_side(field_ref):
    return jnp.concatenate([field_ref[l] for l in range(field_ref.shape[0])], axis=1)


def outgoing_kernel(
    send_hbm, field_hbm, length_hbm, donor_hbm, tile_hbm, kernels_hbm, wave_hbm,
    first_ref, second_ref, field_ref, lengths_ref, donor_ref, tile_ref, kernels_ref, wave_ref,
    send_ref, length_ref, sems,
):
    copies = [
        pltpu.make_async_copy(source, target, sems.at[i])
        for i, (source, target) in enumerate(
            (
                (send_hbm, send_ref),
                (field_hbm, field_ref),
                (length_hbm, length_ref),
                (donor_hbm, donor_ref),
                (tile_hbm, tile_ref),
                (kernels_hbm, kernels_ref),
                (wave_hbm, wave_ref),
            )
        )
    ]
    for copy in copies:
        copy.start()
    copies[0].wait()
    copies[1].wait()
    band = lax.axis_index("lat")
    even = lax.rem(band, 2) == 0
    own = side_by_side(field_ref)
    blocks, count = own.shape[0], send_ref.shape[2]
    rows = lax.broadcasted_iota(jnp.int32, (blocks, count), 0)
    below, above = send_ref[0, 0:1, :], send_ref[0, 1:2, :]
    for ref, listed in (
        (first_ref, jnp.where(even, above, below)),
        (second_ref, jnp.where(even, below, above)),
    ):
        picked = lax.dot_general(
            one_hot(rows == listed), own, CONTRACT_ROWS, preferred_element_type=F32
        )
        ref[...] = picked.astype(BF16)
    copies[2].wait()
    circles = lengths_ref.shape[0]
    for g in range(circles):
        lengths_ref[g] = jnp.full((8, LANES), length_ref[band * circles + g], jnp.int32)
    for copy in copies[3:]:
        copy.wait()


def turn(steps, waves, length, inverse):
    phase = steps * waves
    rest = phase - jnp.round(phase * inverse) * length
    f = rest * inverse
    x = f * f
    s = math.pi ** 11 / -math.factorial(11)
    for k in (9, 7, 5, 3, 1):
        s = s * x + (-1) ** (k // 2) * math.pi**k / math.factorial(k)
    s = s * f
    c = math.pi ** 10 / -math.factorial(10)
    for k in (8, 6, 4, 2, 0):
        c = c * x + (-1) ** (k // 2) * math.pi**k / math.factorial(k)
    return 1.0 - 2.0 * (s * s), 2.0 * (s * c)


def times(a, b):
    return a[0] * b[0] - a[1] * b[1], a[0] * b[1] + a[1] * b[0]


def table_kernel(lengths_ref, wave_ref, slot_hbm, fine_ref, coarse_ref, limits_ref, slot_ref, sem, *, lev):
    circles, tiles = fine_ref.shape[:2]
    coarse = coarse_ref.shape[2]
    fetch = pltpu.make_async_copy(slot_hbm, slot_ref, sem)
    fetch.start()
    step = lax.broadcasted_iota(jnp.int32, (8, LANES), 0).astype(F32)

    def doubled(base, factor_of, groups):
        out = [base]
        while len(out) < groups:
            out += [times(e, factor_of(len(out))) for e in out[: groups - len(out)]]
        return out

    def one(index, _):
        g, t = index // tiles, lax.rem(index, tiles)
        length = lengths_ref[g].astype(F32)
        inverse = 1.0 / length
        waves = jnp.broadcast_to(wave_ref[pl.ds(t, 1), :], (8, LANES)).astype(F32)
        hop_steps = jnp.left_shift(8, lax.broadcasted_iota(jnp.int32, (8, LANES), 0)).astype(F32)
        hops = turn(hop_steps, waves, length, inverse)
        far = turn(hop_steps * float(LANES), waves, length, inverse)

        def hop(table):
            def factor(groups):
                k = groups.bit_length() - 1
                return tuple(jnp.broadcast_to(x[k : k + 1], (8, LANES)) for x in table)

            return factor

        fine = doubled(turn(step, waves, length, inverse), hop(hops), LANES // 8)
        fine_ref[g, t] = jnp.concatenate(
            [jnp.concatenate([e[p] for e in fine], axis=0) for p in range(2)], axis=1
        ).astype(BF16)
        wide = doubled(turn(step * float(LANES), waves, length, inverse), hop(far), coarse // 8)
        coarse_ref[g, t] = jnp.concatenate(
            [jnp.concatenate([e[p] for e in wide], axis=0) for p in range(2)], axis=1
        )
        return 0

    lax.fori_loop(0, circles * tiles, one, 0, unroll=2)

    fetch.wait()
    slots = limits_ref.shape[0]
    first = (lax.axis_index("lat") * lev + lax.axis_index("lev")) * slots
    for s in range(slots):
        limits_ref[s : s + 1] = jnp.full((1, LANES), slot_ref[first + s], jnp.int32)


def transform_kernel(
    lengths_ref, donor_ref, tile_ref, field_ref, first_ref, second_ref, kernels_ref, wave_ref,
    fine_ref, coarse_ref, out_ref, points_ref, coeff_ref, *, top_wave,
):
    levels, blocks = field_ref.shape[:2]
    circles, tiles = fine_ref.shape[:2]
    coarse = coarse_ref.shape[2]
    kinds = kernels_ref.shape[0]
    even = lax.rem(lax.axis_index("lat"), 2) == 0

    first, second = first_ref[...], second_ref[...]
    below, above = jnp.where(even, second, first), jnp.where(even, first, second)
    pool = jnp.concatenate([side_by_side(field_ref), below, above], axis=0)

    listed = jnp.concatenate(
        [donor_ref[...], tile_ref[...], jnp.zeros((4, blocks), jnp.int32)], axis=0
    )
    columns = jnp.transpose(listed.astype(F32))
    lane = lax.broadcasted_iota(jnp.int32, (blocks, pool.shape[0]), 1).astype(F32)
    stacked = jnp.concatenate([kernels_ref[k] for k in range(kinds)], axis=1)
    arrival = [jnp.zeros((blocks, LANES), F32) for _ in range(levels)]
    for k in range(2):
        picked = jnp.dot(
            one_hot(lane == columns[:, k : k + 1]), pool, preferred_element_type=F32
        ).astype(BF16)
        kind = jnp.broadcast_to(columns[:, 2 + k : 3 + k], (blocks, LANES))
        for l in range(levels):
            every = jnp.dot(
                picked[:, l * LANES : (l + 1) * LANES], stacked, preferred_element_type=F32
            )
            value = every[:, :LANES]
            for q in range(1, kinds):
                value = jnp.where(kind == float(q), every[:, q * LANES : (q + 1) * LANES], value)
            arrival[l] = arrival[l] + value

    position = lax.broadcasted_iota(jnp.int32, (coarse, LANES), 0) * LANES
    position = position + lax.broadcasted_iota(jnp.int32, (coarse, LANES), 1)
    for g in range(circles):
        inside = position < jnp.broadcast_to(lengths_ref[g, 0:1], (coarse, LANES))
        for l in range(levels):
            part = arrival[l][g * coarse : (g + 1) * coarse]
            points_ref[g, l * coarse : (l + 1) * coarse] = jnp.where(inside, part * part, 0.0)

    def circle(g, _):
        length = lengths_ref[g, 0:1]
        points = points_ref[g].astype(BF16)
        for t in range(tiles):
            near = jnp.dot(points, fine_ref[g, t], preferred_element_type=F32)
            c, s = coarse_ref[g, t, :, :LANES], coarse_ref[g, t, :, LANES:]
            waves = wave_ref[t : t + 1, :]
            live = (waves >= 1) & (waves < top_wave) & (2 * waves < length)
            for l in range(levels):
                here = near[l * coarse : (l + 1) * coarse]
                a, b = here[:, :LANES], here[:, LANES:]
                real = jnp.sum(a * c - b * s, axis=0, keepdims=True)
                imag = jnp.sum(a * s + b * c, axis=0, keepdims=True)
                for part, value in ((0, real), (1, -imag)):
                    row = (l * 2 + part) * circles + g
                    coeff_ref[t, pl.ds(row, 1), :LANES] = jnp.where(live, value, 0.0)
        return 0

    lax.fori_loop(0, circles, circle, 0, unroll=circles * tiles <= 64)

    devices, height, _ = out_ref.shape
    width = tiles * LANES // devices
    packs = coeff_ref.shape[1] // height
    step = LANES // packs
    lane = lax.broadcasted_iota(jnp.int32, (height, LANES), 1)
    for d in range(devices):
        t, shift = divmod(d * width, LANES)
        chunk = jnp.zeros((height, LANES), F32)
        for p in range(packs):
            rows = slice(p * height, (p + 1) * height)
            at = p * step
            value = pltpu.roll(coeff_ref[t, rows, :LANES], (at - shift) % LANES, 1)
            if shift + width > LANES:
                after = pltpu.roll(coeff_ref[t + 1, rows, :LANES], (at - shift) % LANES, 1)
                value = jnp.where(lane < at + LANES - shift, value, after)
            chunk = value if p == 0 else jnp.where(lane < at, chunk, value)
        out_ref[d] = chunk.astype(BF16)


def legendre_kernel(limits_ref, arrived_ref, legendre_ref, out_hbm, out_ref, sems, *, lat, lev, packs):
    outputs, slots, top_wave = out_ref.shape
    circles = legendre_ref.shape[0] // slots
    own = circles // lat
    per_tile = LANES // circles

    total = arrived_ref.shape[0]
    row = lax.broadcasted_iota(jnp.int32, (total, total), 0)
    col = lax.broadcasted_iota(jnp.int32, (total, total), 1)
    log = lambda n: n.bit_length() - 1
    inner = row & (own - 1)
    group = (row >> log(own)) & (2 * lev - 1)
    outer = row >> log(own * 2 * lev)
    target = (group << log(circles)) | (outer << log(own)) | inner
    turned = lax.dot_general(
        arrived_ref[...], one_hot(col == target), CONTRACT_ROWS, preferred_element_type=F32
    )

    sub = lax.broadcasted_iota(jnp.int32, (8, LANES), 0)
    block = lax.broadcasted_iota(jnp.int32, (8, LANES), 1) >> log(circles)
    chosen = [(block == b) & ((sub & (per_tile - 1)) == b) for b in range(per_tile)]
    halves = 8 // per_tile
    in_half = [(sub >> log(per_tile)) == h for h in range(halves)]
    step = LANES // packs
    spread = []
    for k in range(slots // 8):
        pieces = [None] * outputs
        for l in range(packs):
            for j in range(total // LANES):
                at = l * step + 8 * k
                v = turned[at : at + 8, j * LANES : (j + 1) * LANES]
                rolled = [v] + [pltpu.roll(v, circles * d, 1) for d in range(1, per_tile)]
                for i in range(per_tile):
                    a = jnp.zeros((8, LANES), F32)
                    for b in range(per_tile):
                        a = jnp.where(chosen[b], rolled[(b - i) % per_tile], a)
                    group_lev, part = divmod(j * per_tile + i, 2)
                    pieces[(group_lev * packs + l) * 2 + part] = jnp.concatenate(
                        [jnp.where(in_half[h], a, 0.0) for h in range(halves)], axis=1
                    )
        spread.append(jnp.concatenate(pieces, axis=0).astype(BF16))

    wide = 2 * LANES
    lane = lax.broadcasted_iota(jnp.int32, (8, wide), 1)
    limits = [limits_ref[8 * k : 8 * k + 8] for k in range(slots // 8)]
    limits = [jnp.concatenate([m, m], axis=1) for m in limits]
    copies = []
    for n in range(0, top_wave, wide):
        sums = [
            jnp.dot(
                spread[k],
                legendre_ref[8 * k * circles : 8 * (k + 1) * circles, n : n + wide],
                preferred_element_type=F32,
            )
            for k in range(slots // 8)
        ]
        keep = [lane + n >= m for m in limits]
        for o in range(outputs):
            out_ref[o, :, n : n + wide] = jnp.concatenate(
                [jnp.where(keep[k], sums[k][8 * o : 8 * o + 8], 0.0) for k in range(slots // 8)],
                axis=0,
            ).astype(BF16)
        columns = (slice(None), slice(None), pl.ds(n, wide))
        copies.append(
            pltpu.make_async_copy(
                out_ref.at[columns], out_hbm.at[columns], sems.at[n // wide]
            )
        )
        copies[-1].start()
    for copy in copies:
        copy.wait()


def other_neighbours(size):
    pairs = [(i, i + 1) for i in range(1, size - 1, 2)]
    return pairs + [(j, i) for i, j in pairs]


def body(
    grid_field, send_blocks, donor_index, tile_choice, kernel_tiles, circle_len, slot_wave, legendre
):
    levels, blocks, _ = grid_field.shape
    send_count = send_blocks.shape[2]
    slots, circles, top_wave = legendre.shape
    lat, lev = lax.axis_size("lat"), lax.axis_size("lev")
    devices = lat * lev
    coarse = PTS // LANES
    own = blocks // coarse
    tiles = slot_wave.shape[0] // LANES
    waves = slot_wave.reshape(tiles, LANES)

    def like(x):
        return jax.ShapeDtypeStruct(x.shape, x.dtype)

    def in_hbm(x):
        return pltpu.with_memory_space_constraint(x, pltpu.HBM)

    donors, kinds = donor_index.T, tile_choice.T
    halo = jax.ShapeDtypeStruct((send_count, levels * LANES), BF16)
    lengths = jax.ShapeDtypeStruct((own, 8, LANES), jnp.int32)
    small = (send_blocks, grid_field, circle_len, donors, kinds, kernel_tiles, waves)
    to_first, to_second, field, lengths, donors, kinds, kernels, waves = pl.pallas_call(
        outgoing_kernel,
        out_shape=(halo, halo, like(grid_field), lengths, *map(like, small[3:])),
        in_specs=[HBM] * 7, out_specs=(VMEM,) * 8,
        scratch_shapes=[
            pltpu.VMEM(send_blocks.shape, jnp.int32),
            pltpu.SMEM(circle_len.shape, jnp.int32),
            pltpu.SemaphoreType.DMA((7,)),
        ],
        compiler_params=params(4), name="outgoing",
    )(*map(in_hbm, small))
    first = lax.ppermute(to_first, "lat", [(i, i ^ 1) for i in range(lat)])
    second = lax.ppermute(to_second, "lat", other_neighbours(lat))

    entries = own * tiles * (LANES + coarse) * 2 * LANES
    fine, wide, limits = pl.pallas_call(
        functools.partial(table_kernel, lev=lev),
        out_shape=(
            jax.ShapeDtypeStruct((own, tiles, LANES, 2 * LANES), BF16),
            jax.ShapeDtypeStruct((own, tiles, coarse, 2 * LANES), F32),
            jax.ShapeDtypeStruct((slots, LANES), jnp.int32),
        ),
        in_specs=[VMEM, VMEM, HBM], out_specs=(VMEM,) * 3,
        scratch_shapes=[pltpu.SMEM(slot_wave.shape, jnp.int32), pltpu.SemaphoreType.DMA],
        compiler_params=params(26), name="tables",
        cost_estimate=pl.CostEstimate(flops=8 * entries, bytes_accessed=3 * entries, transcendentals=0),
    )(lengths, waves, in_hbm(slot_wave))

    rows = levels * 2 * own
    packs = 1
    while rows % (16 * packs) == 0 and 2 * packs * slots <= LANES:
        packs *= 2
    coeffs = pl.pallas_call(
        functools.partial(transform_kernel, top_wave=top_wave),
        out_shape=jax.ShapeDtypeStruct((devices, rows // packs, LANES), BF16),
        in_specs=[VMEM] * 10, out_specs=VMEM,
        scratch_shapes=[
            pltpu.VMEM((own, levels * coarse, LANES), F32),
            pltpu.VMEM((tiles, rows, LANES), F32),
        ],
        compiler_params=params(40), name="transform",
    )(
        lengths, donors, kinds, field, first, second, kernels, waves, fine, wide
    )
    arrived = lax.all_to_all(coeffs, ("lat", "lev"), 0, 0, tiled=True)

    outputs = lev * levels * 2
    height = rows // packs
    if packs == levels and height == 2 * own == 8 and LANES == 4 * circles and slots % 8 == 0:
        spectra = pl.pallas_call(
            functools.partial(legendre_kernel, lat=lat, lev=lev, packs=packs),
            out_shape=jax.ShapeDtypeStruct((outputs, slots, top_wave), BF16),
            in_specs=[VMEM] * 3, out_specs=HBM,
            scratch_shapes=[
                pltpu.VMEM((outputs, slots, top_wave), BF16),
                pltpu.SemaphoreType.DMA((top_wave // (2 * LANES),)),
            ],
            compiler_params=params(32), name="legendre",
        )(
            limits,
            arrived.reshape(devices * height, LANES),
            legendre.reshape(slots * circles, top_wave),
        )
        return spectra.reshape(outputs // 2, 2, slots, top_wave)

    gathered = arrived.reshape(lat, lev, height, packs, LANES // packs)[..., :slots]
    gathered = gathered.swapaxes(2, 3).reshape(lat, lev, levels, 2, own, slots)
    gathered = gathered.transpose(1, 2, 3, 0, 4, 5).reshape(outputs // 2, 2, circles, slots)
    spectra = jnp.einsum("lcgs,sgn->lcsn", gathered, legendre, preferred_element_type=F32)
    first_slot = (lax.axis_index("lat") * lev + lax.axis_index("lev")) * slots
    mine = lax.dynamic_slice_in_dim(slot_wave, first_slot, slots)
    allowed = jnp.arange(top_wave, dtype=jnp.int32)[None, :] >= mine[:, None]
    return jnp.where(allowed[None, None], spectra, 0.0).astype(BF16)


def solution(mesh):
    return jax.shard_map(
        body,
        mesh=mesh,
        in_specs=(
            P("lev", "lat", None),
            P("lat", None, None),
            P("lat", None),
            P("lat", None),
            P(),
            P(),
            P(),
            P(("lat", "lev"), None, None),
        ),
        out_specs=P(None, None, ("lat", "lev"), None),
        check_vma=False,
    )
```

```python
import functools
import math

import jax
import jax.numpy as jnp
from jax import lax
from jax.experimental import pallas as pl
from jax.experimental.pallas import tpu as pltpu
from jax.sharding import PartitionSpec as P

PTS = 5120
LANES = 128
BF16 = jnp.bfloat16
F32 = jnp.float32
VMEM = pl.BlockSpec(memory_space=pltpu.VMEM)
HBM = pl.BlockSpec(memory_space=pltpu.HBM)
CONTRACT_ROWS = (((0,), (0,)), ((), ()))


def params(mebibytes):
    return pltpu.CompilerParams(vmem_limit_bytes=mebibytes << 20)


def one_hot(condition):
    return jnp.where(condition, 1.0, 0.0).astype(BF16)


def side_by_side(field_ref):
    return jnp.concatenate([field_ref[l] for l in range(field_ref.shape[0])], axis=1)


def outgoing_kernel(
    send_hbm, field_hbm, length_hbm, wave_hbm, far_ref, near_ref, field_ref, lengths_ref, wave_ref,
    send_ref, length_ref, sems,
):
    pairs = (
        (send_hbm, send_ref), (field_hbm, field_ref), (length_hbm, length_ref), (wave_hbm, wave_ref)
    )
    copies = [pltpu.make_async_copy(*pair, sems.at[i]) for i, pair in enumerate(pairs)]
    for copy in copies:
        copy.start()
    copies[0].wait()
    copies[1].wait()
    band = lax.axis_index("lat")
    even = lax.rem(band, 2) == 0
    own = side_by_side(field_ref)
    blocks, count = own.shape[0], send_ref.shape[2]
    rows = lax.broadcasted_iota(jnp.int32, (blocks, count), 0)
    below, above = send_ref[0, 0:1, :], send_ref[0, 1:2, :]
    for ref, listed in (
        (far_ref, jnp.where(even, below, above)),
        (near_ref, jnp.where(even, above, below)),
    ):
        picked = lax.dot_general(
            one_hot(rows == listed), own, CONTRACT_ROWS, preferred_element_type=F32
        )
        ref[...] = picked.astype(BF16)
    copies[2].wait()
    circles = lengths_ref.shape[0] // 2
    for i in range(2 * circles):
        length = length_ref[band * circles + i % circles]
        lengths_ref[i : i + 1] = jnp.full((1, LANES), length, jnp.int32)
    copies[3].wait()


def turn(steps, waves, length, inverse):
    phase = steps * waves
    rest = phase - jnp.round(phase * inverse) * length
    f = rest * inverse
    x = f * f
    s = math.pi ** 11 / -math.factorial(11)
    for k in (9, 7, 5, 3, 1):
        s = s * x + (-1) ** (k // 2) * math.pi**k / math.factorial(k)
    s = s * f
    c = math.pi ** 10 / -math.factorial(10)
    for k in (8, 6, 4, 2, 0):
        c = c * x + (-1) ** (k // 2) * math.pi**k / math.factorial(k)
    return 1.0 - 2.0 * (s * s), 2.0 * (s * c)


def log(n):
    return n.bit_length() - 1


def times(a, b):
    return a[0] * b[0] - a[1] * b[1], a[0] * b[1] + a[1] * b[0]


def table_kernel(
    lengths_ref, wave_ref, field_ref, slot_hbm, donor_hbm, tile_hbm, kernels_hbm, legendre_hbm,
    fine_ref, coarse_ref, limits_ref, hot_ref, own_ref, kind_ref, kernels_ref, legendre_ref,
    order_ref, slot_ref, donor_ref, tile_ref, sems, *, lat, lev,
):
    circles, tiles = fine_ref.shape[:2]
    coarse = coarse_ref.shape[2]
    pairs = (
        (slot_hbm, slot_ref), (donor_hbm, donor_ref), (tile_hbm, tile_ref),
        (kernels_hbm, kernels_ref), (legendre_hbm, legendre_ref),
    )
    copies = [pltpu.make_async_copy(*pair, sems.at[i]) for i, pair in enumerate(pairs)]
    for copy in copies:
        copy.start()
    step = lax.broadcasted_iota(jnp.int32, (8, LANES), 0).astype(F32)

    def doubled(base, factor_of, groups):
        out = [base]
        while len(out) < groups:
            out += [times(e, factor_of(len(out))) for e in out[: groups - len(out)]]
        return out

    def one(index, _):
        g, t = index // tiles, lax.rem(index, tiles)
        length = jnp.broadcast_to(lengths_ref[pl.ds(g, 1)], (8, LANES)).astype(F32)
        inverse = 1.0 / length
        waves = jnp.broadcast_to(wave_ref[pl.ds(t, 1), :], (8, LANES)).astype(F32)
        hop_steps = jnp.left_shift(8, lax.broadcasted_iota(jnp.int32, (8, LANES), 0)).astype(F32)
        hops = turn(hop_steps, waves, length, inverse)
        far = turn(hop_steps * float(LANES), waves, length, inverse)

        def hop(table):
            def factor(groups):
                k = groups.bit_length() - 1
                return tuple(jnp.broadcast_to(x[k : k + 1], (8, LANES)) for x in table)

            return factor

        fine = doubled(turn(step, waves, length, inverse), hop(hops), LANES // 8)
        fine_ref[g, t] = jnp.concatenate(
            [jnp.concatenate([e[p] for e in fine], axis=0) for p in range(2)], axis=1
        ).astype(BF16)
        wide = doubled(turn(step * float(LANES), waves, length, inverse), hop(far), coarse // 8)
        coarse_ref[g, t] = jnp.concatenate(
            [jnp.concatenate([e[p] for e in wide], axis=0) for p in range(2)], axis=1
        )
        return 0

    lax.fori_loop(0, circles * tiles, one, 0, unroll=2)

    copies[0].wait()
    slots = limits_ref.shape[0]
    first = (lax.axis_index("lat") * lev + lax.axis_index("lev")) * slots
    for s in range(slots):
        limits_ref[s : s + 1] = jnp.full((1, LANES), slot_ref[first + s], jnp.int32)

    copies[1].wait()
    copies[2].wait()
    own = side_by_side(field_ref)
    blocks = own.shape[0]
    listed = jnp.concatenate(
        [donor_ref[...], tile_ref[...], jnp.zeros((4, blocks), jnp.int32)], axis=0
    )
    columns = jnp.transpose(listed.astype(F32))
    lane = lax.broadcasted_iota(jnp.int32, (blocks, blocks), 1).astype(F32)
    halo_lane = lax.broadcasted_iota(jnp.int32, hot_ref.shape[1:], 1).astype(F32) + float(blocks)
    for k in range(2):
        donor = columns[:, k : k + 1]
        own_ref[k] = jnp.dot(one_hot(lane == donor), own, preferred_element_type=F32)
        hot_ref[k] = one_hot(halo_lane == donor)
        kind_ref[k] = jnp.broadcast_to(columns[:, 2 + k : 3 + k], (blocks, LANES))

    total = order_ref.shape[0]
    if total == lat * lev * 2 * circles:
        row = lax.broadcasted_iota(jnp.int32, (total, total), 0)
        col = lax.broadcasted_iota(jnp.int32, (total, total), 1)
        group = (row >> log(circles)) & (2 * lev - 1)
        outer = row >> log(circles * 2 * lev)
        target = (group << log(lat * circles)) | (outer << log(circles)) | (row & (circles - 1))
        order_ref[...] = one_hot(col == target)
    else:
        order_ref[...] = jnp.zeros(order_ref.shape, BF16)
    copies[3].wait()
    copies[4].wait()


def fold(parts):
    row = lax.broadcasted_iota(jnp.int32, (8, LANES), 0)
    for half in (4, 2, 1):
        low = (row & half) == 0
        count = len(parts) // 2
        parts = [
            jnp.where(low, a, pltpu.roll(b, half, 0)) + jnp.where(low, pltpu.roll(a, 8 - half, 0), b)
            for a, b in zip(parts[:count], parts[count:])
        ]
    return parts[0]


def transform_kernel(
    lengths_ref, wave_ref, far_ref, near_ref, hot_ref, own_ref, kind_ref, kernels_ref, fine_ref,
    coarse_ref, out_ref, points_ref, coeff_ref, *, top_wave,
):
    blocks = own_ref.shape[1]
    levels = own_ref.shape[2] // LANES
    circles, tiles = fine_ref.shape[:2]
    coarse = coarse_ref.shape[2]
    kinds = kernels_ref.shape[0]
    band = lax.axis_index("lat")
    even = lax.rem(band, 2) == 0

    near, far = near_ref[...], far_ref[...]
    at_end = (band == 0) | (band == lax.axis_size("lat") - 1)
    far = jnp.where(at_end, jnp.zeros_like(far), far)
    halo = jnp.concatenate([jnp.where(even, far, near), jnp.where(even, near, far)], axis=0)
    stacked = jnp.concatenate([kernels_ref[k] for k in range(kinds)], axis=1)
    arrival = [jnp.zeros((blocks, LANES), F32) for _ in range(levels)]
    for k in range(2):
        picked = jnp.dot(hot_ref[k], halo, preferred_element_type=F32)
        picked = (picked + own_ref[k]).astype(BF16)
        kind = kind_ref[k]
        for l in range(levels):
            every = jnp.dot(
                picked[:, l * LANES : (l + 1) * LANES], stacked, preferred_element_type=F32
            )
            value = every[:, :LANES]
            for q in range(1, kinds):
                value = jnp.where(kind == float(q), every[:, q * LANES : (q + 1) * LANES], value)
            arrival[l] = arrival[l] + value

    position = lax.broadcasted_iota(jnp.int32, (coarse, LANES), 0) * LANES
    position = position + lax.broadcasted_iota(jnp.int32, (coarse, LANES), 1)
    for g in range(circles):
        inside = position < jnp.broadcast_to(lengths_ref[g : g + 1], (coarse, LANES))
        parts = [arrival[l][g * coarse : (g + 1) * coarse] for l in range(levels)]
        parts = [jnp.where(inside, part * part, 0.0) for part in parts]
        points_ref[g] = jnp.concatenate(parts, axis=0).astype(BF16)

    height = 2 * circles
    lengths = lengths_ref[...]
    sine = lax.broadcasted_iota(jnp.int32, (height, LANES), 0) >= circles

    def tile(t, _):
        sums = [[] for _ in range(levels)]
        for g in range(circles):
            turned = jnp.dot(points_ref[g], fine_ref[g, t], preferred_element_type=F32)
            c, s = coarse_ref[g, t, :, :LANES], coarse_ref[g, t, :, LANES:]
            for l in range(levels):
                here = turned[l * coarse : (l + 1) * coarse]
                a, b = here[:, :LANES], here[:, LANES:]
                for value in (a * c - b * s, a * s + b * c):
                    sums[l].append(jnp.sum(value.reshape(coarse // 8, 8, LANES), axis=0))
        waves = jnp.broadcast_to(wave_ref[pl.ds(t, 1), :], (height, LANES))
        live = (waves >= 1) & (waves < top_wave) & (2 * waves < lengths)
        for l in range(levels):
            ordered = sums[l][0::2] + sums[l][1::2]
            rows = [fold(ordered[i : i + 8]) for i in range(0, height, 8)]
            rows = jnp.concatenate(rows, axis=0)
            coeff_ref[t, l * height : (l + 1) * height] = jnp.where(
                live, jnp.where(sine, -rows, rows), 0.0
            )
        return 0

    lax.fori_loop(0, tiles, tile, 0, unroll=circles * tiles <= 64)

    devices, height, _ = out_ref.shape
    width = tiles * LANES // devices
    packs = coeff_ref.shape[1] // height
    step = LANES // packs
    lane = lax.broadcasted_iota(jnp.int32, (height, LANES), 1)
    for d in range(devices):
        t, shift = divmod(d * width, LANES)
        chunk = jnp.zeros((height, LANES), F32)
        for p in range(packs):
            rows = slice(p * height, (p + 1) * height)
            at = p * step
            value = pltpu.roll(coeff_ref[t, rows], (at - shift) % LANES, 1)
            if shift + width > LANES:
                after = pltpu.roll(coeff_ref[t + 1, rows], (at - shift) % LANES, 1)
                value = jnp.where(lane < at + LANES - shift, value, after)
            chunk = value if p == 0 else jnp.where(lane < at, chunk, value)
        out_ref[d] = chunk.astype(BF16)


def legendre_kernel(limits_ref, arrived_ref, order_ref, legendre_ref, out_hbm, out_ref, sems, *, packs):
    outputs, slots, top_wave = out_ref.shape
    circles = legendre_ref.shape[0] // slots
    per_tile = LANES // circles
    total = arrived_ref.shape[0]
    turned = lax.dot_general(
        arrived_ref[...], order_ref[...], CONTRACT_ROWS, preferred_element_type=F32
    )

    sub = lax.broadcasted_iota(jnp.int32, (8, LANES), 0)
    block = lax.broadcasted_iota(jnp.int32, (8, LANES), 1) >> log(circles)
    chosen = [(block == b) & ((sub & (per_tile - 1)) == b) for b in range(per_tile)]
    halves = 8 // per_tile
    in_half = [(sub >> log(per_tile)) == h for h in range(halves)]
    step = LANES // packs
    spread = []
    for k in range(slots // 8):
        pieces = [None] * outputs
        for l in range(packs):
            for j in range(total // LANES):
                at = l * step + 8 * k
                v = turned[at : at + 8, j * LANES : (j + 1) * LANES]
                rolled = [v] + [pltpu.roll(v, circles * d, 1) for d in range(1, per_tile)]
                for i in range(per_tile):
                    a = jnp.zeros((8, LANES), F32)
                    for b in range(per_tile):
                        a = jnp.where(chosen[b], rolled[(b - i) % per_tile], a)
                    group_lev, part = divmod(j * per_tile + i, 2)
                    pieces[(group_lev * packs + l) * 2 + part] = jnp.concatenate(
                        [jnp.where(in_half[h], a, 0.0) for h in range(halves)], axis=1
                    )
        spread.append(jnp.concatenate(pieces, axis=0).astype(BF16))

    wide = 2 * LANES
    lane = lax.broadcasted_iota(jnp.int32, (8, wide), 1)
    limits = [limits_ref[8 * k : 8 * k + 8] for k in range(slots // 8)]
    limits = [jnp.concatenate([m, m], axis=1) for m in limits]
    copies = []
    for n in range(0, top_wave, wide):
        sums = [
            jnp.dot(
                spread[k],
                legendre_ref[8 * k * circles : 8 * (k + 1) * circles, n : n + wide],
                preferred_element_type=F32,
            )
            for k in range(slots // 8)
        ]
        keep = [lane + n >= m for m in limits]
        for o in range(outputs):
            out_ref[o, :, n : n + wide] = jnp.concatenate(
                [jnp.where(keep[k], sums[k][8 * o : 8 * o + 8], 0.0) for k in range(slots // 8)],
                axis=0,
            ).astype(BF16)
        columns = (slice(None), slice(None), pl.ds(n, wide))
        copies.append(
            pltpu.make_async_copy(
                out_ref.at[columns], out_hbm.at[columns], sems.at[n // wide]
            )
        )
        copies[-1].start()
    for copy in copies:
        copy.wait()


def other_neighbours(lat, lev):
    inner = [(i, i + 1) for i in range(1, lat - 1, 2)]
    inner += [(j, i) for i, j in inner]
    pairs = [(i * lev + l, j * lev + l) for i, j in inner for l in range(lev)]
    return pairs + [(i * lev + l, i * lev + (l ^ 1)) for i in (0, lat - 1) for l in range(lev)]


def body(
    grid_field, send_blocks, donor_index, tile_choice, kernel_tiles, circle_len, slot_wave, legendre
):
    levels, blocks, _ = grid_field.shape
    send_count = send_blocks.shape[2]
    slots, circles, top_wave = legendre.shape
    lat, lev = lax.axis_size("lat"), lax.axis_size("lev")
    devices = lat * lev
    coarse = PTS // LANES
    own = blocks // coarse
    tiles = slot_wave.shape[0] // LANES
    waves = slot_wave.reshape(tiles, LANES)

    def like(x):
        return jax.ShapeDtypeStruct(x.shape, x.dtype)

    def in_hbm(x):
        return pltpu.with_memory_space_constraint(x, pltpu.HBM)

    halo = jax.ShapeDtypeStruct((send_count, levels * LANES), BF16)
    to_far, to_near, field, lengths, waves = pl.pallas_call(
        outgoing_kernel,
        out_shape=(
            halo, halo, like(grid_field), jax.ShapeDtypeStruct((2 * own, LANES), jnp.int32), like(waves)
        ),
        in_specs=[HBM] * 4, out_specs=(VMEM,) * 5,
        scratch_shapes=[
            pltpu.VMEM(send_blocks.shape, jnp.int32),
            pltpu.SMEM(circle_len.shape, jnp.int32),
            pltpu.SemaphoreType.DMA((4,)),
        ],
        compiler_params=params(4), name="outgoing",
    )(*map(in_hbm, (send_blocks, grid_field, circle_len, waves)))
    near = lax.ppermute(to_near, "lat", [(i, i ^ 1) for i in range(lat)])
    far = lax.ppermute(to_far, ("lat", "lev"), other_neighbours(lat, lev))

    direct = levels == 2 and 2 * own == 8 and 4 * circles == LANES and slots % 8 == 0
    direct = direct and 2 * slots <= LANES and lev & (lev - 1) == 0
    total = devices * 2 * own if direct else 16
    entries = own * tiles * (LANES + coarse) * 2 * LANES
    donors, kinds = donor_index.T, tile_choice.T
    fine, wide, limits, hot, own_part, kind, kernels, functions, order = pl.pallas_call(
        functools.partial(table_kernel, lat=lat, lev=lev),
        out_shape=(
            jax.ShapeDtypeStruct((own, tiles, LANES, 2 * LANES), BF16),
            jax.ShapeDtypeStruct((own, tiles, coarse, 2 * LANES), F32),
            jax.ShapeDtypeStruct((slots, LANES), jnp.int32),
            jax.ShapeDtypeStruct((2, blocks, 2 * send_count), BF16),
            jax.ShapeDtypeStruct((2, blocks, levels * LANES), F32),
            jax.ShapeDtypeStruct((2, blocks, LANES), F32),
            like(kernel_tiles),
            like(legendre),
            jax.ShapeDtypeStruct((total, total), BF16),
        ),
        in_specs=[VMEM] * 3 + [HBM] * 5, out_specs=(VMEM,) * 9,
        scratch_shapes=[
            pltpu.SMEM(slot_wave.shape, jnp.int32),
            pltpu.VMEM(donors.shape, jnp.int32),
            pltpu.VMEM(donors.shape, jnp.int32),
            pltpu.SemaphoreType.DMA((5,)),
        ],
        compiler_params=params(32), name="tables",
        cost_estimate=pl.CostEstimate(flops=8 * entries, bytes_accessed=3 * entries, transcendentals=0),
    )(lengths, waves, field, *map(in_hbm, (slot_wave, donors, kinds, kernel_tiles, legendre)))

    rows = levels * 2 * own
    packs = 1
    while rows % (16 * packs) == 0 and 2 * packs * slots <= LANES:
        packs *= 2
    coeffs = pl.pallas_call(
        functools.partial(transform_kernel, top_wave=top_wave),
        out_shape=jax.ShapeDtypeStruct((devices, rows // packs, LANES), BF16),
        in_specs=[VMEM] * 10, out_specs=VMEM,
        scratch_shapes=[
            pltpu.VMEM((own, levels * coarse, LANES), BF16),
            pltpu.VMEM((tiles, rows, LANES), F32),
        ],
        compiler_params=params(40), name="transform",
    )(lengths, waves, far, near, hot, own_part, kind, kernels, fine, wide)
    arrived = lax.all_to_all(coeffs, ("lat", "lev"), 0, 0, tiled=True)

    outputs = lev * levels * 2
    height = rows // packs
    if direct:
        spectra = pl.pallas_call(
            functools.partial(legendre_kernel, packs=packs),
            out_shape=jax.ShapeDtypeStruct((outputs, slots, top_wave), BF16),
            in_specs=[VMEM] * 4, out_specs=HBM,
            scratch_shapes=[
                pltpu.VMEM((outputs, slots, top_wave), BF16),
                pltpu.SemaphoreType.DMA((top_wave // (2 * LANES),)),
            ],
            compiler_params=params(32), name="legendre",
        )(
            limits,
            arrived.reshape(devices * height, LANES),
            order,
            functions.reshape(slots * circles, top_wave),
        )
        return spectra.reshape(outputs // 2, 2, slots, top_wave)

    gathered = arrived.reshape(lat, lev, height, packs, LANES // packs)[..., :slots]
    gathered = gathered.swapaxes(2, 3).reshape(lat, lev, levels, 2, own, slots)
    gathered = gathered.transpose(1, 2, 3, 0, 4, 5).reshape(outputs // 2, 2, circles, slots)
    spectra = jnp.einsum("lcgs,sgn->lcsn", gathered, functions, preferred_element_type=F32)
    first_slot = (lax.axis_index("lat") * lev + lax.axis_index("lev")) * slots
    mine = lax.dynamic_slice_in_dim(slot_wave, first_slot, slots)
    allowed = jnp.arange(top_wave, dtype=jnp.int32)[None, :] >= mine[:, None]
    return jnp.where(allowed[None, None], spectra, 0.0).astype(BF16)


def solution(mesh):
    return jax.shard_map(
        body,
        mesh=mesh,
        in_specs=(
            P("lev", "lat", None),
            P("lat", None, None),
            P("lat", None),
            P("lat", None),
            P(),
            P(),
            P(),
            P(("lat", "lev"), None, None),
        ),
        out_specs=P(None, None, ("lat", "lev"), None),
        check_vma=False,
    )
```

```python
import functools
import math

import jax
import jax.numpy as jnp
from jax import lax
from jax.experimental import pallas as pl
from jax.experimental.pallas import tpu as pltpu
from jax.sharding import PartitionSpec as P

PTS = 5120
LANES = 128
BF16 = jnp.bfloat16
F32 = jnp.float32
VMEM = pl.BlockSpec(memory_space=pltpu.VMEM)
HBM = pl.BlockSpec(memory_space=pltpu.HBM)
CONTRACT_ROWS = (((0,), (0,)), ((), ()))


def params(mebibytes):
    return pltpu.CompilerParams(vmem_limit_bytes=mebibytes << 20)


def one_hot(condition):
    return jnp.where(condition, 1.0, 0.0).astype(BF16)


def side_by_side(field_ref):
    return jnp.concatenate([field_ref[l] for l in range(field_ref.shape[0])], axis=1)


def outgoing_kernel(
    send_hbm, field_hbm, length_hbm, wave_hbm, far_ref, near_ref, field_ref, lengths_ref, wave_ref,
    send_ref, length_ref, sems,
):
    pairs = (
        (send_hbm, send_ref), (field_hbm, field_ref), (length_hbm, length_ref), (wave_hbm, wave_ref)
    )
    copies = [pltpu.make_async_copy(*pair, sems.at[i]) for i, pair in enumerate(pairs)]
    for copy in copies:
        copy.start()
    copies[0].wait()
    copies[1].wait()
    band = lax.axis_index("lat")
    even = lax.rem(band, 2) == 0
    own = side_by_side(field_ref)
    blocks, count = own.shape[0], send_ref.shape[2]
    rows = lax.broadcasted_iota(jnp.int32, (blocks, count), 0)
    below, above = send_ref[0, 0:1, :], send_ref[0, 1:2, :]
    for ref, listed in (
        (far_ref, jnp.where(even, below, above)),
        (near_ref, jnp.where(even, above, below)),
    ):
        picked = lax.dot_general(
            one_hot(rows == listed), own, CONTRACT_ROWS, preferred_element_type=F32
        )
        ref[...] = picked.astype(BF16)
    copies[2].wait()
    circles = lengths_ref.shape[0] // 2
    for i in range(2 * circles):
        length = length_ref[band * circles + i % circles]
        lengths_ref[i : i + 1] = jnp.full((1, LANES), length, jnp.int32)
    copies[3].wait()


def turn(steps, waves, length, inverse):
    phase = steps * waves
    rest = phase - jnp.round(phase * inverse) * length
    f = rest * inverse
    x = f * f
    s = math.pi ** 11 / -math.factorial(11)
    for k in (9, 7, 5, 3, 1):
        s = s * x + (-1) ** (k // 2) * math.pi**k / math.factorial(k)
    s = s * f
    c = math.pi ** 10 / -math.factorial(10)
    for k in (8, 6, 4, 2, 0):
        c = c * x + (-1) ** (k // 2) * math.pi**k / math.factorial(k)
    return 1.0 - 2.0 * (s * s), 2.0 * (s * c)


def log(n):
    return n.bit_length() - 1


def times(a, b):
    return a[0] * b[0] - a[1] * b[1], a[0] * b[1] + a[1] * b[0]


def table_kernel(
    lengths_ref, wave_ref, field_ref, slot_hbm, donor_hbm, tile_hbm, kernels_hbm, legendre_hbm,
    fine_ref, coarse_ref, limits_ref, choice_ref, arrival_ref, kernels_ref, legendre_ref, order_ref,
    slot_ref, donor_ref, tile_ref, sems, *, lat, lev,
):
    circles, tiles = fine_ref.shape[:2]
    levels, blocks, _ = field_ref.shape
    coarse = blocks // circles
    pairs = (
        (slot_hbm, slot_ref), (donor_hbm, donor_ref), (tile_hbm, tile_ref),
        (kernels_hbm, kernels_ref), (legendre_hbm, legendre_ref),
    )
    copies = [pltpu.make_async_copy(*pair, sems.at[i]) for i, pair in enumerate(pairs)]
    for copy in copies:
        copy.start()
    step = lax.broadcasted_iota(jnp.int32, (8, LANES), 0).astype(F32)

    def doubled(base, factor_of, groups):
        out = [base]
        while len(out) < groups:
            out += [times(e, factor_of(len(out))) for e in out[: groups - len(out)]]
        return out

    def one(index, _):
        g, t = index // tiles, lax.rem(index, tiles)
        length = jnp.broadcast_to(lengths_ref[pl.ds(g, 1)], (8, LANES)).astype(F32)
        inverse = 1.0 / length
        waves = jnp.broadcast_to(wave_ref[pl.ds(t, 1), :], (8, LANES)).astype(F32)
        hop_steps = jnp.left_shift(8, lax.broadcasted_iota(jnp.int32, (8, LANES), 0)).astype(F32)
        hops = turn(hop_steps, waves, length, inverse)
        far = turn(hop_steps * float(LANES), waves, length, inverse)

        def hop(table):
            def factor(groups):
                k = groups.bit_length() - 1
                return tuple(jnp.broadcast_to(x[k : k + 1], (8, LANES)) for x in table)

            return factor

        middle = float(LANES // 2 * (coarse - 1))
        fine = doubled(turn(step + middle, waves, length, inverse), hop(hops), LANES // 8)
        fine_ref[g, t] = jnp.concatenate(
            [jnp.concatenate([e[p] for e in fine], axis=0) for p in range(2)], axis=1
        ).astype(BF16)
        start = turn(step * float(LANES) + float(LANES // 2), waves, length, inverse)
        half = coarse // 2
        wide = doubled(start, hop(far), -(-half // 8))
        wide = [jnp.concatenate([e[p] for e in wide], axis=0)[:half] for p in range(2)]
        coarse_ref[g, t] = jnp.concatenate(
            [jnp.concatenate([part] * levels, axis=0) for part in wide], axis=1
        )
        return 0

    lax.fori_loop(0, circles * tiles, one, 0, unroll=2)

    copies[0].wait()
    slots = limits_ref.shape[0]
    first = (lax.axis_index("lat") * lev + lax.axis_index("lev")) * slots
    for s in range(slots):
        limits_ref[s : s + 1] = jnp.full((1, LANES), slot_ref[first + s], jnp.int32)

    copies[1].wait()
    copies[2].wait()
    copies[3].wait()
    donor, kind = donor_ref[...], tile_ref[...]
    listed = jnp.concatenate(
        [donor & 15, donor >> 4, kind, jnp.zeros((2, blocks), jnp.int32)], axis=0
    )
    source = lax.broadcasted_iota(jnp.int32, (blocks, blocks), 0)
    place = lax.broadcasted_iota(jnp.int32, (blocks, blocks), 1)
    begin = jnp.zeros((blocks, blocks), jnp.int32)
    for g in range(1, circles):
        begin = jnp.where(place >= g * coarse, g * coarse, begin)
    place = place - begin
    half = coarse // 2
    wanted = begin + jnp.where(place < half, place + half, coarse - 1 - place)
    listed = jnp.dot(
        listed.astype(F32).astype(BF16), one_hot(source == wanted), preferred_element_type=F32
    )
    columns = jnp.transpose(listed)
    own = side_by_side(field_ref)
    kinds = kernels_ref.shape[0]
    count = choice_ref.shape[1] // kinds
    stacked = jnp.concatenate([kernels_ref[k] for k in range(kinds)], axis=1)
    lane = lax.broadcasted_iota(jnp.int32, (blocks, blocks), 1).astype(F32)
    entry = lax.broadcasted_iota(jnp.int32, choice_ref.shape, 1).astype(F32)
    arrival = [jnp.zeros((blocks, LANES), F32) for _ in range(levels)]
    choice = jnp.zeros(choice_ref.shape, F32)
    for k in range(2):
        donor = columns[:, k : k + 1] + 16.0 * columns[:, 2 + k : 3 + k]
        kind = columns[:, 4 + k : 5 + k]
        code = jnp.where(donor >= float(blocks), donor - float(blocks) + float(count) * kind, -1.0)
        choice = choice + jnp.where(entry == code, 1.0, 0.0)
        picked = jnp.dot(one_hot(lane == donor), own, preferred_element_type=F32).astype(BF16)
        kind = jnp.broadcast_to(kind, (blocks, LANES))
        for l in range(levels):
            every = jnp.dot(
                picked[:, l * LANES : (l + 1) * LANES], stacked, preferred_element_type=F32
            )
            value = every[:, :LANES]
            for q in range(1, kinds):
                value = jnp.where(kind == float(q), every[:, q * LANES : (q + 1) * LANES], value)
            arrival[l] = arrival[l] + value
    choice_ref[...] = choice.astype(BF16)
    for l in range(levels):
        arrival_ref[l] = arrival[l]

    total = order_ref.shape[0]
    if total == lat * lev * 2 * circles:
        row = lax.broadcasted_iota(jnp.int32, (total, total), 0)
        col = lax.broadcasted_iota(jnp.int32, (total, total), 1)
        group = (row >> log(circles)) & (2 * lev - 1)
        outer = row >> log(circles * 2 * lev)
        target = (group << log(lat * circles)) | (outer << log(circles)) | (row & (circles - 1))
        order_ref[...] = one_hot(col == target)
    else:
        order_ref[...] = jnp.zeros(order_ref.shape, BF16)
    copies[4].wait()


def fold(parts):
    row = lax.broadcasted_iota(jnp.int32, (8, LANES), 0)
    for half in (4, 2, 1):
        low = (row & half) == 0
        count = len(parts) // 2
        parts = [
            jnp.where(low, a, pltpu.roll(b, half, 0)) + jnp.where(low, pltpu.roll(a, 8 - half, 0), b)
            for a, b in zip(parts[:count], parts[count:])
        ]
    return parts[0]


def transform_kernel(
    lengths_ref, wave_ref, far_ref, near_ref, choice_ref, arrival_ref, kernels_ref, fine_ref,
    coarse_ref, out_ref, points_ref, coeff_ref, *, top_wave,
):
    levels, blocks, _ = arrival_ref.shape
    circles, tiles = fine_ref.shape[:2]
    coarse = blocks // circles
    half = coarse // 2
    kinds = kernels_ref.shape[0]
    band = lax.axis_index("lat")
    even = lax.rem(band, 2) == 0

    near, far = near_ref[...], far_ref[...]
    at_end = (band == 0) | (band == lax.axis_size("lat") - 1)
    far = jnp.where(at_end, jnp.zeros_like(far), far)
    halo = jnp.concatenate([jnp.where(even, far, near), jnp.where(even, near, far)], axis=0)
    stacked = jnp.concatenate([kernels_ref[k] for k in range(kinds)], axis=1)
    high, low = [], []
    for l in range(levels):
        every = jnp.dot(
            halo[:, l * LANES : (l + 1) * LANES], stacked, preferred_element_type=F32
        )
        every = jnp.concatenate(
            [every[:, q * LANES : (q + 1) * LANES] for q in range(kinds)], axis=0
        )
        high.append(every.astype(BF16))
        low.append((every - high[-1].astype(F32)).astype(BF16))
    arrival = jnp.dot(
        choice_ref[...], jnp.concatenate(high, axis=1), preferred_element_type=F32
    ) + jnp.dot(choice_ref[...], jnp.concatenate(low, axis=1), preferred_element_type=F32)

    distance = lax.broadcasted_iota(jnp.int32, (coarse, LANES), 0)
    row = jnp.where(distance < half, distance + half, coarse - 1 - distance)
    position = row * LANES + lax.broadcasted_iota(jnp.int32, (coarse, LANES), 1)
    for g in range(circles):
        inside = position < jnp.broadcast_to(lengths_ref[g : g + 1], (coarse, LANES))
        sums, differences = [], []
        for l in range(levels):
            rows = slice(g * coarse, (g + 1) * coarse)
            part = arrival[rows, l * LANES : (l + 1) * LANES] + arrival_ref[l, rows]
            part = jnp.where(inside, part * part, 0.0)
            sums.append(part[:half] + part[half:])
            differences.append(part[:half] - part[half:])
        points_ref[g] = jnp.concatenate(sums + differences, axis=0).astype(BF16)

    height = 2 * circles
    lengths = lengths_ref[...]
    sine = lax.broadcasted_iota(jnp.int32, (height, LANES), 0) >= circles
    sub = lax.broadcasted_iota(jnp.int32, (8, LANES), 0)

    def level_sum(value, l):
        first, last = l * half, (l + 1) * half
        total = None
        for at in range(first // 8 * 8, last, 8):
            piece = value[at : at + 8]
            if at < first:
                piece = jnp.where(sub >= first - at, piece, 0.0)
            if at + 8 > last:
                piece = jnp.where(sub < last - at, piece, 0.0)
            total = piece if total is None else total + piece
        return total

    def tile(t):
        sums = [([], []) for _ in range(levels)]
        for g in range(circles):
            turned = jnp.dot(points_ref[g], fine_ref[g, t], preferred_element_type=F32)
            both, apart = turned[: levels * half], turned[levels * half :]
            c, s = coarse_ref[g, t, :, :LANES], coarse_ref[g, t, :, LANES:]
            real = both[:, :LANES] * c - apart[:, LANES:] * s
            imag = both[:, LANES:] * c + apart[:, :LANES] * s
            for l in range(levels):
                sums[l][0].append(level_sum(real, l))
                sums[l][1].append(level_sum(imag, l))
        waves = jnp.broadcast_to(wave_ref[pl.ds(t, 1), :], (height, LANES))
        live = (waves >= 1) & (waves < top_wave) & (2 * waves < lengths)
        found = []
        for l in range(levels):
            ordered = sums[l][0] + sums[l][1]
            rows = [fold(ordered[i : i + 8]) for i in range(0, height, 8)]
            rows = jnp.concatenate(rows, axis=0)
            found.append(jnp.where(live, jnp.where(sine, -rows, rows), 0.0))
        return jnp.concatenate(found, axis=0)

    def stored(t, _):
        coeff_ref[t] = tile(t)
        return 0

    devices, chunk_rows, _ = out_ref.shape
    width = tiles * LANES // devices
    packs = coeff_ref.shape[1] // chunk_rows
    step = LANES // packs
    lane = lax.broadcasted_iota(jnp.int32, (chunk_rows, LANES), 1)
    if circles * tiles <= 64:
        coeffs = [tile(t) for t in range(tiles)]
    else:
        lax.fori_loop(0, tiles, stored, 0)
        coeffs = [coeff_ref.at[t] for t in range(tiles)]
    for d in range(devices):
        t, shift = divmod(d * width, LANES)
        chunk = jnp.zeros((chunk_rows, LANES), F32)
        for p in range(packs):
            rows = slice(p * chunk_rows, (p + 1) * chunk_rows)
            at = p * step
            value = pltpu.roll(coeffs[t][rows], (at - shift) % LANES, 1)
            if shift + width > LANES:
                after = pltpu.roll(coeffs[t + 1][rows], (at - shift) % LANES, 1)
                value = jnp.where(lane < at + LANES - shift, value, after)
            chunk = value if p == 0 else jnp.where(lane < at, chunk, value)
        out_ref[d] = chunk.astype(BF16)


def legendre_kernel(limits_ref, arrived_ref, order_ref, legendre_ref, out_hbm, out_ref, sems, *, packs):
    outputs, slots, top_wave = out_ref.shape
    circles = legendre_ref.shape[0] // slots
    per_tile = LANES // circles
    total = arrived_ref.shape[0]
    turned = lax.dot_general(
        arrived_ref[...], order_ref[...], CONTRACT_ROWS, preferred_element_type=F32
    )

    sub = lax.broadcasted_iota(jnp.int32, (8, LANES), 0)
    block = lax.broadcasted_iota(jnp.int32, (8, LANES), 1) >> log(circles)
    chosen = [(block == b) & ((sub & (per_tile - 1)) == b) for b in range(per_tile)]
    halves = 8 // per_tile
    in_half = [(sub >> log(per_tile)) == h for h in range(halves)]
    step = LANES // packs
    spread = []
    for k in range(slots // 8):
        pieces = [None] * outputs
        for l in range(packs):
            for j in range(total // LANES):
                at = l * step + 8 * k
                v = turned[at : at + 8, j * LANES : (j + 1) * LANES]
                rolled = [v] + [pltpu.roll(v, circles * d, 1) for d in range(1, per_tile)]
                for i in range(per_tile):
                    a = jnp.zeros((8, LANES), F32)
                    for b in range(per_tile):
                        a = jnp.where(chosen[b], rolled[(b - i) % per_tile], a)
                    group_lev, part = divmod(j * per_tile + i, 2)
                    pieces[(group_lev * packs + l) * 2 + part] = jnp.concatenate(
                        [jnp.where(in_half[h], a, 0.0) for h in range(halves)], axis=1
                    )
        spread.append(jnp.concatenate(pieces, axis=0).astype(BF16))

    wide = 2 * LANES
    lane = lax.broadcasted_iota(jnp.int32, (8, wide), 1)
    limits = [limits_ref[8 * k : 8 * k + 8] for k in range(slots // 8)]
    limits = [jnp.concatenate([m, m], axis=1) for m in limits]
    copies = []
    for n in range(0, top_wave, wide):
        sums = [
            jnp.dot(
                spread[k],
                legendre_ref[8 * k * circles : 8 * (k + 1) * circles, n : n + wide],
                preferred_element_type=F32,
            )
            for k in range(slots // 8)
        ]
        keep = [lane + n >= m for m in limits]
        for o in range(outputs):
            out_ref[o, :, n : n + wide] = jnp.concatenate(
                [jnp.where(keep[k], sums[k][8 * o : 8 * o + 8], 0.0) for k in range(slots // 8)],
                axis=0,
            ).astype(BF16)
        columns = (slice(None), slice(None), pl.ds(n, wide))
        copies.append(
            pltpu.make_async_copy(
                out_ref.at[columns], out_hbm.at[columns], sems.at[n // wide]
            )
        )
        copies[-1].start()
    for copy in copies:
        copy.wait()


def other_neighbours(lat, lev):
    inner = [(i, i + 1) for i in range(1, lat - 1, 2)]
    inner += [(j, i) for i, j in inner]
    pairs = [(i * lev + l, j * lev + l) for i, j in inner for l in range(lev)]
    return pairs + [(i * lev + l, i * lev + (l ^ 1)) for i in (0, lat - 1) for l in range(lev)]


def body(
    grid_field, send_blocks, donor_index, tile_choice, kernel_tiles, circle_len, slot_wave, legendre
):
    levels, blocks, _ = grid_field.shape
    send_count = send_blocks.shape[2]
    slots, circles, top_wave = legendre.shape
    lat, lev = lax.axis_size("lat"), lax.axis_size("lev")
    devices = lat * lev
    coarse = PTS // LANES
    own = blocks // coarse
    tiles = slot_wave.shape[0] // LANES
    waves = slot_wave.reshape(tiles, LANES)

    def like(x):
        return jax.ShapeDtypeStruct(x.shape, x.dtype)

    def in_hbm(x):
        return pltpu.with_memory_space_constraint(x, pltpu.HBM)

    halo = jax.ShapeDtypeStruct((send_count, levels * LANES), BF16)
    to_far, to_near, field, lengths, waves = pl.pallas_call(
        outgoing_kernel,
        out_shape=(
            halo, halo, like(grid_field), jax.ShapeDtypeStruct((2 * own, LANES), jnp.int32), like(waves)
        ),
        in_specs=[HBM] * 4, out_specs=(VMEM,) * 5,
        scratch_shapes=[
            pltpu.VMEM(send_blocks.shape, jnp.int32),
            pltpu.SMEM(circle_len.shape, jnp.int32),
            pltpu.SemaphoreType.DMA((4,)),
        ],
        compiler_params=params(4), name="outgoing",
    )(*map(in_hbm, (send_blocks, grid_field, circle_len, waves)))
    near = lax.ppermute(to_near, "lat", [(i, i ^ 1) for i in range(lat)])
    far = lax.ppermute(to_far, ("lat", "lev"), other_neighbours(lat, lev))

    direct = levels == 2 and 2 * own == 8 and 4 * circles == LANES and slots % 8 == 0
    direct = direct and 2 * slots <= LANES and lev & (lev - 1) == 0
    total = devices * 2 * own if direct else 16
    entries = own * tiles * (LANES + coarse) * 2 * LANES
    donors, kinds = donor_index.T, tile_choice.T
    fine, wide, limits, choice, own_part, kernels, functions, order = pl.pallas_call(
        functools.partial(table_kernel, lat=lat, lev=lev),
        out_shape=(
            jax.ShapeDtypeStruct((own, tiles, LANES, 2 * LANES), BF16),
            jax.ShapeDtypeStruct((own, tiles, levels * coarse // 2, 2 * LANES), F32),
            jax.ShapeDtypeStruct((slots, LANES), jnp.int32),
            jax.ShapeDtypeStruct((blocks, kernel_tiles.shape[0] * 2 * send_count), BF16),
            jax.ShapeDtypeStruct((levels, blocks, LANES), F32),
            like(kernel_tiles),
            like(legendre),
            jax.ShapeDtypeStruct((total, total), BF16),
        ),
        in_specs=[VMEM] * 3 + [HBM] * 5, out_specs=(VMEM,) * 8,
        scratch_shapes=[
            pltpu.SMEM(slot_wave.shape, jnp.int32),
            pltpu.VMEM(donors.shape, jnp.int32),
            pltpu.VMEM(donors.shape, jnp.int32),
            pltpu.SemaphoreType.DMA((5,)),
        ],
        compiler_params=params(32), name="tables",
        cost_estimate=pl.CostEstimate(flops=8 * entries, bytes_accessed=3 * entries, transcendentals=0),
    )(lengths, waves, field, *map(in_hbm, (slot_wave, donors, kinds, kernel_tiles, legendre)))

    rows = levels * 2 * own
    packs = 1
    while rows % (16 * packs) == 0 and 2 * packs * slots <= LANES:
        packs *= 2
    coeffs = pl.pallas_call(
        functools.partial(transform_kernel, top_wave=top_wave),
        out_shape=jax.ShapeDtypeStruct((devices, rows // packs, LANES), BF16),
        in_specs=[VMEM] * 9, out_specs=VMEM,
        scratch_shapes=[
            pltpu.VMEM((own, levels * coarse, LANES), BF16),
            pltpu.VMEM((tiles, rows, LANES), F32),
        ],
        compiler_params=params(40), name="transform",
    )(lengths, waves, far, near, choice, own_part, kernels, fine, wide)
    arrived = lax.all_to_all(coeffs, ("lat", "lev"), 0, 0, tiled=True)

    outputs = lev * levels * 2
    height = rows // packs
    if direct:
        spectra = pl.pallas_call(
            functools.partial(legendre_kernel, packs=packs),
            out_shape=jax.ShapeDtypeStruct((outputs, slots, top_wave), BF16),
            in_specs=[VMEM] * 4, out_specs=HBM,
            scratch_shapes=[
                pltpu.VMEM((outputs, slots, top_wave), BF16),
                pltpu.SemaphoreType.DMA((top_wave // (2 * LANES),)),
            ],
            compiler_params=params(32), name="legendre",
        )(
            limits,
            arrived.reshape(devices * height, LANES),
            order,
            functions.reshape(slots * circles, top_wave),
        )
        return spectra.reshape(outputs // 2, 2, slots, top_wave)

    gathered = arrived.reshape(lat, lev, height, packs, LANES // packs)[..., :slots]
    gathered = gathered.swapaxes(2, 3).reshape(lat, lev, levels, 2, own, slots)
    gathered = gathered.transpose(1, 2, 3, 0, 4, 5).reshape(outputs // 2, 2, circles, slots)
    spectra = jnp.einsum("lcgs,sgn->lcsn", gathered, functions, preferred_element_type=F32)
    first_slot = (lax.axis_index("lat") * lev + lax.axis_index("lev")) * slots
    mine = lax.dynamic_slice_in_dim(slot_wave, first_slot, slots)
    allowed = jnp.arange(top_wave, dtype=jnp.int32)[None, :] >= mine[:, None]
    return jnp.where(allowed[None, None], spectra, 0.0).astype(BF16)


def solution(mesh):
    return jax.shard_map(
        body,
        mesh=mesh,
        in_specs=(
            P("lev", "lat", None),
            P("lat", None, None),
            P("lat", None),
            P("lat", None),
            P(),
            P(),
            P(),
            P(("lat", "lev"), None, None),
        ),
        out_specs=P(None, None, ("lat", "lev"), None),
        check_vma=False,
    )
```

```python
import functools
import math

import jax
import jax.numpy as jnp
from jax import lax
from jax.experimental import pallas as pl
from jax.experimental.pallas import tpu as pltpu
from jax.sharding import PartitionSpec as P

PTS = 5120
LANES = 128
BF16 = jnp.bfloat16
F32 = jnp.float32
VMEM = pl.BlockSpec(memory_space=pltpu.VMEM)
HBM = pl.BlockSpec(memory_space=pltpu.HBM)
CONTRACT_ROWS = (((0,), (0,)), ((), ()))


def params(mebibytes):
    return pltpu.CompilerParams(vmem_limit_bytes=mebibytes << 20)


def one_hot(condition):
    return jnp.where(condition, 1.0, 0.0).astype(BF16)


def side_by_side(field_ref):
    return jnp.concatenate([field_ref[l] for l in range(field_ref.shape[0])], axis=1)


def outgoing_kernel(
    send_hbm, field_hbm, length_hbm, wave_hbm, donor_hbm, tile_hbm,
    far_ref, near_ref, field_ref, lengths_ref, wave_ref, donor_ref, tile_ref,
    send_ref, length_ref, sems,
):
    pairs = (
        (send_hbm, send_ref), (field_hbm, field_ref), (length_hbm, length_ref), (wave_hbm, wave_ref),
        (donor_hbm, donor_ref), (tile_hbm, tile_ref),
    )
    copies = [pltpu.make_async_copy(*pair, sems.at[i]) for i, pair in enumerate(pairs)]
    for copy in copies:
        copy.start()
    copies[0].wait()
    copies[1].wait()
    band = lax.axis_index("lat")
    even = lax.rem(band, 2) == 0
    own = side_by_side(field_ref)
    blocks, count = own.shape[0], send_ref.shape[2]
    rows = lax.broadcasted_iota(jnp.int32, (blocks, count), 0)
    below, above = send_ref[0, 0:1, :], send_ref[0, 1:2, :]
    for ref, listed in (
        (far_ref, jnp.where(even, below, above)),
        (near_ref, jnp.where(even, above, below)),
    ):
        picked = lax.dot_general(
            one_hot(rows == listed), own, CONTRACT_ROWS, preferred_element_type=F32
        )
        ref[...] = picked.astype(BF16)
    copies[2].wait()
    circles = lengths_ref.shape[0] // 2
    for i in range(2 * circles):
        length = length_ref[band * circles + i % circles]
        lengths_ref[i : i + 1] = jnp.full((1, LANES), length, jnp.int32)
    for copy in copies[3:]:
        copy.wait()


SINE = (0.07761395, -0.59827207, 2.55007494, -5.16770998, 3.14159264)
COSINE = (0.21953804, -1.33180992, 4.05840238, -4.93479245, 0.99999995)
ROUND = 1.5 * 2.0**23


def turn(steps, waves, length, inverse):
    phase = steps * waves
    rest = phase - ((phase * inverse + ROUND) - ROUND) * length
    f = rest * inverse
    x = f * f
    s, c = SINE[0], COSINE[0]
    for p, q in zip(SINE[1:], COSINE[1:]):
        s, c = s * x + p, c * x + q
    s = s * f
    twice = s + s
    return 1.0 - twice * s, twice * c


def log(n):
    return n.bit_length() - 1


def times(a, b):
    return a[0] * b[0] - a[1] * b[1], a[0] * b[1] + a[1] * b[0]


def table_kernel(
    lengths_ref, wave_ref, field_ref, donor_ref, tile_ref, slot_hbm, kernels_hbm,
    fine_ref, coarse_ref, limits_ref, choice_ref, arrival_ref, kernels_ref, order_ref,
    slot_ref, sems, *, lat, lev,
):
    circles, tiles = fine_ref.shape[:2]
    levels, blocks, _ = field_ref.shape
    coarse = blocks // circles
    half = coarse // 2
    pairs = ((slot_hbm, slot_ref), (kernels_hbm, kernels_ref))
    copies = [pltpu.make_async_copy(*pair, sems.at[i]) for i, pair in enumerate(pairs)]
    for copy in copies:
        copy.start()
    row = lax.broadcasted_iota(jnp.int32, (8, LANES), 0)
    near_step = (row + LANES // 2 * (coarse - 1)).astype(F32)
    far_step = (row * LANES + LANES // 2).astype(F32)
    hop_step = jnp.left_shift(8, jnp.where(row < 4, row, row - 4 + log(LANES))).astype(F32)

    def doubled(base, hops, groups):
        out = [base]
        while len(out) < groups:
            k = log(len(out))
            hop = tuple(jnp.broadcast_to(x[k : k + 1], (8, LANES)) for x in hops)
            out += [times(e, hop) for e in out[: groups - len(out)]]
        return [jnp.concatenate(part, axis=0) for part in zip(*out)]

    def circle(g):
        length = jnp.broadcast_to(lengths_ref[pl.ds(g, 1)], (8, LANES)).astype(F32)
        return length, 1.0 / length

    def table(g, t, length, inverse):
        waves = jnp.broadcast_to(wave_ref[pl.ds(t, 1), :], (8, LANES)).astype(F32)
        hops = turn(hop_step, waves, length, inverse)
        fine = doubled(turn(near_step, waves, length, inverse), hops, LANES // 8)
        fine_ref[g, t] = jnp.concatenate(fine, axis=1).astype(BF16)
        wide = doubled(
            turn(far_step, waves, length, inverse), tuple(x[4:] for x in hops), -(-half // 8)
        )
        coarse_ref[g, t] = jnp.concatenate(
            [jnp.concatenate([part[:half]] * levels, axis=0) for part in wide], axis=1
        )

    def looped(index, _):
        table(index // tiles, lax.rem(index, tiles), *circle(index // tiles))
        return 0

    place = lax.broadcasted_iota(jnp.int32, (8, blocks), 1)
    begin = jnp.zeros((8, blocks), jnp.int32)
    for g in range(1, circles):
        begin = jnp.where(place >= g * coarse, g * coarse, begin)
    place = place - begin
    wanted = begin + jnp.where(place < half, place + half, coarse - 1 - place)
    source = lax.broadcasted_iota(jnp.int32, (blocks, blocks), 0)
    donor = donor_ref[...]
    listed = jnp.concatenate(
        [donor & 15, donor >> 4, tile_ref[...], jnp.zeros((2, blocks), jnp.int32)], axis=0
    )
    listed = jnp.dot(
        listed.astype(F32).astype(BF16), one_hot(source == wanted[0:1]), preferred_element_type=F32
    )
    columns = jnp.transpose(listed)
    own = side_by_side(field_ref)
    kinds = kernels_ref.shape[0]
    count = choice_ref.shape[1] // kinds
    lane = lax.broadcasted_iota(jnp.int32, (blocks, blocks), 1).astype(F32)
    entry = lax.broadcasted_iota(jnp.int32, choice_ref.shape, 1).astype(F32)
    choice, picked, kind = None, [], []
    for k in range(2):
        donor = columns[:, k : k + 1] + 16.0 * columns[:, 2 + k : 3 + k]
        tile = columns[:, 4 + k : 5 + k]
        code = jnp.where(donor >= float(blocks), donor - float(blocks) + float(count) * tile, -1.0)
        chosen = jnp.where(entry == code, 1.0, 0.0)
        choice = chosen if k == 0 else choice + chosen
        picked.append(
            jnp.dot(one_hot(lane == donor), own, preferred_element_type=F32).astype(BF16)
        )
        kind.append(jnp.broadcast_to(tile, (blocks, LANES)))
    choice_ref[...] = choice.astype(BF16)

    unrolled = circles * tiles <= 64
    if unrolled:
        for g in range(circles):
            for t in range(tiles):
                table(g, t, *circle(g))
    else:
        lax.fori_loop(0, circles * tiles, looped, 0, unroll=2)

    for copy in copies:
        copy.wait()
    stacked = jnp.concatenate([kernels_ref[k] for k in range(kinds)], axis=1)
    for l in range(levels):
        total = None
        for k in range(2):
            every = jnp.dot(
                picked[k][:, l * LANES : (l + 1) * LANES], stacked, preferred_element_type=F32
            )
            value = every[:, :LANES]
            for q in range(1, kinds):
                value = jnp.where(kind[k] == float(q), every[:, q * LANES : (q + 1) * LANES], value)
            total = value if k == 0 else total + value
        arrival_ref[l] = total


    slots = limits_ref.shape[0]
    first = (lax.axis_index("lat") * lev + lax.axis_index("lev")) * slots
    for s in range(slots):
        limits_ref[s : s + 1] = jnp.full((1, LANES), slot_ref[first + s], jnp.int32)

    total = order_ref.shape[0]
    if total == lat * lev * 2 * circles:
        at = lax.broadcasted_iota(jnp.int32, (8, total), 1)
        outer = (at >> log(circles)) & (lat - 1)
        group = at >> log(lat * circles)
        source = (outer << log(circles * 2 * lev)) | (group << log(circles)) | (at & (circles - 1))
        row = lax.broadcasted_iota(jnp.int32, (total, total), 0)
        order_ref[...] = one_hot(row == source[0:1])
    else:
        order_ref[...] = jnp.zeros(order_ref.shape, BF16)


def fold(parts):
    row = lax.broadcasted_iota(jnp.int32, (8, LANES), 0)
    for half in (4, 2, 1):
        low = (row & half) == 0
        count = len(parts) // 2
        parts = [
            jnp.where(low, a, pltpu.roll(b, half, 0)) + jnp.where(low, pltpu.roll(a, 8 - half, 0), b)
            for a, b in zip(parts[:count], parts[count:])
        ]
    return parts[0]


def transform_kernel(
    lengths_ref, wave_ref, far_ref, near_ref, choice_ref, arrival_ref, kernels_ref, fine_ref,
    coarse_ref, out_ref, points_ref, coeff_ref, *, top_wave,
):
    levels, blocks, _ = arrival_ref.shape
    circles, tiles = fine_ref.shape[:2]
    coarse = blocks // circles
    half = coarse // 2
    kinds = kernels_ref.shape[0]
    band = lax.axis_index("lat")
    even = lax.rem(band, 2) == 0

    near, far = near_ref[...], far_ref[...]
    at_end = (band == 0) | (band == lax.axis_size("lat") - 1)
    far = jnp.where(at_end, jnp.zeros_like(far), far)
    halo = jnp.concatenate([jnp.where(even, far, near), jnp.where(even, near, far)], axis=0)
    stacked = jnp.concatenate([kernels_ref[k] for k in range(kinds)], axis=1)
    rows = jnp.concatenate(
        [halo[:, l * LANES : (l + 1) * LANES] for l in range(levels)], axis=0
    )
    every = jnp.dot(rows, stacked, preferred_element_type=F32)
    count = halo.shape[0]
    every = jnp.concatenate(
        [
            jnp.concatenate(
                [every[l * count : (l + 1) * count, q * LANES : (q + 1) * LANES] for q in range(kinds)],
                axis=0,
            )
            for l in range(levels)
        ],
        axis=1,
    )
    high = every.astype(BF16)
    low = (every - high.astype(F32)).astype(BF16)
    arrival = jnp.dot(choice_ref[...], high, preferred_element_type=F32)
    arrival = arrival + jnp.dot(choice_ref[...], low, preferred_element_type=F32)

    distance = lax.broadcasted_iota(jnp.int32, (coarse, LANES), 0)
    row = jnp.where(distance < half, distance + half, coarse - 1 - distance)
    position = row * LANES + lax.broadcasted_iota(jnp.int32, (coarse, LANES), 1)
    for g in range(circles):
        inside = position < jnp.broadcast_to(lengths_ref[g : g + 1], (coarse, LANES))
        sums, differences = [], []
        for l in range(levels):
            rows = slice(g * coarse, (g + 1) * coarse)
            part = arrival[rows, l * LANES : (l + 1) * LANES] + arrival_ref[l, rows]
            part = jnp.where(inside, part * part, 0.0)
            sums.append(part[:half] + part[half:])
            differences.append(part[:half] - part[half:])
        points_ref[g] = jnp.concatenate(sums + differences, axis=0).astype(BF16)

    height = 2 * circles
    lengths = lengths_ref[...]
    sine = lax.broadcasted_iota(jnp.int32, (height, LANES), 0) >= circles
    sub = lax.broadcasted_iota(jnp.int32, (8, LANES), 0)

    def level_sum(value, l):
        first, last = l * half, (l + 1) * half
        total = None
        for at in range(first // 8 * 8, last, 8):
            piece = value[at : at + 8]
            if at < first:
                piece = jnp.where(sub >= first - at, piece, 0.0)
            if at + 8 > last:
                piece = jnp.where(sub < last - at, piece, 0.0)
            total = piece if total is None else total + piece
        return total

    def tile(t):
        sums = [([], []) for _ in range(levels)]
        for g in range(circles):
            turned = jnp.dot(points_ref[g], fine_ref[g, t], preferred_element_type=F32)
            both, apart = turned[: levels * half], turned[levels * half :]
            c, s = coarse_ref[g, t, :, :LANES], coarse_ref[g, t, :, LANES:]
            real = both[:, :LANES] * c - apart[:, LANES:] * s
            imag = both[:, LANES:] * c + apart[:, :LANES] * s
            for l in range(levels):
                sums[l][0].append(level_sum(real, l))
                sums[l][1].append(level_sum(imag, l))
        waves = jnp.broadcast_to(wave_ref[pl.ds(t, 1), :], (height, LANES))
        live = (waves >= 1) & (waves < top_wave) & (2 * waves < lengths)
        found = []
        for l in range(levels):
            ordered = sums[l][0] + sums[l][1]
            rows = [fold(ordered[i : i + 8]) for i in range(0, height, 8)]
            rows = jnp.concatenate(rows, axis=0)
            found.append(jnp.where(live, jnp.where(sine, -rows, rows), 0.0))
        return jnp.concatenate(found, axis=0)

    def stored(t, _):
        coeff_ref[t] = tile(t)
        return 0

    devices, chunk_rows, _ = out_ref.shape
    width = tiles * LANES // devices
    packs = coeff_ref.shape[1] // chunk_rows
    step = LANES // packs
    lane = lax.broadcasted_iota(jnp.int32, (chunk_rows, LANES), 1)
    if circles * tiles <= 64:
        coeffs = [tile(t) for t in range(tiles)]
    else:
        lax.fori_loop(0, tiles, stored, 0)
        coeffs = [coeff_ref.at[t] for t in range(tiles)]
    for d in range(devices):
        t, shift = divmod(d * width, LANES)
        chunk = jnp.zeros((chunk_rows, LANES), F32)
        for p in range(packs):
            rows = slice(p * chunk_rows, (p + 1) * chunk_rows)
            at = p * step
            value = pltpu.roll(coeffs[t][rows], (at - shift) % LANES, 1)
            if shift + width > LANES:
                after = pltpu.roll(coeffs[t + 1][rows], (at - shift) % LANES, 1)
                value = jnp.where(lane < at + LANES - shift, value, after)
            chunk = value if p == 0 else jnp.where(lane < at, chunk, value)
        out_ref[d] = chunk.astype(BF16)


def legendre_kernel(limits_ref, arrived_ref, order_ref, legendre_ref, out_hbm, out_ref, sems, *, packs):
    outputs, slots, top_wave = out_ref.shape
    circles = legendre_ref.shape[0] // slots
    per_tile = LANES // circles
    total = arrived_ref.shape[0]
    turned = lax.dot_general(
        arrived_ref[...], order_ref[...], CONTRACT_ROWS, preferred_element_type=F32
    )

    sub = lax.broadcasted_iota(jnp.int32, (8, LANES), 0)
    block = lax.broadcasted_iota(jnp.int32, (8, LANES), 1) >> log(circles)
    chosen = [(block == b) & ((sub & (per_tile - 1)) == b) for b in range(per_tile)]
    halves = 8 // per_tile
    in_half = [(sub >> log(per_tile)) == h for h in range(halves)]
    step = LANES // packs
    spread = []
    for k in range(slots // 8):
        pieces = [None] * outputs
        for l in range(packs):
            for j in range(total // LANES):
                at = l * step + 8 * k
                v = turned[at : at + 8, j * LANES : (j + 1) * LANES]
                rolled = [v] + [pltpu.roll(v, circles * d, 1) for d in range(1, per_tile)]
                for i in range(per_tile):
                    a = jnp.zeros((8, LANES), F32)
                    for b in range(per_tile):
                        a = jnp.where(chosen[b], rolled[(b - i) % per_tile], a)
                    group_lev, part = divmod(j * per_tile + i, 2)
                    pieces[(group_lev * packs + l) * 2 + part] = jnp.concatenate(
                        [jnp.where(in_half[h], a, 0.0) for h in range(halves)], axis=1
                    )
        spread.append(jnp.concatenate(pieces, axis=0).astype(BF16))

    wide = 2 * LANES
    lane = lax.broadcasted_iota(jnp.int32, (8, wide), 1)
    limits = [limits_ref[8 * k : 8 * k + 8] for k in range(slots // 8)]
    limits = [jnp.concatenate([m, m], axis=1) for m in limits]
    copies = []
    for n in range(0, top_wave, wide):
        sums = [
            jnp.dot(
                spread[k],
                legendre_ref[8 * k * circles : 8 * (k + 1) * circles, n : n + wide],
                preferred_element_type=F32,
            )
            for k in range(slots // 8)
        ]
        keep = [lane + n >= m for m in limits]
        for o in range(outputs):
            out_ref[o, :, n : n + wide] = jnp.concatenate(
                [jnp.where(keep[k], sums[k][8 * o : 8 * o + 8], 0.0) for k in range(slots // 8)],
                axis=0,
            ).astype(BF16)
        columns = (slice(None), slice(None), pl.ds(n, wide))
        copies.append(
            pltpu.make_async_copy(
                out_ref.at[columns], out_hbm.at[columns], sems.at[n // wide]
            )
        )
        copies[-1].start()
    for copy in copies:
        copy.wait()


def other_neighbours(lat, lev):
    inner = [(i, i + 1) for i in range(1, lat - 1, 2)]
    inner += [(j, i) for i, j in inner]
    pairs = [(i * lev + l, j * lev + l) for i, j in inner for l in range(lev)]
    return pairs + [(i * lev + l, i * lev + (l ^ 1)) for i in (0, lat - 1) for l in range(lev)]


def body(
    grid_field, send_blocks, donor_index, tile_choice, kernel_tiles, circle_len, slot_wave, legendre
):
    levels, blocks, _ = grid_field.shape
    send_count = send_blocks.shape[2]
    slots, circles, top_wave = legendre.shape
    lat, lev = lax.axis_size("lat"), lax.axis_size("lev")
    devices = lat * lev
    coarse = PTS // LANES
    own = blocks // coarse
    tiles = slot_wave.shape[0] // LANES
    waves = slot_wave.reshape(tiles, LANES)

    def like(x):
        return jax.ShapeDtypeStruct(x.shape, x.dtype)

    def in_hbm(x):
        return pltpu.with_memory_space_constraint(x, pltpu.HBM)

    halo = jax.ShapeDtypeStruct((send_count, levels * LANES), BF16)
    donors, kinds = donor_index.T, tile_choice.T
    to_far, to_near, field, lengths, waves, donors, kinds = pl.pallas_call(
        outgoing_kernel,
        out_shape=(
            halo, halo, like(grid_field), jax.ShapeDtypeStruct((2 * own, LANES), jnp.int32),
            like(waves), like(donors), like(kinds),
        ),
        in_specs=[HBM] * 6, out_specs=(VMEM,) * 7,
        scratch_shapes=[
            pltpu.VMEM(send_blocks.shape, jnp.int32),
            pltpu.SMEM(circle_len.shape, jnp.int32),
            pltpu.SemaphoreType.DMA((6,)),
        ],
        compiler_params=params(4), name="outgoing",
    )(*map(in_hbm, (send_blocks, grid_field, circle_len, waves, donors, kinds)))
    near = lax.ppermute(to_near, "lat", [(i, i ^ 1) for i in range(lat)])
    far = lax.ppermute(to_far, ("lat", "lev"), other_neighbours(lat, lev))

    direct = levels == 2 and 2 * own == 8 and 4 * circles == LANES and slots % 8 == 0
    direct = direct and 2 * slots <= LANES and lev & (lev - 1) == 0
    total = devices * 2 * own if direct else 16
    entries = own * tiles * (LANES + coarse) * 2 * LANES
    fine, wide, limits, choice, own_part, kernels, order = pl.pallas_call(
        functools.partial(table_kernel, lat=lat, lev=lev),
        out_shape=(
            jax.ShapeDtypeStruct((own, tiles, LANES, 2 * LANES), BF16),
            jax.ShapeDtypeStruct((own, tiles, levels * coarse // 2, 2 * LANES), F32),
            jax.ShapeDtypeStruct((slots, LANES), jnp.int32),
            jax.ShapeDtypeStruct((blocks, kernel_tiles.shape[0] * 2 * send_count), BF16),
            jax.ShapeDtypeStruct((levels, blocks, LANES), F32),
            like(kernel_tiles),
            jax.ShapeDtypeStruct((total, total), BF16),
        ),
        in_specs=[VMEM] * 5 + [HBM] * 2, out_specs=(VMEM,) * 7,
        scratch_shapes=[
            pltpu.SMEM(slot_wave.shape, jnp.int32),
            pltpu.SemaphoreType.DMA((2,)),
        ],
        compiler_params=params(32), name="tables",
        cost_estimate=pl.CostEstimate(flops=8 * entries, bytes_accessed=3 * entries, transcendentals=0),
    )(lengths, waves, field, donors, kinds, *map(in_hbm, (slot_wave, kernel_tiles)))

    rows = levels * 2 * own
    packs = 1
    while rows % (16 * packs) == 0 and 2 * packs * slots <= LANES:
        packs *= 2
    coeffs = pl.pallas_call(
        functools.partial(transform_kernel, top_wave=top_wave),
        out_shape=jax.ShapeDtypeStruct((devices, rows // packs, LANES), BF16),
        in_specs=[VMEM] * 9, out_specs=VMEM,
        scratch_shapes=[
            pltpu.VMEM((own, levels * coarse, LANES), BF16),
            pltpu.VMEM((tiles, rows, LANES), F32),
        ],
        compiler_params=params(40), name="transform",
    )(lengths, waves, far, near, choice, own_part, kernels, fine, wide)
    arrived = lax.all_to_all(coeffs, ("lat", "lev"), 0, 0, tiled=True)

    outputs = lev * levels * 2
    height = rows // packs
    if direct:
        spectra = pl.pallas_call(
            functools.partial(legendre_kernel, packs=packs),
            out_shape=jax.ShapeDtypeStruct((outputs, slots, top_wave), BF16),
            in_specs=[VMEM] * 4, out_specs=HBM,
            scratch_shapes=[
                pltpu.VMEM((outputs, slots, top_wave), BF16),
                pltpu.SemaphoreType.DMA((top_wave // (2 * LANES),)),
            ],
            compiler_params=params(32), name="legendre",
        )(
            limits,
            arrived.reshape(devices * height, LANES),
            order,
            legendre.reshape(slots * circles, top_wave),
        )
        return spectra.reshape(outputs // 2, 2, slots, top_wave)

    gathered = arrived.reshape(lat, lev, height, packs, LANES // packs)[..., :slots]
    gathered = gathered.swapaxes(2, 3).reshape(lat, lev, levels, 2, own, slots)
    gathered = gathered.transpose(1, 2, 3, 0, 4, 5).reshape(outputs // 2, 2, circles, slots)
    spectra = jnp.einsum("lcgs,sgn->lcsn", gathered, legendre, preferred_element_type=F32)
    first_slot = (lax.axis_index("lat") * lev + lax.axis_index("lev")) * slots
    mine = lax.dynamic_slice_in_dim(slot_wave, first_slot, slots)
    allowed = jnp.arange(top_wave, dtype=jnp.int32)[None, :] >= mine[:, None]
    return jnp.where(allowed[None, None], spectra, 0.0).astype(BF16)


def solution(mesh):
    return jax.shard_map(
        body,
        mesh=mesh,
        in_specs=(
            P("lev", "lat", None),
            P("lat", None, None),
            P("lat", None),
            P("lat", None),
            P(),
            P(),
            P(),
            P(("lat", "lev"), None, None),
        ),
        out_specs=P(None, None, ("lat", "lev"), None),
        check_vma=False,
    )
```

```python
import functools
import math

import jax
import jax.numpy as jnp
from jax import lax
from jax.experimental import pallas as pl
from jax.experimental.pallas import tpu as pltpu
from jax.sharding import PartitionSpec as P

PTS = 5120
LANES = 128
BF16 = jnp.bfloat16
F32 = jnp.float32
VMEM = pl.BlockSpec(memory_space=pltpu.VMEM)
HBM = pl.BlockSpec(memory_space=pltpu.HBM)
CONTRACT_ROWS = (((0,), (0,)), ((), ()))


def params(mebibytes):
    return pltpu.CompilerParams(vmem_limit_bytes=mebibytes << 20)


def one_hot(condition):
    return jnp.where(condition, 1.0, 0.0).astype(BF16)


def side_by_side(field_ref):
    return jnp.concatenate([field_ref[l] for l in range(field_ref.shape[0])], axis=1)


def outgoing_kernel(
    send_hbm, field_hbm, length_hbm, wave_hbm, donor_hbm, tile_hbm, kernels_hbm,
    far_ref, near_ref, field_ref, lengths_ref, wave_ref, donor_ref, tile_ref, kernels_ref,
    send_ref, length_ref, sems,
):
    pairs = (
        (send_hbm, send_ref), (field_hbm, field_ref), (length_hbm, length_ref), (wave_hbm, wave_ref),
        (donor_hbm, donor_ref), (tile_hbm, tile_ref), (kernels_hbm, kernels_ref),
    )
    copies = [pltpu.make_async_copy(*pair, sems.at[i]) for i, pair in enumerate(pairs)]
    for copy in copies:
        copy.start()
    copies[0].wait()
    copies[1].wait()
    band = lax.axis_index("lat")
    even = lax.rem(band, 2) == 0
    own = side_by_side(field_ref)
    blocks, count = own.shape[0], send_ref.shape[2]
    rows = lax.broadcasted_iota(jnp.int32, (blocks, count), 0)
    below, above = send_ref[0, 0:1, :], send_ref[0, 1:2, :]
    for ref, listed in (
        (far_ref, jnp.where(even, below, above)),
        (near_ref, jnp.where(even, above, below)),
    ):
        picked = lax.dot_general(
            one_hot(rows == listed), own, CONTRACT_ROWS, preferred_element_type=F32
        )
        ref[...] = picked.astype(BF16)
    copies[2].wait()
    circles = lengths_ref.shape[0] // 2
    for i in range(2 * circles):
        length = length_ref[band * circles + i % circles]
        lengths_ref[i : i + 1] = jnp.full((1, LANES), length, jnp.int32)
    for copy in copies[3:]:
        copy.wait()


SINE = (0.07761395, -0.59827207, 2.55007494, -5.16770998, 3.14159264)
COSINE = (0.21953804, -1.33180992, 4.05840238, -4.93479245, 0.99999995)
ROUND = 1.5 * 2.0**23


def turn(steps, waves, length, inverse):
    phase = steps * waves
    rest = phase - ((phase * inverse + ROUND) - ROUND) * length
    f = rest * inverse
    x = f * f
    s, c = SINE[0], COSINE[0]
    for p, q in zip(SINE[1:], COSINE[1:]):
        s, c = s * x + p, c * x + q
    s = s * f
    twice = s + s
    return 1.0 - twice * s, twice * c


def log(n):
    return n.bit_length() - 1


def times(a, b):
    return a[0] * b[0] - a[1] * b[1], a[0] * b[1] + a[1] * b[0]


def folded_order(array, coarse):
    half, count = coarse // 2, coarse // 8
    assert coarse % 8 == 0 and half % 8 == 4
    sub = lax.broadcasted_iota(jnp.int32, (8, array.shape[1]), 0)

    def reverse(v):
        v = pltpu.roll(v, 4, 0)
        for h in (2, 1):
            v = jnp.where((sub & h) == 0, pltpu.roll(v, 8 - h, 0), pltpu.roll(v, h, 0))
        return v

    out = []
    for begin in range(0, array.shape[0], coarse):
        rows = [array[begin + 8 * i : begin + 8 * i + 8] for i in range(count)]
        swapped = {i: pltpu.roll(rows[i], 4, 0) for i in range(half // 8, count)}
        for i in range(count):
            q = (8 * i + half) // 8
            if 8 * i + 8 <= half:
                out.append(jnp.where(sub < 4, swapped[q], swapped[q + 1]))
            elif 8 * i < half:
                out.append(jnp.where(sub < 4, swapped[q], reverse(rows[count - 1 - i])))
            else:
                out.append(reverse(rows[count - 1 - i]))
    return jnp.concatenate(out, axis=0)


def table_kernel(
    lengths_ref, wave_ref, field_ref, donor_ref, tile_ref, kernels_ref, slot_hbm,
    fine_ref, coarse_ref, limits_ref, choice_ref, arrival_ref, order_ref,
    slot_ref, sem, *, lat, lev,
):
    circles, tiles = fine_ref.shape[:2]
    levels, blocks, _ = field_ref.shape
    coarse = blocks // circles
    half = coarse // 2
    fetch = pltpu.make_async_copy(slot_hbm, slot_ref, sem)
    fetch.start()
    row = lax.broadcasted_iota(jnp.int32, (8, LANES), 0)
    near_step = (row + LANES // 2 * (coarse - 1)).astype(F32)
    far_step = (row * LANES + LANES // 2).astype(F32)
    hop_step = jnp.left_shift(8, jnp.where(row < 4, row, row - 4 + log(LANES))).astype(F32)

    def doubled(base, hops, groups):
        out = [base]
        while len(out) < groups:
            k = log(len(out))
            hop = tuple(jnp.broadcast_to(x[k : k + 1], (8, LANES)) for x in hops)
            out += [times(e, hop) for e in out[: groups - len(out)]]
        return [jnp.concatenate(part, axis=0) for part in zip(*out)]

    def circle(g):
        length = jnp.broadcast_to(lengths_ref[pl.ds(g, 1)], (8, LANES)).astype(F32)
        return length, 1.0 / length

    def table(g, t, length, inverse):
        waves = jnp.broadcast_to(wave_ref[pl.ds(t, 1), :], (8, LANES)).astype(F32)
        hops = turn(hop_step, waves, length, inverse)
        fine = doubled(turn(near_step, waves, length, inverse), hops, LANES // 8)
        fine_ref[g, t] = jnp.concatenate(fine, axis=1).astype(BF16)
        wide = doubled(
            turn(far_step, waves, length, inverse), tuple(x[4:] for x in hops), -(-half // 8)
        )
        coarse_ref[g, t] = jnp.concatenate(
            [jnp.concatenate([part[:half]] * levels, axis=0) for part in wide], axis=1
        )

    def looped(index, _):
        table(index // tiles, lax.rem(index, tiles), *circle(index // tiles))
        return 0

    listed = jnp.concatenate(
        [donor_ref[...], tile_ref[...], jnp.zeros((4, blocks), jnp.int32)], axis=0
    )
    columns = folded_order(jnp.transpose(listed.astype(F32)), coarse)
    own = side_by_side(field_ref)
    kinds = kernels_ref.shape[0]
    count = choice_ref.shape[1] // kinds
    lane = lax.broadcasted_iota(jnp.int32, (blocks, blocks), 1).astype(F32)
    entry = lax.broadcasted_iota(jnp.int32, choice_ref.shape, 1).astype(F32)
    choice, picked, kind = None, [], []
    for k in range(2):
        donor = columns[:, k : k + 1]
        tile = columns[:, 2 + k : 3 + k]
        code = jnp.where(donor >= float(blocks), donor - float(blocks) + float(count) * tile, -1.0)
        chosen = jnp.where(entry == code, 1.0, 0.0)
        choice = chosen if k == 0 else choice + chosen
        picked.append(
            jnp.dot(one_hot(lane == donor), own, preferred_element_type=F32).astype(BF16)
        )
        kind.append(jnp.broadcast_to(tile, (blocks, LANES)))
    choice_ref[...] = choice.astype(BF16)

    stacked = jnp.concatenate([kernels_ref[k] for k in range(kinds)], axis=1)
    for l in range(levels):
        total = None
        for k in range(2):
            every = jnp.dot(
                picked[k][:, l * LANES : (l + 1) * LANES], stacked, preferred_element_type=F32
            )
            value = every[:, :LANES]
            for q in range(1, kinds):
                value = jnp.where(kind[k] == float(q), every[:, q * LANES : (q + 1) * LANES], value)
            total = value if k == 0 else total + value
        arrival_ref[l] = total

    unrolled = circles * tiles <= 64
    if unrolled:
        for g in range(circles):
            for t in range(tiles):
                table(g, t, *circle(g))
    else:
        lax.fori_loop(0, circles * tiles, looped, 0, unroll=2)

    fetch.wait()
    slots = limits_ref.shape[0]
    first = (lax.axis_index("lat") * lev + lax.axis_index("lev")) * slots
    for s in range(slots):
        limits_ref[s : s + 1] = jnp.full((1, LANES), slot_ref[first + s], jnp.int32)

    total = order_ref.shape[0]
    if total == lat * lev * 2 * circles:
        at = lax.broadcasted_iota(jnp.int32, (8, total), 1)
        outer = (at >> log(circles)) & (lat - 1)
        group = at >> log(lat * circles)
        source = (outer << log(circles * 2 * lev)) | (group << log(circles)) | (at & (circles - 1))
        row = lax.broadcasted_iota(jnp.int32, (total, total), 0)
        order_ref[...] = one_hot(row == source[0:1])
    else:
        order_ref[...] = jnp.zeros(order_ref.shape, BF16)


def fold(parts):
    row = lax.broadcasted_iota(jnp.int32, (8, LANES), 0)
    for half in (4, 2, 1):
        low = (row & half) == 0
        count = len(parts) // 2
        parts = [
            jnp.where(low, a, pltpu.roll(b, half, 0)) + jnp.where(low, pltpu.roll(a, 8 - half, 0), b)
            for a, b in zip(parts[:count], parts[count:])
        ]
    return parts[0]


def transform_kernel(
    lengths_ref, wave_ref, far_ref, near_ref, choice_ref, arrival_ref, kernels_ref, fine_ref,
    coarse_ref, out_ref, points_ref, coeff_ref, *, top_wave,
):
    levels, blocks, _ = arrival_ref.shape
    circles, tiles = fine_ref.shape[:2]
    coarse = blocks // circles
    half = coarse // 2
    kinds = kernels_ref.shape[0]
    band = lax.axis_index("lat")
    even = lax.rem(band, 2) == 0

    near, far = near_ref[...], far_ref[...]
    at_end = (band == 0) | (band == lax.axis_size("lat") - 1)
    far = jnp.where(at_end, jnp.zeros_like(far), far)
    halo = jnp.concatenate([jnp.where(even, far, near), jnp.where(even, near, far)], axis=0)
    stacked = jnp.concatenate([kernels_ref[k] for k in range(kinds)], axis=1)
    rows = jnp.concatenate(
        [halo[:, l * LANES : (l + 1) * LANES] for l in range(levels)], axis=0
    )
    every = jnp.dot(rows, stacked, preferred_element_type=F32)
    count = halo.shape[0]
    every = jnp.concatenate(
        [
            jnp.concatenate(
                [every[l * count : (l + 1) * count, q * LANES : (q + 1) * LANES] for q in range(kinds)],
                axis=0,
            )
            for l in range(levels)
        ],
        axis=1,
    )
    high = every.astype(BF16)
    low = (every - high.astype(F32)).astype(BF16)
    arrival = jnp.dot(choice_ref[...], high, preferred_element_type=F32)
    arrival = arrival + jnp.dot(choice_ref[...], low, preferred_element_type=F32)

    distance = lax.broadcasted_iota(jnp.int32, (coarse, LANES), 0)
    row = jnp.where(distance < half, distance + half, coarse - 1 - distance)
    position = row * LANES + lax.broadcasted_iota(jnp.int32, (coarse, LANES), 1)
    for g in range(circles):
        inside = position < jnp.broadcast_to(lengths_ref[g : g + 1], (coarse, LANES))
        sums, differences = [], []
        for l in range(levels):
            rows = slice(g * coarse, (g + 1) * coarse)
            part = arrival[rows, l * LANES : (l + 1) * LANES] + arrival_ref[l, rows]
            part = jnp.where(inside, part * part, 0.0)
            sums.append(part[:half] + part[half:])
            differences.append(part[:half] - part[half:])
        points_ref[g] = jnp.concatenate(sums + differences, axis=0).astype(BF16)

    height = 2 * circles
    lengths = lengths_ref[...]
    sine = lax.broadcasted_iota(jnp.int32, (height, LANES), 0) >= circles
    sub = lax.broadcasted_iota(jnp.int32, (8, LANES), 0)

    def level_sum(value, l):
        first, last = l * half, (l + 1) * half
        total = None
        for at in range(first // 8 * 8, last, 8):
            piece = value[at : at + 8]
            if at < first:
                piece = jnp.where(sub >= first - at, piece, 0.0)
            if at + 8 > last:
                piece = jnp.where(sub < last - at, piece, 0.0)
            total = piece if total is None else total + piece
        return total

    def tile(t):
        sums = [([], []) for _ in range(levels)]
        for g in range(circles):
            turned = jnp.dot(points_ref[g], fine_ref[g, t], preferred_element_type=F32)
            both, apart = turned[: levels * half], turned[levels * half :]
            c, s = coarse_ref[g, t, :, :LANES], coarse_ref[g, t, :, LANES:]
            real = both[:, :LANES] * c - apart[:, LANES:] * s
            imag = both[:, LANES:] * c + apart[:, :LANES] * s
            for l in range(levels):
                sums[l][0].append(level_sum(real, l))
                sums[l][1].append(level_sum(imag, l))
        waves = jnp.broadcast_to(wave_ref[pl.ds(t, 1), :], (height, LANES))
        live = (waves >= 1) & (waves < top_wave) & (2 * waves < lengths)
        found = []
        for l in range(levels):
            ordered = sums[l][0] + sums[l][1]
            rows = [fold(ordered[i : i + 8]) for i in range(0, height, 8)]
            rows = jnp.concatenate(rows, axis=0)
            found.append(jnp.where(live, jnp.where(sine, -rows, rows), 0.0))
        return jnp.concatenate(found, axis=0)

    def stored(t, _):
        coeff_ref[t] = tile(t)
        return 0

    devices, chunk_rows, _ = out_ref.shape
    width = tiles * LANES // devices
    packs = coeff_ref.shape[1] // chunk_rows
    step = LANES // packs
    lane = lax.broadcasted_iota(jnp.int32, (chunk_rows, LANES), 1)
    if circles * tiles <= 64:
        coeffs = [tile(t) for t in range(tiles)]
    else:
        lax.fori_loop(0, tiles, stored, 0)
        coeffs = [coeff_ref.at[t] for t in range(tiles)]
    for d in range(devices):
        t, shift = divmod(d * width, LANES)
        chunk = jnp.zeros((chunk_rows, LANES), F32)
        for p in range(packs):
            rows = slice(p * chunk_rows, (p + 1) * chunk_rows)
            at = p * step
            value = pltpu.roll(coeffs[t][rows], (at - shift) % LANES, 1)
            if shift + width > LANES:
                after = pltpu.roll(coeffs[t + 1][rows], (at - shift) % LANES, 1)
                value = jnp.where(lane < at + LANES - shift, value, after)
            chunk = value if p == 0 else jnp.where(lane < at, chunk, value)
        out_ref[d] = chunk.astype(BF16)


def legendre_kernel(limits_ref, arrived_ref, order_ref, legendre_ref, out_hbm, out_ref, sems, *, packs):
    outputs, slots, top_wave = out_ref.shape
    circles = legendre_ref.shape[0] // slots
    per_tile = LANES // circles
    total = arrived_ref.shape[0]
    turned = lax.dot_general(
        arrived_ref[...], order_ref[...], CONTRACT_ROWS, preferred_element_type=F32
    )

    sub = lax.broadcasted_iota(jnp.int32, (8, LANES), 0)
    block = lax.broadcasted_iota(jnp.int32, (8, LANES), 1) >> log(circles)
    chosen = [(block == b) & ((sub & (per_tile - 1)) == b) for b in range(per_tile)]
    halves = 8 // per_tile
    in_half = [(sub >> log(per_tile)) == h for h in range(halves)]
    step = LANES // packs
    spread = []
    for k in range(slots // 8):
        pieces = [None] * outputs
        for l in range(packs):
            for j in range(total // LANES):
                at = l * step + 8 * k
                v = turned[at : at + 8, j * LANES : (j + 1) * LANES]
                rolled = [v] + [pltpu.roll(v, circles * d, 1) for d in range(1, per_tile)]
                for i in range(per_tile):
                    a = jnp.zeros((8, LANES), F32)
                    for b in range(per_tile):
                        a = jnp.where(chosen[b], rolled[(b - i) % per_tile], a)
                    group_lev, part = divmod(j * per_tile + i, 2)
                    pieces[(group_lev * packs + l) * 2 + part] = jnp.concatenate(
                        [jnp.where(in_half[h], a, 0.0) for h in range(halves)], axis=1
                    )
        spread.append(jnp.concatenate(pieces, axis=0).astype(BF16))

    wide = 2 * LANES
    lane = lax.broadcasted_iota(jnp.int32, (8, wide), 1)
    limits = [limits_ref[8 * k : 8 * k + 8] for k in range(slots // 8)]
    limits = [jnp.concatenate([m, m], axis=1) for m in limits]
    copies = []
    for n in range(0, top_wave, wide):
        sums = [
            jnp.dot(
                spread[k],
                legendre_ref[8 * k * circles : 8 * (k + 1) * circles, n : n + wide],
                preferred_element_type=F32,
            )
            for k in range(slots // 8)
        ]
        keep = [lane + n >= m for m in limits]
        for o in range(outputs):
            out_ref[o, :, n : n + wide] = jnp.concatenate(
                [jnp.where(keep[k], sums[k][8 * o : 8 * o + 8], 0.0) for k in range(slots // 8)],
                axis=0,
            ).astype(BF16)
        columns = (slice(None), slice(None), pl.ds(n, wide))
        copies.append(
            pltpu.make_async_copy(
                out_ref.at[columns], out_hbm.at[columns], sems.at[n // wide]
            )
        )
        copies[-1].start()
    for copy in copies:
        copy.wait()


def other_neighbours(lat, lev):
    inner = [(i, i + 1) for i in range(1, lat - 1, 2)]
    inner += [(j, i) for i, j in inner]
    pairs = [(i * lev + l, j * lev + l) for i, j in inner for l in range(lev)]
    return pairs + [(i * lev + l, i * lev + (l ^ 1)) for i in (0, lat - 1) for l in range(lev)]


def body(
    grid_field, send_blocks, donor_index, tile_choice, kernel_tiles, circle_len, slot_wave, legendre
):
    levels, blocks, _ = grid_field.shape
    send_count = send_blocks.shape[2]
    slots, circles, top_wave = legendre.shape
    lat, lev = lax.axis_size("lat"), lax.axis_size("lev")
    devices = lat * lev
    coarse = PTS // LANES
    own = blocks // coarse
    tiles = slot_wave.shape[0] // LANES
    waves = slot_wave.reshape(tiles, LANES)

    def like(x):
        return jax.ShapeDtypeStruct(x.shape, x.dtype)

    def in_hbm(x):
        return pltpu.with_memory_space_constraint(x, pltpu.HBM)

    halo = jax.ShapeDtypeStruct((send_count, levels * LANES), BF16)
    donors, kinds = donor_index.T, tile_choice.T
    to_far, to_near, field, lengths, waves, donors, kinds, kernels = pl.pallas_call(
        outgoing_kernel,
        out_shape=(
            halo, halo, like(grid_field), jax.ShapeDtypeStruct((2 * own, LANES), jnp.int32),
            like(waves), like(donors), like(kinds), like(kernel_tiles),
        ),
        in_specs=[HBM] * 7, out_specs=(VMEM,) * 8,
        scratch_shapes=[
            pltpu.VMEM(send_blocks.shape, jnp.int32),
            pltpu.SMEM(circle_len.shape, jnp.int32),
            pltpu.SemaphoreType.DMA((7,)),
        ],
        compiler_params=params(4), name="outgoing",
    )(
        *map(in_hbm, (send_blocks, grid_field, circle_len, waves, donors, kinds, kernel_tiles))
    )
    near = lax.ppermute(to_near, "lat", [(i, i ^ 1) for i in range(lat)])
    far = lax.ppermute(to_far, ("lat", "lev"), other_neighbours(lat, lev))

    direct = levels == 2 and 2 * own == 8 and 4 * circles == LANES and slots % 8 == 0
    direct = direct and 2 * slots <= LANES and lev & (lev - 1) == 0
    total = devices * 2 * own if direct else 16
    entries = own * tiles * (LANES + coarse) * 2 * LANES
    fine, wide, limits, choice, own_part, order = pl.pallas_call(
        functools.partial(table_kernel, lat=lat, lev=lev),
        out_shape=(
            jax.ShapeDtypeStruct((own, tiles, LANES, 2 * LANES), BF16),
            jax.ShapeDtypeStruct((own, tiles, levels * coarse // 2, 2 * LANES), F32),
            jax.ShapeDtypeStruct((slots, LANES), jnp.int32),
            jax.ShapeDtypeStruct((blocks, kernel_tiles.shape[0] * 2 * send_count), BF16),
            jax.ShapeDtypeStruct((levels, blocks, LANES), F32),
            jax.ShapeDtypeStruct((total, total), BF16),
        ),
        in_specs=[VMEM] * 6 + [HBM], out_specs=(VMEM,) * 6,
        scratch_shapes=[
            pltpu.SMEM(slot_wave.shape, jnp.int32),
            pltpu.SemaphoreType.DMA,
        ],
        compiler_params=params(32), name="tables",
        cost_estimate=pl.CostEstimate(flops=8 * entries, bytes_accessed=3 * entries, transcendentals=0),
    )(lengths, waves, field, donors, kinds, kernels, in_hbm(slot_wave))

    rows = levels * 2 * own
    packs = 1
    while rows % (16 * packs) == 0 and 2 * packs * slots <= LANES:
        packs *= 2
    coeffs = pl.pallas_call(
        functools.partial(transform_kernel, top_wave=top_wave),
        out_shape=jax.ShapeDtypeStruct((devices, rows // packs, LANES), BF16),
        in_specs=[VMEM] * 9, out_specs=VMEM,
        scratch_shapes=[
            pltpu.VMEM((own, levels * coarse, LANES), BF16),
            pltpu.VMEM((tiles, rows, LANES), F32),
        ],
        compiler_params=params(40), name="transform",
    )(lengths, waves, far, near, choice, own_part, kernels, fine, wide)
    arrived = lax.all_to_all(coeffs, ("lat", "lev"), 0, 0, tiled=True)

    outputs = lev * levels * 2
    height = rows // packs
    if direct:
        spectra = pl.pallas_call(
            functools.partial(legendre_kernel, packs=packs),
            out_shape=jax.ShapeDtypeStruct((outputs, slots, top_wave), BF16),
            in_specs=[VMEM] * 4, out_specs=HBM,
            scratch_shapes=[
                pltpu.VMEM((outputs, slots, top_wave), BF16),
                pltpu.SemaphoreType.DMA((top_wave // (2 * LANES),)),
            ],
            compiler_params=params(32), name="legendre",
        )(
            limits,
            arrived.reshape(devices * height, LANES),
            order,
            legendre.reshape(slots * circles, top_wave),
        )
        return spectra.reshape(outputs // 2, 2, slots, top_wave)

    gathered = arrived.reshape(lat, lev, height, packs, LANES // packs)[..., :slots]
    gathered = gathered.swapaxes(2, 3).reshape(lat, lev, levels, 2, own, slots)
    gathered = gathered.transpose(1, 2, 3, 0, 4, 5).reshape(outputs // 2, 2, circles, slots)
    spectra = jnp.einsum("lcgs,sgn->lcsn", gathered, legendre, preferred_element_type=F32)
    first_slot = (lax.axis_index("lat") * lev + lax.axis_index("lev")) * slots
    mine = lax.dynamic_slice_in_dim(slot_wave, first_slot, slots)
    allowed = jnp.arange(top_wave, dtype=jnp.int32)[None, :] >= mine[:, None]
    return jnp.where(allowed[None, None], spectra, 0.0).astype(BF16)


def solution(mesh):
    return jax.shard_map(
        body,
        mesh=mesh,
        in_specs=(
            P("lev", "lat", None),
            P("lat", None, None),
            P("lat", None),
            P("lat", None),
            P(),
            P(),
            P(),
            P(("lat", "lev"), None, None),
        ),
        out_specs=P(None, None, ("lat", "lev"), None),
        check_vma=False,
    )
```

```python
import functools
import math

import jax
import jax.numpy as jnp
from jax import lax
from jax.experimental import pallas as pl
from jax.experimental.pallas import tpu as pltpu
from jax.sharding import PartitionSpec as P

PTS = 5120
LANES = 128
BF16 = jnp.bfloat16
F32 = jnp.float32
VMEM = pl.BlockSpec(memory_space=pltpu.VMEM)
HBM = pl.BlockSpec(memory_space=pltpu.HBM)
CONTRACT_ROWS = (((0,), (0,)), ((), ()))


def params(mebibytes):
    return pltpu.CompilerParams(vmem_limit_bytes=mebibytes << 20)


def one_hot(condition):
    return jnp.where(condition, 1.0, 0.0).astype(BF16)


def side_by_side(field_ref):
    return jnp.concatenate([field_ref[l] for l in range(field_ref.shape[0])], axis=1)


def outgoing_kernel(
    send_hbm, field_hbm, length_hbm, wave_hbm, donor_hbm, tile_hbm, kernels_hbm,
    far_ref, near_ref, field_ref, lengths_ref, wave_ref, donor_ref, tile_ref, kernels_ref,
    send_ref, length_ref, sems,
):
    pairs = (
        (send_hbm, send_ref), (field_hbm, field_ref), (length_hbm, length_ref), (wave_hbm, wave_ref),
        (donor_hbm, donor_ref), (tile_hbm, tile_ref), (kernels_hbm, kernels_ref),
    )
    copies = [pltpu.make_async_copy(*pair, sems.at[i]) for i, pair in enumerate(pairs)]
    for copy in copies:
        copy.start()
    copies[0].wait()
    copies[1].wait()
    band = lax.axis_index("lat")
    even = lax.rem(band, 2) == 0
    own = side_by_side(field_ref)
    blocks, count = own.shape[0], send_ref.shape[2]
    rows = lax.broadcasted_iota(jnp.int32, (blocks, count), 0)
    below, above = send_ref[0, 0:1, :], send_ref[0, 1:2, :]
    for ref, listed in (
        (far_ref, jnp.where(even, below, above)),
        (near_ref, jnp.where(even, above, below)),
    ):
        picked = lax.dot_general(
            one_hot(rows == listed), own, CONTRACT_ROWS, preferred_element_type=F32
        )
        ref[...] = picked.astype(BF16)
    copies[2].wait()
    circles = lengths_ref.shape[0] // 2
    for i in range(2 * circles):
        length = length_ref[band * circles + i % circles]
        lengths_ref[i : i + 1] = jnp.full((1, LANES), length, jnp.int32)
    for copy in copies[3:]:
        copy.wait()


SINE = (0.07761395, -0.59827207, 2.55007494, -5.16770998, 3.14159264)
COSINE = (0.21953804, -1.33180992, 4.05840238, -4.93479245, 0.99999995)
ROUND = 1.5 * 2.0**23


def turn(steps, waves, length, inverse):
    phase = steps * waves
    rest = phase - ((phase * inverse + ROUND) - ROUND) * length
    f = rest * inverse
    x = f * f
    s, c = SINE[0], COSINE[0]
    for p, q in zip(SINE[1:], COSINE[1:]):
        s, c = s * x + p, c * x + q
    s = s * f
    twice = s + s
    return 1.0 - twice * s, twice * c


def log(n):
    return n.bit_length() - 1


def times(a, b):
    return a[0] * b[0] - a[1] * b[1], a[0] * b[1] + a[1] * b[0]


def folded_order(array, coarse):
    half, count = coarse // 2, coarse // 8
    assert coarse % 8 == 0 and half % 8 == 4
    sub = lax.broadcasted_iota(jnp.int32, (8, array.shape[1]), 0)

    def reverse(v):
        v = pltpu.roll(v, 4, 0)
        for h in (2, 1):
            v = jnp.where((sub & h) == 0, pltpu.roll(v, 8 - h, 0), pltpu.roll(v, h, 0))
        return v

    out = []
    for begin in range(0, array.shape[0], coarse):
        rows = [array[begin + 8 * i : begin + 8 * i + 8] for i in range(count)]
        swapped = {i: pltpu.roll(rows[i], 4, 0) for i in range(half // 8, count)}
        for i in range(count):
            q = (8 * i + half) // 8
            if 8 * i + 8 <= half:
                out.append(jnp.where(sub < 4, swapped[q], swapped[q + 1]))
            elif 8 * i < half:
                out.append(jnp.where(sub < 4, swapped[q], reverse(rows[count - 1 - i])))
            else:
                out.append(reverse(rows[count - 1 - i]))
    return jnp.concatenate(out, axis=0)


def table_kernel(
    lengths_ref, wave_ref, field_ref, donor_ref, tile_ref, kernels_ref, slot_hbm,
    fine_ref, coarse_ref, limits_ref, far_choice_ref, near_choice_ref, arrival_ref, order_ref,
    slot_ref, sem, *, lat, lev,
):
    circles, tiles = fine_ref.shape[:2]
    levels, blocks, _ = field_ref.shape
    coarse = blocks // circles
    half = coarse // 2
    fetch = pltpu.make_async_copy(slot_hbm, slot_ref, sem)
    fetch.start()
    row = lax.broadcasted_iota(jnp.int32, (8, LANES), 0)
    near_step = (row + LANES // 2 * (coarse - 1)).astype(F32)
    far_step = (row * LANES + LANES // 2).astype(F32)
    hop_step = jnp.left_shift(8, jnp.where(row < 4, row, row - 4 + log(LANES))).astype(F32)

    def doubled(base, hops, groups):
        out = [base]
        while len(out) < groups:
            k = log(len(out))
            hop = tuple(jnp.broadcast_to(x[k : k + 1], (8, LANES)) for x in hops)
            out += [times(e, hop) for e in out[: groups - len(out)]]
        return [jnp.concatenate(part, axis=0) for part in zip(*out)]

    def circle(g):
        length = jnp.broadcast_to(lengths_ref[pl.ds(g, 1)], (8, LANES)).astype(F32)
        return length, 1.0 / length

    def table(g, t, length, inverse):
        waves = jnp.broadcast_to(wave_ref[pl.ds(t, 1), :], (8, LANES)).astype(F32)
        hops = turn(hop_step, waves, length, inverse)
        fine = doubled(turn(near_step, waves, length, inverse), hops, LANES // 8)
        fine_ref[g, t] = jnp.concatenate(fine, axis=1).astype(BF16)
        wide = doubled(
            turn(far_step, waves, length, inverse), tuple(x[4:] for x in hops), -(-half // 8)
        )
        coarse_ref[g, t] = jnp.concatenate(
            [jnp.concatenate([part[:half]] * levels, axis=0) for part in wide], axis=1
        )

    def looped(index, _):
        table(index // tiles, lax.rem(index, tiles), *circle(index // tiles))
        return 0

    listed = jnp.concatenate(
        [donor_ref[...], tile_ref[...], jnp.zeros((4, blocks), jnp.int32)], axis=0
    )
    columns = folded_order(jnp.transpose(listed.astype(F32)), coarse)
    own = side_by_side(field_ref)
    kinds = kernels_ref.shape[0]
    count = far_choice_ref.shape[1] // kinds
    even = lax.rem(lax.axis_index("lat"), 2) == 0
    lane = lax.broadcasted_iota(jnp.int32, (blocks, blocks), 1).astype(F32)
    entry = lax.broadcasted_iota(jnp.int32, far_choice_ref.shape, 1).astype(F32)
    far_choice, near_choice, picked, kind = [], [], [], []
    for k in range(2):
        donor = columns[:, k : k + 1]
        tile = columns[:, 2 + k : 3 + k]
        place = donor - float(blocks)
        above = place >= float(count)
        code = jnp.where(above, place - float(count), place) + float(count) * tile
        code = jnp.where(place >= 0.0, code, -1.0)
        is_far = jnp.logical_xor(above, even)
        far_choice.append(jnp.where(entry == jnp.where(is_far, code, -1.0), 1.0, 0.0))
        near_choice.append(jnp.where(entry == jnp.where(is_far, -1.0, code), 1.0, 0.0))
        picked.append(
            jnp.dot(one_hot(lane == donor), own, preferred_element_type=F32).astype(BF16)
        )
        kind.append(jnp.broadcast_to(tile, (blocks, LANES)))
    far_choice_ref[...] = (far_choice[0] + far_choice[1]).astype(BF16)
    near_choice_ref[...] = (near_choice[0] + near_choice[1]).astype(BF16)
    stacked = jnp.concatenate([kernels_ref[k] for k in range(kinds)], axis=1)
    for l in range(levels):
        total = None
        for k in range(2):
            every = jnp.dot(
                picked[k][:, l * LANES : (l + 1) * LANES], stacked, preferred_element_type=F32
            )
            value = every[:, :LANES]
            for q in range(1, kinds):
                value = jnp.where(kind[k] == float(q), every[:, q * LANES : (q + 1) * LANES], value)
            total = value if k == 0 else total + value
        arrival_ref[:, l * LANES : (l + 1) * LANES] = total

    unrolled = circles * tiles <= 64
    if unrolled:
        for g in range(circles):
            for t in range(tiles):
                table(g, t, *circle(g))
    else:
        lax.fori_loop(0, circles * tiles, looped, 0, unroll=2)

    fetch.wait()
    slots = limits_ref.shape[0]
    first = (lax.axis_index("lat") * lev + lax.axis_index("lev")) * slots
    for s in range(slots):
        limits_ref[s : s + 1] = jnp.full((1, LANES), slot_ref[first + s], jnp.int32)

    total = order_ref.shape[0]
    if total == lat * lev * 2 * circles:
        at = lax.broadcasted_iota(jnp.int32, (8, total), 1)
        outer = (at >> log(circles)) & (lat - 1)
        group = at >> log(lat * circles)
        source = (outer << log(circles * 2 * lev)) | (group << log(circles)) | (at & (circles - 1))
        row = lax.broadcasted_iota(jnp.int32, (total, total), 0)
        order_ref[...] = one_hot(row == source[0:1])
    else:
        order_ref[...] = jnp.zeros(order_ref.shape, BF16)


def fold(parts):
    row = lax.broadcasted_iota(jnp.int32, (8, LANES), 0)
    for half in (4, 2, 1):
        low = (row & half) == 0
        count = len(parts) // 2
        parts = [
            jnp.where(low, a, pltpu.roll(b, half, 0)) + jnp.where(low, pltpu.roll(a, 8 - half, 0), b)
            for a, b in zip(parts[:count], parts[count:])
        ]
    return parts[0]


def from_halo(halo, kernels_ref, choice):
    kinds = kernels_ref.shape[0]
    count, levels = halo.shape[0], halo.shape[1] // LANES
    stacked = jnp.concatenate([kernels_ref[k] for k in range(kinds)], axis=1)
    rows = jnp.concatenate(
        [halo[:, l * LANES : (l + 1) * LANES] for l in range(levels)], axis=0
    )
    every = jnp.dot(rows, stacked, preferred_element_type=F32)
    every = jnp.concatenate(
        [
            jnp.concatenate(
                [every[l * count : (l + 1) * count, q * LANES : (q + 1) * LANES] for q in range(kinds)],
                axis=0,
            )
            for l in range(levels)
        ],
        axis=1,
    )
    high = every.astype(BF16)
    low = (every - high.astype(F32)).astype(BF16)
    return jnp.dot(choice, high, preferred_element_type=F32) + jnp.dot(
        choice, low, preferred_element_type=F32
    )


def far_kernel(far_ref, choice_ref, kernels_ref, own_ref, arrival_ref):
    band = lax.axis_index("lat")
    at_end = (band == 0) | (band == lax.axis_size("lat") - 1)
    far = far_ref[...]
    far = jnp.where(at_end, jnp.zeros_like(far), far)
    arrival_ref[...] = own_ref[...] + from_halo(far, kernels_ref, choice_ref[...])


def transform_kernel(
    lengths_ref, wave_ref, near_ref, choice_ref, arrival_ref, kernels_ref, fine_ref,
    coarse_ref, out_ref, points_ref, coeff_ref, *, top_wave,
):
    blocks = arrival_ref.shape[0]
    levels = arrival_ref.shape[1] // LANES
    circles, tiles = fine_ref.shape[:2]
    coarse = blocks // circles
    half = coarse // 2
    arrival = arrival_ref[...] + from_halo(near_ref[...], kernels_ref, choice_ref[...])

    distance = lax.broadcasted_iota(jnp.int32, (coarse, LANES), 0)
    row = jnp.where(distance < half, distance + half, coarse - 1 - distance)
    position = row * LANES + lax.broadcasted_iota(jnp.int32, (coarse, LANES), 1)
    for g in range(circles):
        inside = position < jnp.broadcast_to(lengths_ref[g : g + 1], (coarse, LANES))
        sums, differences = [], []
        for l in range(levels):
            rows = slice(g * coarse, (g + 1) * coarse)
            part = arrival[rows, l * LANES : (l + 1) * LANES]
            part = jnp.where(inside, part * part, 0.0)
            sums.append(part[:half] + part[half:])
            differences.append(part[:half] - part[half:])
        points_ref[g] = jnp.concatenate(sums + differences, axis=0).astype(BF16)

    height = 2 * circles
    lengths = lengths_ref[...]
    sine = lax.broadcasted_iota(jnp.int32, (height, LANES), 0) >= circles
    sub = lax.broadcasted_iota(jnp.int32, (8, LANES), 0)

    def level_sum(value, l):
        first, last = l * half, (l + 1) * half
        total = None
        for at in range(first // 8 * 8, last, 8):
            piece = value[at : at + 8]
            if at < first:
                piece = jnp.where(sub >= first - at, piece, 0.0)
            if at + 8 > last:
                piece = jnp.where(sub < last - at, piece, 0.0)
            total = piece if total is None else total + piece
        return total

    def tile(t):
        sums = [([], []) for _ in range(levels)]
        for g in range(circles):
            turned = jnp.dot(points_ref[g], fine_ref[g, t], preferred_element_type=F32)
            both, apart = turned[: levels * half], turned[levels * half :]
            c, s = coarse_ref[g, t, :, :LANES], coarse_ref[g, t, :, LANES:]
            real = both[:, :LANES] * c - apart[:, LANES:] * s
            imag = both[:, LANES:] * c + apart[:, :LANES] * s
            for l in range(levels):
                sums[l][0].append(level_sum(real, l))
                sums[l][1].append(level_sum(imag, l))
        waves = jnp.broadcast_to(wave_ref[pl.ds(t, 1), :], (height, LANES))
        live = (waves >= 1) & (waves < top_wave) & (2 * waves < lengths)
        found = []
        for l in range(levels):
            ordered = sums[l][0] + sums[l][1]
            rows = [fold(ordered[i : i + 8]) for i in range(0, height, 8)]
            rows = jnp.concatenate(rows, axis=0)
            found.append(jnp.where(live, jnp.where(sine, -rows, rows), 0.0))
        return jnp.concatenate(found, axis=0)

    def stored(t, _):
        coeff_ref[t] = tile(t)
        return 0

    devices, chunk_rows, _ = out_ref.shape
    width = tiles * LANES // devices
    packs = coeff_ref.shape[1] // chunk_rows
    step = LANES // packs
    lane = lax.broadcasted_iota(jnp.int32, (chunk_rows, LANES), 1)
    if circles * tiles <= 64:
        coeffs = [tile(t) for t in range(tiles)]
    else:
        lax.fori_loop(0, tiles, stored, 0)
        coeffs = [coeff_ref.at[t] for t in range(tiles)]
    for d in range(devices):
        t, shift = divmod(d * width, LANES)
        chunk = jnp.zeros((chunk_rows, LANES), F32)
        for p in range(packs):
            rows = slice(p * chunk_rows, (p + 1) * chunk_rows)
            at = p * step
            value = pltpu.roll(coeffs[t][rows], (at - shift) % LANES, 1)
            if shift + width > LANES:
                after = pltpu.roll(coeffs[t + 1][rows], (at - shift) % LANES, 1)
                value = jnp.where(lane < at + LANES - shift, value, after)
            chunk = value if p == 0 else jnp.where(lane < at, chunk, value)
        out_ref[d] = chunk.astype(BF16)


def legendre_kernel(limits_ref, arrived_ref, order_ref, legendre_ref, out_hbm, out_ref, sems, *, packs):
    outputs, slots, top_wave = out_ref.shape
    circles = legendre_ref.shape[0] // slots
    per_tile = LANES // circles
    total = arrived_ref.shape[0]
    turned = lax.dot_general(
        arrived_ref[...], order_ref[...], CONTRACT_ROWS, preferred_element_type=F32
    )

    sub = lax.broadcasted_iota(jnp.int32, (8, LANES), 0)
    block = lax.broadcasted_iota(jnp.int32, (8, LANES), 1) >> log(circles)
    chosen = [(block == b) & ((sub & (per_tile - 1)) == b) for b in range(per_tile)]
    halves = 8 // per_tile
    in_half = [(sub >> log(per_tile)) == h for h in range(halves)]
    step = LANES // packs
    spread = []
    for k in range(slots // 8):
        pieces = [None] * outputs
        for l in range(packs):
            for j in range(total // LANES):
                at = l * step + 8 * k
                v = turned[at : at + 8, j * LANES : (j + 1) * LANES]
                rolled = [v] + [pltpu.roll(v, circles * d, 1) for d in range(1, per_tile)]
                for i in range(per_tile):
                    a = jnp.zeros((8, LANES), F32)
                    for b in range(per_tile):
                        a = jnp.where(chosen[b], rolled[(b - i) % per_tile], a)
                    group_lev, part = divmod(j * per_tile + i, 2)
                    pieces[(group_lev * packs + l) * 2 + part] = jnp.concatenate(
                        [jnp.where(in_half[h], a, 0.0) for h in range(halves)], axis=1
                    )
        spread.append(jnp.concatenate(pieces, axis=0).astype(BF16))

    wide = 2 * LANES
    lane = lax.broadcasted_iota(jnp.int32, (8, wide), 1)
    limits = [limits_ref[8 * k : 8 * k + 8] for k in range(slots // 8)]
    limits = [jnp.concatenate([m, m], axis=1) for m in limits]
    copies = []
    for n in range(0, top_wave, wide):
        sums = [
            jnp.dot(
                spread[k],
                legendre_ref[8 * k * circles : 8 * (k + 1) * circles, n : n + wide],
                preferred_element_type=F32,
            )
            for k in range(slots // 8)
        ]
        keep = [lane + n >= m for m in limits]
        for o in range(outputs):
            out_ref[o, :, n : n + wide] = jnp.concatenate(
                [jnp.where(keep[k], sums[k][8 * o : 8 * o + 8], 0.0) for k in range(slots // 8)],
                axis=0,
            ).astype(BF16)
        columns = (slice(None), slice(None), pl.ds(n, wide))
        copies.append(
            pltpu.make_async_copy(
                out_ref.at[columns], out_hbm.at[columns], sems.at[n // wide]
            )
        )
        copies[-1].start()
    for copy in copies:
        copy.wait()


def other_neighbours(lat, lev):
    inner = [(i, i + 1) for i in range(1, lat - 1, 2)]
    inner += [(j, i) for i, j in inner]
    pairs = [(i * lev + l, j * lev + l) for i, j in inner for l in range(lev)]
    return pairs + [(i * lev + l, i * lev + (l ^ 1)) for i in (0, lat - 1) for l in range(lev)]


def body(
    grid_field, send_blocks, donor_index, tile_choice, kernel_tiles, circle_len, slot_wave, legendre
):
    levels, blocks, _ = grid_field.shape
    send_count = send_blocks.shape[2]
    slots, circles, top_wave = legendre.shape
    lat, lev = lax.axis_size("lat"), lax.axis_size("lev")
    devices = lat * lev
    coarse = PTS // LANES
    own = blocks // coarse
    tiles = slot_wave.shape[0] // LANES
    waves = slot_wave.reshape(tiles, LANES)

    def like(x):
        return jax.ShapeDtypeStruct(x.shape, x.dtype)

    def in_hbm(x):
        return pltpu.with_memory_space_constraint(x, pltpu.HBM)

    halo = jax.ShapeDtypeStruct((send_count, levels * LANES), BF16)
    donors, kinds = donor_index.T, tile_choice.T
    to_far, to_near, field, lengths, waves, donors, kinds, kernels = pl.pallas_call(
        outgoing_kernel,
        out_shape=(
            halo, halo, like(grid_field), jax.ShapeDtypeStruct((2 * own, LANES), jnp.int32),
            like(waves), like(donors), like(kinds), like(kernel_tiles),
        ),
        in_specs=[HBM] * 7, out_specs=(VMEM,) * 8,
        scratch_shapes=[
            pltpu.VMEM(send_blocks.shape, jnp.int32),
            pltpu.SMEM(circle_len.shape, jnp.int32),
            pltpu.SemaphoreType.DMA((7,)),
        ],
        compiler_params=params(4), name="outgoing",
    )(
        *map(in_hbm, (send_blocks, grid_field, circle_len, waves, donors, kinds, kernel_tiles))
    )
    near = lax.ppermute(to_near, "lat", [(i, i ^ 1) for i in range(lat)])
    far = lax.ppermute(to_far, ("lat", "lev"), other_neighbours(lat, lev))

    direct = levels == 2 and 2 * own == 8 and 4 * circles == LANES and slots % 8 == 0
    direct = direct and 2 * slots <= LANES and lev & (lev - 1) == 0
    total = devices * 2 * own if direct else 16
    entries = own * tiles * (LANES + coarse) * 2 * LANES
    choice = jax.ShapeDtypeStruct((blocks, kernel_tiles.shape[0] * send_count), BF16)
    arrival = jax.ShapeDtypeStruct((blocks, levels * LANES), F32)
    fine, wide, limits, far_choice, near_choice, own_part, order = pl.pallas_call(
        functools.partial(table_kernel, lat=lat, lev=lev),
        out_shape=(
            jax.ShapeDtypeStruct((own, tiles, LANES, 2 * LANES), BF16),
            jax.ShapeDtypeStruct((own, tiles, levels * coarse // 2, 2 * LANES), F32),
            jax.ShapeDtypeStruct((slots, LANES), jnp.int32),
            choice,
            choice,
            arrival,
            jax.ShapeDtypeStruct((total, total), BF16),
        ),
        in_specs=[VMEM] * 6 + [HBM], out_specs=(VMEM,) * 7,
        scratch_shapes=[
            pltpu.SMEM(slot_wave.shape, jnp.int32),
            pltpu.SemaphoreType.DMA,
        ],
        compiler_params=params(32), name="tables",
        cost_estimate=pl.CostEstimate(flops=8 * entries, bytes_accessed=3 * entries, transcendentals=0),
    )(lengths, waves, field, donors, kinds, kernels, in_hbm(slot_wave))

    rows = levels * 2 * own
    packs = 1
    while rows % (16 * packs) == 0 and 2 * packs * slots <= LANES:
        packs *= 2
    arrival = pl.pallas_call(
        far_kernel, out_shape=arrival, in_specs=[VMEM] * 4, out_specs=VMEM,
        compiler_params=params(8), name="far_part",
    )(far, far_choice, kernels, own_part)
    coeffs = pl.pallas_call(
        functools.partial(transform_kernel, top_wave=top_wave),
        out_shape=jax.ShapeDtypeStruct((devices, rows // packs, LANES), BF16),
        in_specs=[VMEM] * 8, out_specs=VMEM,
        scratch_shapes=[
            pltpu.VMEM((own, levels * coarse, LANES), BF16),
            pltpu.VMEM((tiles, rows, LANES), F32),
        ],
        compiler_params=params(40), name="transform",
    )(lengths, waves, near, near_choice, arrival, kernels, fine, wide)
    arrived = lax.all_to_all(coeffs, ("lat", "lev"), 0, 0, tiled=True)

    outputs = lev * levels * 2
    height = rows // packs
    if direct:
        spectra = pl.pallas_call(
            functools.partial(legendre_kernel, packs=packs),
            out_shape=jax.ShapeDtypeStruct((outputs, slots, top_wave), BF16),
            in_specs=[VMEM] * 4, out_specs=HBM,
            scratch_shapes=[
                pltpu.VMEM((outputs, slots, top_wave), BF16),
                pltpu.SemaphoreType.DMA((top_wave // (2 * LANES),)),
            ],
            compiler_params=params(32), name="legendre",
        )(
            limits,
            arrived.reshape(devices * height, LANES),
            order,
            legendre.reshape(slots * circles, top_wave),
        )
        return spectra.reshape(outputs // 2, 2, slots, top_wave)

    gathered = arrived.reshape(lat, lev, height, packs, LANES // packs)[..., :slots]
    gathered = gathered.swapaxes(2, 3).reshape(lat, lev, levels, 2, own, slots)
    gathered = gathered.transpose(1, 2, 3, 0, 4, 5).reshape(outputs // 2, 2, circles, slots)
    spectra = jnp.einsum("lcgs,sgn->lcsn", gathered, legendre, preferred_element_type=F32)
    first_slot = (lax.axis_index("lat") * lev + lax.axis_index("lev")) * slots
    mine = lax.dynamic_slice_in_dim(slot_wave, first_slot, slots)
    allowed = jnp.arange(top_wave, dtype=jnp.int32)[None, :] >= mine[:, None]
    return jnp.where(allowed[None, None], spectra, 0.0).astype(BF16)


def solution(mesh):
    return jax.shard_map(
        body,
        mesh=mesh,
        in_specs=(
            P("lev", "lat", None),
            P("lat", None, None),
            P("lat", None),
            P("lat", None),
            P(),
            P(),
            P(),
            P(("lat", "lev"), None, None),
        ),
        out_specs=P(None, None, ("lat", "lev"), None),
        check_vma=False,
    )
```

```python
import functools
import math

import jax
import jax.numpy as jnp
from jax import lax
from jax.experimental import pallas as pl
from jax.experimental.pallas import tpu as pltpu
from jax.sharding import PartitionSpec as P

PTS = 5120
LANES = 128
BF16 = jnp.bfloat16
F32 = jnp.float32
VMEM = pl.BlockSpec(memory_space=pltpu.VMEM)
HBM = pl.BlockSpec(memory_space=pltpu.HBM)
CONTRACT_ROWS = (((0,), (0,)), ((), ()))


def params(mebibytes):
    return pltpu.CompilerParams(vmem_limit_bytes=mebibytes << 20)


def one_hot(condition):
    return jnp.where(condition, 1.0, 0.0).astype(BF16)


def side_by_side(field_ref):
    return jnp.concatenate([field_ref[l] for l in range(field_ref.shape[0])], axis=1)


def outgoing_kernel(
    send_hbm, field_hbm, length_hbm, wave_hbm, donor_hbm, tile_hbm, kernels_hbm,
    far_ref, near_ref, field_ref, lengths_ref, wave_ref, donor_ref, tile_ref, kernels_ref,
    send_ref, length_ref, sems,
):
    pairs = (
        (send_hbm, send_ref), (field_hbm, field_ref), (length_hbm, length_ref), (wave_hbm, wave_ref),
        (donor_hbm, donor_ref), (tile_hbm, tile_ref), (kernels_hbm, kernels_ref),
    )
    copies = [pltpu.make_async_copy(*pair, sems.at[i]) for i, pair in enumerate(pairs)]
    for copy in copies:
        copy.start()
    band = lax.axis_index("lat")
    even = lax.rem(band, 2) == 0
    blocks, count = field_ref.shape[1], send_ref.shape[2]
    rows = lax.broadcasted_iota(jnp.int32, (blocks, count), 0)
    copies[0].wait()
    below, above = send_ref[0, 0:1, :], send_ref[0, 1:2, :]
    far_hot = jnp.transpose(jnp.where(rows == jnp.where(even, below, above), 1.0, 0.0)).astype(BF16)
    near_hot = jnp.transpose(jnp.where(rows == jnp.where(even, above, below), 1.0, 0.0)).astype(BF16)
    copies[1].wait()
    own = side_by_side(field_ref)
    for ref, hot in ((far_ref, far_hot), (near_ref, near_hot)):
        picked = jnp.dot(hot, own, preferred_element_type=F32)
        ref[...] = picked.astype(BF16)
    copies[2].wait()
    circles = lengths_ref.shape[0] // 2
    for i in range(2 * circles):
        length = length_ref[band * circles + i % circles]
        lengths_ref[i : i + 1] = jnp.full((1, LANES), length, jnp.int32)
    for copy in copies[3:]:
        copy.wait()


SINE = (0.07761395, -0.59827207, 2.55007494, -5.16770998, 3.14159264)
COSINE = (0.21953804, -1.33180992, 4.05840238, -4.93479245, 0.99999995)
ROUND = 1.5 * 2.0**23


def turn(steps, waves, length, inverse):
    phase = steps * waves
    rest = phase - ((phase * inverse + ROUND) - ROUND) * length
    f = rest * inverse
    x = f * f
    s, c = SINE[0], COSINE[0]
    for p, q in zip(SINE[1:], COSINE[1:]):
        s, c = s * x + p, c * x + q
    s = s * f
    twice = s + s
    return 1.0 - twice * s, twice * c


def log(n):
    return n.bit_length() - 1


def times(a, b):
    return a[0] * b[0] - a[1] * b[1], a[0] * b[1] + a[1] * b[0]


def folded_order(array, coarse):
    half, count = coarse // 2, coarse // 8
    assert coarse % 8 == 0 and half % 8 == 4
    sub = lax.broadcasted_iota(jnp.int32, (8, array.shape[1]), 0)

    def reverse(v):
        v = pltpu.roll(v, 4, 0)
        for h in (2, 1):
            v = jnp.where((sub & h) == 0, pltpu.roll(v, 8 - h, 0), pltpu.roll(v, h, 0))
        return v

    out = []
    for begin in range(0, array.shape[0], coarse):
        rows = [array[begin + 8 * i : begin + 8 * i + 8] for i in range(count)]
        swapped = {i: pltpu.roll(rows[i], 4, 0) for i in range(half // 8, count)}
        for i in range(count):
            q = (8 * i + half) // 8
            if 8 * i + 8 <= half:
                out.append(jnp.where(sub < 4, swapped[q], swapped[q + 1]))
            elif 8 * i < half:
                out.append(jnp.where(sub < 4, swapped[q], reverse(rows[count - 1 - i])))
            else:
                out.append(reverse(rows[count - 1 - i]))
    return jnp.concatenate(out, axis=0)


def table_kernel(
    lengths_ref, wave_ref, field_ref, donor_ref, tile_ref, kernels_ref, slot_hbm,
    fine_ref, coarse_ref, limits_ref, far_choice_ref, near_choice_ref, arrival_ref, order_ref,
    slot_ref, sem, *, lat, lev,
):
    circles, tiles = fine_ref.shape[:2]
    levels, blocks, _ = field_ref.shape
    coarse = blocks // circles
    half = coarse // 2
    fetch = pltpu.make_async_copy(slot_hbm, slot_ref, sem)
    fetch.start()
    row = lax.broadcasted_iota(jnp.int32, (8, LANES), 0)
    near_step = (row + LANES // 2 * (coarse - 1)).astype(F32)
    far_step = (row * LANES + LANES // 2).astype(F32)
    hop_step = jnp.where((row & 1) == 0, 8, 8 * LANES).astype(F32)
    group = 4 if circles % 4 == 0 else 1

    def stepped(base, hop, groups):
        out = [base, times(base, hop)]
        twice = hop[0] + hop[0]
        while len(out) < groups:
            out.append(tuple(twice * x - y for x, y in zip(out[-1], out[-2])))
        return [jnp.concatenate(part, axis=0) for part in zip(*out[:groups])]

    def lengths_of(first):
        each = [
            jnp.broadcast_to(lengths_ref[pl.ds(first + i, 1)], (8, LANES)) for i in range(group)
        ]
        mixed = each[0]
        for i in range(1, group):
            mixed = jnp.where(row >= 2 * i, each[i], mixed)
        return [(x.astype(F32), 1.0 / x.astype(F32)) for x in (*each, mixed)]

    def table(first, t, scales):
        waves = jnp.broadcast_to(wave_ref[pl.ds(t, 1), :], (8, LANES)).astype(F32)
        hops = turn(hop_step, waves, *scales[group])
        for i in range(group):
            near_hop, far_hop = (
                tuple(jnp.broadcast_to(x[k : k + 1], (8, LANES)) for x in hops)
                for k in (2 * i, 2 * i + 1)
            )
            fine = stepped(turn(near_step, waves, *scales[i]), near_hop, LANES // 8)
            fine_ref[first + i, t] = jnp.concatenate(fine, axis=1).astype(BF16)
            wide = stepped(turn(far_step, waves, *scales[i]), far_hop, -(-half // 8))
            coarse_ref[first + i, t] = jnp.concatenate(
                [jnp.concatenate([part[:half]] * levels, axis=0) for part in wide], axis=1
            )

    def looped(index, _):
        first = index // tiles * group
        table(first, lax.rem(index, tiles), lengths_of(first))
        return 0

    listed = jnp.concatenate(
        [donor_ref[...], tile_ref[...], jnp.zeros((4, blocks), jnp.int32)], axis=0
    )
    columns = folded_order(jnp.transpose(listed.astype(F32)), coarse)
    own = side_by_side(field_ref)
    kinds = kernels_ref.shape[0]
    count = far_choice_ref.shape[1] // kinds
    even = lax.rem(lax.axis_index("lat"), 2) == 0
    lane = lax.broadcasted_iota(jnp.int32, (blocks, blocks), 1).astype(F32)
    entry = lax.broadcasted_iota(jnp.int32, far_choice_ref.shape, 1).astype(F32)
    far_choice, near_choice, picked, kind = [], [], [], []
    for k in range(2):
        donor = columns[:, k : k + 1]
        tile = columns[:, 2 + k : 3 + k]
        place = donor - float(blocks)
        above = place >= float(count)
        code = jnp.where(above, place - float(count), place) + float(count) * tile
        code = jnp.where(place >= 0.0, code, -1.0)
        is_far = jnp.logical_xor(above, even)
        far_choice.append(jnp.where(entry == jnp.where(is_far, code, -1.0), 1.0, 0.0))
        near_choice.append(jnp.where(entry == jnp.where(is_far, -1.0, code), 1.0, 0.0))
        picked.append(
            jnp.dot(one_hot(lane == donor), own, preferred_element_type=F32).astype(BF16)
        )
        kind.append(jnp.broadcast_to(tile, (blocks, LANES)))
    far_choice_ref[...] = (far_choice[0] + far_choice[1]).astype(BF16)
    near_choice_ref[...] = (near_choice[0] + near_choice[1]).astype(BF16)
    stacked = jnp.concatenate([kernels_ref[k] for k in range(kinds)], axis=1)
    for l in range(levels):
        total = None
        for k in range(2):
            every = jnp.dot(
                picked[k][:, l * LANES : (l + 1) * LANES], stacked, preferred_element_type=F32
            )
            value = every[:, :LANES]
            for q in range(1, kinds):
                value = jnp.where(kind[k] == float(q), every[:, q * LANES : (q + 1) * LANES], value)
            total = value if k == 0 else total + value
        arrival_ref[:, l * LANES : (l + 1) * LANES] = total

    if circles * tiles <= 64:
        for first in range(0, circles, group):
            scales = lengths_of(first)
            for t in range(tiles):
                table(first, t, scales)
    else:
        lax.fori_loop(0, circles // group * tiles, looped, 0)

    fetch.wait()
    slots = limits_ref.shape[0]
    first = (lax.axis_index("lat") * lev + lax.axis_index("lev")) * slots
    for s in range(slots):
        limits_ref[s : s + 1] = jnp.full((1, LANES), slot_ref[first + s], jnp.int32)

    total = order_ref.shape[0]
    if total == lat * lev * 2 * circles:
        at = lax.broadcasted_iota(jnp.int32, (8, total), 1)
        outer = (at >> log(circles)) & (lat - 1)
        group = at >> log(lat * circles)
        source = (outer << log(circles * 2 * lev)) | (group << log(circles)) | (at & (circles - 1))
        row = lax.broadcasted_iota(jnp.int32, (total, total), 0)
        order_ref[...] = one_hot(row == source[0:1])
    else:
        order_ref[...] = jnp.zeros(order_ref.shape, BF16)


def fold(parts):
    row = lax.broadcasted_iota(jnp.int32, (8, LANES), 0)
    for half in (4, 2, 1):
        low = (row & half) == 0
        count = len(parts) // 2
        parts = [
            jnp.where(low, a, pltpu.roll(b, half, 0)) + jnp.where(low, pltpu.roll(a, 8 - half, 0), b)
            for a, b in zip(parts[:count], parts[count:])
        ]
    return parts[0]


def from_halo(halo, kernels_ref, choice):
    kinds = kernels_ref.shape[0]
    count, levels = halo.shape[0], halo.shape[1] // LANES
    stacked = jnp.concatenate([kernels_ref[k] for k in range(kinds)], axis=1)
    rows = jnp.concatenate(
        [halo[:, l * LANES : (l + 1) * LANES] for l in range(levels)], axis=0
    )
    every = jnp.dot(rows, stacked, preferred_element_type=F32)
    every = jnp.concatenate(
        [
            jnp.concatenate(
                [every[l * count : (l + 1) * count, q * LANES : (q + 1) * LANES] for q in range(kinds)],
                axis=0,
            )
            for l in range(levels)
        ],
        axis=1,
    )
    high = every.astype(BF16)
    low = (every - high.astype(F32)).astype(BF16)
    return jnp.dot(choice, high, preferred_element_type=F32) + jnp.dot(
        choice, low, preferred_element_type=F32
    )


def far_kernel(far_ref, choice_ref, kernels_ref, own_ref, arrival_ref):
    band = lax.axis_index("lat")
    at_end = (band == 0) | (band == lax.axis_size("lat") - 1)
    far = far_ref[...]
    far = jnp.where(at_end, jnp.zeros_like(far), far)
    arrival_ref[...] = own_ref[...] + from_halo(far, kernels_ref, choice_ref[...])


def transform_kernel(
    lengths_ref, wave_ref, near_ref, choice_ref, arrival_ref, kernels_ref, fine_ref,
    coarse_ref, out_ref, points_ref, coeff_ref, *, top_wave,
):
    blocks = arrival_ref.shape[0]
    levels = arrival_ref.shape[1] // LANES
    circles, tiles = fine_ref.shape[:2]
    coarse = blocks // circles
    half = coarse // 2
    arrival = arrival_ref[...] + from_halo(near_ref[...], kernels_ref, choice_ref[...])

    distance = lax.broadcasted_iota(jnp.int32, (coarse, LANES), 0)
    row = jnp.where(distance < half, distance + half, coarse - 1 - distance)
    position = row * LANES + lax.broadcasted_iota(jnp.int32, (coarse, LANES), 1)
    for g in range(circles):
        inside = position < jnp.broadcast_to(lengths_ref[g : g + 1], (coarse, LANES))
        sums, differences = [], []
        for l in range(levels):
            rows = slice(g * coarse, (g + 1) * coarse)
            part = arrival[rows, l * LANES : (l + 1) * LANES]
            part = jnp.where(inside, part * part, 0.0)
            sums.append(part[:half] + part[half:])
            differences.append(part[:half] - part[half:])
        points_ref[g] = jnp.concatenate(sums + differences, axis=0).astype(BF16)

    height = 2 * circles
    lengths = lengths_ref[...]
    sine = lax.broadcasted_iota(jnp.int32, (height, LANES), 0) >= circles
    sub = lax.broadcasted_iota(jnp.int32, (8, LANES), 0)

    def level_sum(value, l):
        first, last = l * half, (l + 1) * half
        total = None
        for at in range(first // 8 * 8, last, 8):
            piece = value[at : at + 8]
            if at < first:
                piece = jnp.where(sub >= first - at, piece, 0.0)
            if at + 8 > last:
                piece = jnp.where(sub < last - at, piece, 0.0)
            total = piece if total is None else total + piece
        return total

    def tile(t):
        sums = [([], []) for _ in range(levels)]
        for g in range(circles):
            turned = jnp.dot(points_ref[g], fine_ref[g, t], preferred_element_type=F32)
            both, apart = turned[: levels * half], turned[levels * half :]
            c, s = coarse_ref[g, t, :, :LANES], coarse_ref[g, t, :, LANES:]
            real = both[:, :LANES] * c - apart[:, LANES:] * s
            imag = both[:, LANES:] * c + apart[:, :LANES] * s
            for l in range(levels):
                sums[l][0].append(level_sum(real, l))
                sums[l][1].append(level_sum(imag, l))
        waves = jnp.broadcast_to(wave_ref[pl.ds(t, 1), :], (height, LANES))
        live = (waves >= 1) & (waves < top_wave) & (2 * waves < lengths)
        found = []
        for l in range(levels):
            ordered = sums[l][0] + sums[l][1]
            rows = [fold(ordered[i : i + 8]) for i in range(0, height, 8)]
            rows = jnp.concatenate(rows, axis=0)
            found.append(jnp.where(live, jnp.where(sine, -rows, rows), 0.0))
        return jnp.concatenate(found, axis=0)

    def stored(t, _):
        coeff_ref[t] = tile(t)
        return 0

    devices, chunk_rows, _ = out_ref.shape
    width = tiles * LANES // devices
    packs = coeff_ref.shape[1] // chunk_rows
    step = LANES // packs
    lane = lax.broadcasted_iota(jnp.int32, (chunk_rows, LANES), 1)
    if circles * tiles <= 64:
        coeffs = [tile(t) for t in range(tiles)]
    else:
        lax.fori_loop(0, tiles, stored, 0)
        coeffs = [coeff_ref.at[t] for t in range(tiles)]
    for d in range(devices):
        t, shift = divmod(d * width, LANES)
        chunk = jnp.zeros((chunk_rows, LANES), F32)
        for p in range(packs):
            rows = slice(p * chunk_rows, (p + 1) * chunk_rows)
            at = p * step
            value = pltpu.roll(coeffs[t][rows], (at - shift) % LANES, 1)
            if shift + width > LANES:
                after = pltpu.roll(coeffs[t + 1][rows], (at - shift) % LANES, 1)
                value = jnp.where(lane < at + LANES - shift, value, after)
            chunk = value if p == 0 else jnp.where(lane < at, chunk, value)
        out_ref[d] = chunk.astype(BF16)


def legendre_kernel(limits_ref, arrived_ref, order_ref, legendre_ref, out_hbm, out_ref, sems, *, packs):
    outputs, slots, top_wave = out_ref.shape
    circles = legendre_ref.shape[0] // slots
    per_tile = LANES // circles
    total = arrived_ref.shape[0]
    turned = lax.dot_general(
        arrived_ref[...], order_ref[...], CONTRACT_ROWS, preferred_element_type=F32
    )

    sub = lax.broadcasted_iota(jnp.int32, (8, LANES), 0)
    block = lax.broadcasted_iota(jnp.int32, (8, LANES), 1) >> log(circles)
    chosen = [(block == b) & ((sub & (per_tile - 1)) == b) for b in range(per_tile)]
    halves = 8 // per_tile
    in_half = [(sub >> log(per_tile)) == h for h in range(halves)]
    step = LANES // packs
    spread = []
    for k in range(slots // 8):
        pieces = [None] * outputs
        for l in range(packs):
            for j in range(total // LANES):
                at = l * step + 8 * k
                v = turned[at : at + 8, j * LANES : (j + 1) * LANES]
                rolled = [v] + [pltpu.roll(v, circles * d, 1) for d in range(1, per_tile)]
                for i in range(per_tile):
                    a = jnp.zeros((8, LANES), F32)
                    for b in range(per_tile):
                        a = jnp.where(chosen[b], rolled[(b - i) % per_tile], a)
                    group_lev, part = divmod(j * per_tile + i, 2)
                    pieces[(group_lev * packs + l) * 2 + part] = jnp.concatenate(
                        [jnp.where(in_half[h], a, 0.0) for h in range(halves)], axis=1
                    )
        spread.append(jnp.concatenate(pieces, axis=0).astype(BF16))

    wide = 2 * LANES
    lane = lax.broadcasted_iota(jnp.int32, (8, wide), 1)
    limits = [limits_ref[8 * k : 8 * k + 8] for k in range(slots // 8)]
    limits = [jnp.concatenate([m, m], axis=1) for m in limits]
    copies = []
    for n in range(0, top_wave, wide):
        sums = [
            jnp.dot(
                spread[k],
                legendre_ref[8 * k * circles : 8 * (k + 1) * circles, n : n + wide],
                preferred_element_type=F32,
            )
            for k in range(slots // 8)
        ]
        keep = [lane + n >= m for m in limits]
        for o in range(outputs):
            out_ref[o, :, n : n + wide] = jnp.concatenate(
                [jnp.where(keep[k], sums[k][8 * o : 8 * o + 8], 0.0) for k in range(slots // 8)],
                axis=0,
            ).astype(BF16)
        columns = (slice(None), slice(None), pl.ds(n, wide))
        copies.append(
            pltpu.make_async_copy(
                out_ref.at[columns], out_hbm.at[columns], sems.at[n // wide]
            )
        )
        copies[-1].start()
    for copy in copies:
        copy.wait()


def other_neighbours(lat, lev):
    inner = [(i, i + 1) for i in range(1, lat - 1, 2)]
    inner += [(j, i) for i, j in inner]
    pairs = [(i * lev + l, j * lev + l) for i, j in inner for l in range(lev)]
    return pairs + [(i * lev + l, i * lev + (l ^ 1)) for i in (0, lat - 1) for l in range(lev)]


def body(
    grid_field, send_blocks, donor_index, tile_choice, kernel_tiles, circle_len, slot_wave, legendre
):
    levels, blocks, _ = grid_field.shape
    send_count = send_blocks.shape[2]
    slots, circles, top_wave = legendre.shape
    lat, lev = lax.axis_size("lat"), lax.axis_size("lev")
    devices = lat * lev
    coarse = PTS // LANES
    own = blocks // coarse
    tiles = slot_wave.shape[0] // LANES
    waves = slot_wave.reshape(tiles, LANES)

    def like(x):
        return jax.ShapeDtypeStruct(x.shape, x.dtype)

    def in_hbm(x):
        return pltpu.with_memory_space_constraint(x, pltpu.HBM)

    halo = jax.ShapeDtypeStruct((send_count, levels * LANES), BF16)
    donors, kinds = donor_index.T, tile_choice.T
    to_far, to_near, field, lengths, waves, donors, kinds, kernels = pl.pallas_call(
        outgoing_kernel,
        out_shape=(
            halo, halo, like(grid_field), jax.ShapeDtypeStruct((2 * own, LANES), jnp.int32),
            like(waves), like(donors), like(kinds), like(kernel_tiles),
        ),
        in_specs=[HBM] * 7, out_specs=(VMEM,) * 8,
        scratch_shapes=[
            pltpu.VMEM(send_blocks.shape, jnp.int32),
            pltpu.SMEM(circle_len.shape, jnp.int32),
            pltpu.SemaphoreType.DMA((7,)),
        ],
        compiler_params=params(4), name="outgoing",
    )(
        *map(in_hbm, (send_blocks, grid_field, circle_len, waves, donors, kinds, kernel_tiles))
    )
    near = lax.ppermute(to_near, "lat", [(i, i ^ 1) for i in range(lat)])
    far = lax.ppermute(to_far, ("lat", "lev"), other_neighbours(lat, lev))

    direct = levels == 2 and 2 * own == 8 and 4 * circles == LANES and slots % 8 == 0
    direct = direct and 2 * slots <= LANES and lev & (lev - 1) == 0
    total = devices * 2 * own if direct else 16
    entries = own * tiles * (LANES + coarse) * 2 * LANES
    choice = jax.ShapeDtypeStruct((blocks, kernel_tiles.shape[0] * send_count), BF16)
    arrival = jax.ShapeDtypeStruct((blocks, levels * LANES), F32)
    fine, wide, limits, far_choice, near_choice, own_part, order = pl.pallas_call(
        functools.partial(table_kernel, lat=lat, lev=lev),
        out_shape=(
            jax.ShapeDtypeStruct((own, tiles, LANES, 2 * LANES), BF16),
            jax.ShapeDtypeStruct((own, tiles, levels * coarse // 2, 2 * LANES), F32),
            jax.ShapeDtypeStruct((slots, LANES), jnp.int32),
            choice,
            choice,
            arrival,
            jax.ShapeDtypeStruct((total, total), BF16),
        ),
        in_specs=[VMEM] * 6 + [HBM], out_specs=(VMEM,) * 7,
        scratch_shapes=[
            pltpu.SMEM(slot_wave.shape, jnp.int32),
            pltpu.SemaphoreType.DMA,
        ],
        compiler_params=params(32), name="tables",
        cost_estimate=pl.CostEstimate(flops=8 * entries, bytes_accessed=3 * entries, transcendentals=0),
    )(lengths, waves, field, donors, kinds, kernels, in_hbm(slot_wave))

    rows = levels * 2 * own
    packs = 1
    while rows % (16 * packs) == 0 and 2 * packs * slots <= LANES:
        packs *= 2
    arrival = pl.pallas_call(
        far_kernel, out_shape=arrival, in_specs=[VMEM] * 4, out_specs=VMEM,
        compiler_params=params(8), name="far_part",
    )(far, far_choice, kernels, own_part)
    coeffs = pl.pallas_call(
        functools.partial(transform_kernel, top_wave=top_wave),
        out_shape=jax.ShapeDtypeStruct((devices, rows // packs, LANES), BF16),
        in_specs=[VMEM] * 8, out_specs=VMEM,
        scratch_shapes=[
            pltpu.VMEM((own, levels * coarse, LANES), BF16),
            pltpu.VMEM((tiles, rows, LANES), F32),
        ],
        compiler_params=params(40), name="transform",
    )(lengths, waves, near, near_choice, arrival, kernels, fine, wide)
    arrived = lax.all_to_all(coeffs, ("lat", "lev"), 0, 0, tiled=True)

    outputs = lev * levels * 2
    height = rows // packs
    if direct:
        spectra = pl.pallas_call(
            functools.partial(legendre_kernel, packs=packs),
            out_shape=jax.ShapeDtypeStruct((outputs, slots, top_wave), BF16),
            in_specs=[VMEM] * 4, out_specs=HBM,
            scratch_shapes=[
                pltpu.VMEM((outputs, slots, top_wave), BF16),
                pltpu.SemaphoreType.DMA((top_wave // (2 * LANES),)),
            ],
            compiler_params=params(32), name="legendre",
        )(
            limits,
            arrived.reshape(devices * height, LANES),
            order,
            legendre.reshape(slots * circles, top_wave),
        )
        return spectra.reshape(outputs // 2, 2, slots, top_wave)

    gathered = arrived.reshape(lat, lev, height, packs, LANES // packs)[..., :slots]
    gathered = gathered.swapaxes(2, 3).reshape(lat, lev, levels, 2, own, slots)
    gathered = gathered.transpose(1, 2, 3, 0, 4, 5).reshape(outputs // 2, 2, circles, slots)
    spectra = jnp.einsum("lcgs,sgn->lcsn", gathered, legendre, preferred_element_type=F32)
    first_slot = (lax.axis_index("lat") * lev + lax.axis_index("lev")) * slots
    mine = lax.dynamic_slice_in_dim(slot_wave, first_slot, slots)
    allowed = jnp.arange(top_wave, dtype=jnp.int32)[None, :] >= mine[:, None]
    return jnp.where(allowed[None, None], spectra, 0.0).astype(BF16)


def solution(mesh):
    return jax.shard_map(
        body,
        mesh=mesh,
        in_specs=(
            P("lev", "lat", None),
            P("lat", None, None),
            P("lat", None),
            P("lat", None),
            P(),
            P(),
            P(),
            P(("lat", "lev"), None, None),
        ),
        out_specs=P(None, None, ("lat", "lev"), None),
        check_vma=False,
    )
```

```python
import functools
import math

import jax
import jax.numpy as jnp
from jax import lax
from jax.experimental import pallas as pl
from jax.experimental.pallas import tpu as pltpu
from jax.sharding import PartitionSpec as P

PTS = 5120
LANES = 128
BF16 = jnp.bfloat16
F32 = jnp.float32
VMEM = pl.BlockSpec(memory_space=pltpu.VMEM)
HBM = pl.BlockSpec(memory_space=pltpu.HBM)
CONTRACT_ROWS = (((0,), (0,)), ((), ()))


def params(mebibytes):
    return pltpu.CompilerParams(vmem_limit_bytes=mebibytes << 20)


def one_hot(condition):
    return jnp.where(condition, 1.0, 0.0).astype(BF16)


def side_by_side(field_ref):
    return jnp.concatenate([field_ref[l] for l in range(field_ref.shape[0])], axis=1)


def outgoing_kernel(
    send_hbm, field_hbm, length_hbm, wave_hbm, donor_hbm, tile_hbm, kernels_hbm,
    far_ref, near_ref, field_ref, lengths_ref, wave_ref, donor_ref, tile_ref, kernels_ref,
    send_ref, length_ref, sems,
):
    pairs = (
        (send_hbm, send_ref), (field_hbm, field_ref), (length_hbm, length_ref), (wave_hbm, wave_ref),
        (donor_hbm, donor_ref), (tile_hbm, tile_ref), (kernels_hbm, kernels_ref),
    )
    copies = [pltpu.make_async_copy(*pair, sems.at[i]) for i, pair in enumerate(pairs)]
    for copy in copies:
        copy.start()
    band = lax.axis_index("lat")
    even = lax.rem(band, 2) == 0
    blocks, count = field_ref.shape[1], send_ref.shape[2]
    rows = lax.broadcasted_iota(jnp.int32, (blocks, count), 0)
    copies[0].wait()
    below, above = send_ref[0, 0:1, :], send_ref[0, 1:2, :]
    far_hot = jnp.transpose(jnp.where(rows == jnp.where(even, below, above), 1.0, 0.0)).astype(BF16)
    near_hot = jnp.transpose(jnp.where(rows == jnp.where(even, above, below), 1.0, 0.0)).astype(BF16)
    copies[1].wait()
    own = side_by_side(field_ref)
    for ref, hot in ((far_ref, far_hot), (near_ref, near_hot)):
        picked = jnp.dot(hot, own, preferred_element_type=F32)
        ref[...] = picked.astype(BF16)
    copies[2].wait()
    circles = lengths_ref.shape[0] // 2
    for i in range(2 * circles):
        length = length_ref[band * circles + i % circles]
        lengths_ref[i : i + 1] = jnp.full((1, LANES), length, jnp.int32)
    for copy in copies[3:]:
        copy.wait()


SINE = (0.07761395, -0.59827207, 2.55007494, -5.16770998, 3.14159264)
COSINE = (0.21953804, -1.33180992, 4.05840238, -4.93479245, 0.99999995)


def turn(steps, waves, length, inverse):
    phase = steps * waves
    rest = phase - jnp.floor(phase * inverse + 0.5) * length
    f = rest * inverse
    x = f * f
    s, c = SINE[0], COSINE[0]
    for p, q in zip(SINE[1:], COSINE[1:]):
        s, c = s * x + p, c * x + q
    s = s * f
    twice = s + s
    return 1.0 - twice * s, twice * c


def log(n):
    return n.bit_length() - 1


def times(a, b):
    return a[0] * b[0] - a[1] * b[1], a[0] * b[1] + a[1] * b[0]


def folded_order(array, coarse):
    half, count = coarse // 2, coarse // 8
    assert coarse % 8 == 0 and half % 8 == 4
    sub = lax.broadcasted_iota(jnp.int32, (8, array.shape[1]), 0)

    def reverse(v):
        v = pltpu.roll(v, 4, 0)
        for h in (2, 1):
            v = jnp.where((sub & h) == 0, pltpu.roll(v, 8 - h, 0), pltpu.roll(v, h, 0))
        return v

    out = []
    for begin in range(0, array.shape[0], coarse):
        rows = [array[begin + 8 * i : begin + 8 * i + 8] for i in range(count)]
        swapped = {i: pltpu.roll(rows[i], 4, 0) for i in range(half // 8, count)}
        for i in range(count):
            q = (8 * i + half) // 8
            if 8 * i + 8 <= half:
                out.append(jnp.where(sub < 4, swapped[q], swapped[q + 1]))
            elif 8 * i < half:
                out.append(jnp.where(sub < 4, swapped[q], reverse(rows[count - 1 - i])))
            else:
                out.append(reverse(rows[count - 1 - i]))
    return jnp.concatenate(out, axis=0)


def table_kernel(
    lengths_ref, wave_ref, field_ref, donor_ref, tile_ref, kernels_ref, slot_hbm,
    fine_ref, coarse_ref, limits_ref, far_choice_ref, near_choice_ref, arrival_ref, order_ref,
    slot_ref, sem, *, lat, lev,
):
    circles, tiles = fine_ref.shape[:2]
    levels, blocks, _ = field_ref.shape
    coarse = blocks // circles
    half = coarse // 2
    fetch = pltpu.make_async_copy(slot_hbm, slot_ref, sem)
    fetch.start()
    row = lax.broadcasted_iota(jnp.int32, (8, LANES), 0)
    near_step = (row + LANES // 2 * (coarse - 1)).astype(F32)
    far_step = (row * LANES + LANES // 2).astype(F32)
    hop_step = jnp.where((row & 1) == 0, 8, 8 * LANES).astype(F32)
    group = 4 if circles % 4 == 0 else 1

    def stepped(base, hop, groups):
        out = [base, times(base, hop)]
        twice = hop[0] + hop[0]
        while len(out) < groups:
            out.append(tuple(twice * x - y for x, y in zip(out[-1], out[-2])))
        return [jnp.concatenate(part, axis=0) for part in zip(*out[:groups])]

    def lengths_of(first):
        each = [
            jnp.broadcast_to(lengths_ref[pl.ds(first + i, 1)], (8, LANES)) for i in range(group)
        ]
        mixed = each[0]
        for i in range(1, group):
            mixed = jnp.where(row >= 2 * i, each[i], mixed)
        return [(x.astype(F32), 1.0 / x.astype(F32)) for x in (*each, mixed)]

    def table(first, t, scales):
        waves = jnp.broadcast_to(wave_ref[pl.ds(t, 1), :], (8, LANES)).astype(F32)
        hops = turn(hop_step, waves, *scales[group])
        for i in range(group):
            near_hop, far_hop = (
                tuple(jnp.broadcast_to(x[k : k + 1], (8, LANES)) for x in hops)
                for k in (2 * i, 2 * i + 1)
            )
            fine = stepped(turn(near_step, waves, *scales[i]), near_hop, LANES // 8)
            fine_ref[first + i, t] = jnp.concatenate(fine, axis=1).astype(BF16)
            wide = stepped(turn(far_step, waves, *scales[i]), far_hop, -(-half // 8))
            coarse_ref[first + i, t] = jnp.concatenate(
                [jnp.concatenate([part[:half]] * levels, axis=0) for part in wide], axis=1
            )

    def looped(index, _):
        first = index // tiles * group
        table(first, lax.rem(index, tiles), lengths_of(first))
        return 0

    listed = jnp.concatenate(
        [donor_ref[...], tile_ref[...], jnp.zeros((4, blocks), jnp.int32)], axis=0
    )
    columns = folded_order(jnp.transpose(listed.astype(F32)), coarse)
    own = side_by_side(field_ref)
    kinds = kernels_ref.shape[0]
    count = far_choice_ref.shape[1] // kinds
    even = lax.rem(lax.axis_index("lat"), 2) == 0
    lane = lax.broadcasted_iota(jnp.int32, (blocks, blocks), 1).astype(F32)
    entry = lax.broadcasted_iota(jnp.int32, far_choice_ref.shape, 1).astype(F32)
    far_choice, near_choice, picked, kind = [], [], [], []
    for k in range(2):
        donor = columns[:, k : k + 1]
        tile = columns[:, 2 + k : 3 + k]
        place = donor - float(blocks)
        above = place >= float(count)
        code = jnp.where(above, place - float(count), place) + float(count) * tile
        code = jnp.where(place >= 0.0, code, -1.0)
        is_far = jnp.logical_xor(above, even)
        far_choice.append(jnp.where(entry == jnp.where(is_far, code, -1.0), 1.0, 0.0))
        near_choice.append(jnp.where(entry == jnp.where(is_far, -1.0, code), 1.0, 0.0))
        picked.append(
            jnp.dot(one_hot(lane == donor), own, preferred_element_type=F32).astype(BF16)
        )
        kind.append(jnp.broadcast_to(tile, (blocks, LANES)))
    far_choice_ref[...] = (far_choice[0] + far_choice[1]).astype(BF16)
    near_choice_ref[...] = (near_choice[0] + near_choice[1]).astype(BF16)
    stacked = jnp.concatenate([kernels_ref[k] for k in range(kinds)], axis=1)
    for l in range(levels):
        total = None
        for k in range(2):
            every = jnp.dot(
                picked[k][:, l * LANES : (l + 1) * LANES], stacked, preferred_element_type=F32
            )
            value = every[:, :LANES]
            for q in range(1, kinds):
                value = jnp.where(kind[k] == float(q), every[:, q * LANES : (q + 1) * LANES], value)
            total = value if k == 0 else total + value
        arrival_ref[:, l * LANES : (l + 1) * LANES] = total

    if circles * tiles <= 64:
        for first in range(0, circles, group):
            scales = lengths_of(first)
            for t in range(tiles):
                table(first, t, scales)
    else:
        lax.fori_loop(0, circles // group * tiles, looped, 0)

    fetch.wait()
    slots = limits_ref.shape[0]
    first = (lax.axis_index("lat") * lev + lax.axis_index("lev")) * slots
    for s in range(slots):
        limits_ref[s : s + 1] = jnp.full((1, LANES), slot_ref[first + s], jnp.int32)

    total = order_ref.shape[0]
    if total == lat * lev * 2 * circles:
        at = lax.broadcasted_iota(jnp.int32, (8, total), 1)
        outer = (at >> log(circles)) & (lat - 1)
        group = at >> log(lat * circles)
        source = (outer << log(circles * 2 * lev)) | (group << log(circles)) | (at & (circles - 1))
        row = lax.broadcasted_iota(jnp.int32, (total, total), 0)
        order_ref[...] = one_hot(row == source[0:1])
    else:
        order_ref[...] = jnp.zeros(order_ref.shape, BF16)


def fold(parts):
    row = lax.broadcasted_iota(jnp.int32, (8, LANES), 0)
    for half in (4, 2, 1):
        low = (row & half) == 0
        count = len(parts) // 2
        parts = [
            jnp.where(low, a, pltpu.roll(b, half, 0)) + jnp.where(low, pltpu.roll(a, 8 - half, 0), b)
            for a, b in zip(parts[:count], parts[count:])
        ]
    return parts[0]


def from_halo(halo, kernels_ref, choice):
    kinds = kernels_ref.shape[0]
    count, levels = halo.shape[0], halo.shape[1] // LANES
    stacked = jnp.concatenate([kernels_ref[k] for k in range(kinds)], axis=1)
    rows = jnp.concatenate(
        [halo[:, l * LANES : (l + 1) * LANES] for l in range(levels)], axis=0
    )
    every = jnp.dot(rows, stacked, preferred_element_type=F32)
    every = jnp.concatenate(
        [
            jnp.concatenate(
                [every[l * count : (l + 1) * count, q * LANES : (q + 1) * LANES] for q in range(kinds)],
                axis=0,
            )
            for l in range(levels)
        ],
        axis=1,
    )
    high = every.astype(BF16)
    low = (every - high.astype(F32)).astype(BF16)
    return jnp.dot(choice, high, preferred_element_type=F32) + jnp.dot(
        choice, low, preferred_element_type=F32
    )


def far_kernel(far_ref, choice_ref, kernels_ref, own_ref, arrival_ref):
    band = lax.axis_index("lat")
    at_end = (band == 0) | (band == lax.axis_size("lat") - 1)
    far = far_ref[...]
    far = jnp.where(at_end, jnp.zeros_like(far), far)
    arrival_ref[...] = own_ref[...] + from_halo(far, kernels_ref, choice_ref[...])


def transform_kernel(
    lengths_ref, wave_ref, near_ref, choice_ref, arrival_ref, kernels_ref, fine_ref,
    coarse_ref, out_ref, points_ref, coeff_ref, *, top_wave,
):
    blocks = arrival_ref.shape[0]
    levels = arrival_ref.shape[1] // LANES
    circles, tiles = fine_ref.shape[:2]
    coarse = blocks // circles
    half = coarse // 2
    arrival = arrival_ref[...] + from_halo(near_ref[...], kernels_ref, choice_ref[...])

    distance = lax.broadcasted_iota(jnp.int32, (coarse, LANES), 0)
    row = jnp.where(distance < half, distance + half, coarse - 1 - distance)
    position = row * LANES + lax.broadcasted_iota(jnp.int32, (coarse, LANES), 1)
    for g in range(circles):
        inside = position < jnp.broadcast_to(lengths_ref[g : g + 1], (coarse, LANES))
        sums, differences = [], []
        for l in range(levels):
            rows = slice(g * coarse, (g + 1) * coarse)
            part = arrival[rows, l * LANES : (l + 1) * LANES]
            part = jnp.where(inside, part * part, 0.0)
            sums.append(part[:half] + part[half:])
            differences.append(part[:half] - part[half:])
        points_ref[g] = jnp.concatenate(sums + differences, axis=0).astype(BF16)

    height = 2 * circles
    lengths = lengths_ref[...]
    sine = lax.broadcasted_iota(jnp.int32, (height, LANES), 0) >= circles
    sub = lax.broadcasted_iota(jnp.int32, (8, LANES), 0)

    def level_sum(value, l):
        first, last = l * half, (l + 1) * half
        total = None
        for at in range(first // 8 * 8, last, 8):
            piece = value[at : at + 8]
            if at < first:
                piece = jnp.where(sub >= first - at, piece, 0.0)
            if at + 8 > last:
                piece = jnp.where(sub < last - at, piece, 0.0)
            total = piece if total is None else total + piece
        return total

    def tile(t):
        sums = [([], []) for _ in range(levels)]
        for g in range(circles):
            turned = jnp.dot(points_ref[g], fine_ref[g, t], preferred_element_type=F32)
            both, apart = turned[: levels * half], turned[levels * half :]
            c, s = coarse_ref[g, t, :, :LANES], coarse_ref[g, t, :, LANES:]
            real = both[:, :LANES] * c - apart[:, LANES:] * s
            imag = both[:, LANES:] * c + apart[:, :LANES] * s
            for l in range(levels):
                sums[l][0].append(level_sum(real, l))
                sums[l][1].append(level_sum(imag, l))
        waves = jnp.broadcast_to(wave_ref[pl.ds(t, 1), :], (height, LANES))
        live = (waves >= 1) & (waves < top_wave) & (2 * waves < lengths)
        found = []
        for l in range(levels):
            ordered = sums[l][0] + sums[l][1]
            rows = [fold(ordered[i : i + 8]) for i in range(0, height, 8)]
            rows = jnp.concatenate(rows, axis=0)
            found.append(jnp.where(live, jnp.where(sine, -rows, rows), 0.0))
        return jnp.concatenate(found, axis=0)

    def stored(t, _):
        coeff_ref[t] = tile(t)
        return 0

    devices, chunk_rows, _ = out_ref.shape
    width = tiles * LANES // devices
    packs = coeff_ref.shape[1] // chunk_rows
    step = LANES // packs
    lane = lax.broadcasted_iota(jnp.int32, (chunk_rows, LANES), 1)
    if circles * tiles <= 64:
        coeffs = [tile(t) for t in range(tiles)]
    else:
        lax.fori_loop(0, tiles, stored, 0)
        coeffs = [coeff_ref.at[t] for t in range(tiles)]
    for d in range(devices):
        t, shift = divmod(d * width, LANES)
        chunk = jnp.zeros((chunk_rows, LANES), F32)
        for p in range(packs):
            rows = slice(p * chunk_rows, (p + 1) * chunk_rows)
            at = p * step
            value = pltpu.roll(coeffs[t][rows], (at - shift) % LANES, 1)
            if shift + width > LANES:
                after = pltpu.roll(coeffs[t + 1][rows], (at - shift) % LANES, 1)
                value = jnp.where(lane < at + LANES - shift, value, after)
            chunk = value if p == 0 else jnp.where(lane < at, chunk, value)
        out_ref[d] = chunk.astype(BF16)


def legendre_kernel(limits_ref, arrived_ref, order_ref, legendre_ref, out_hbm, out_ref, sems, *, packs):
    outputs, slots, top_wave = out_ref.shape
    circles = legendre_ref.shape[0] // slots
    per_tile = LANES // circles
    total = arrived_ref.shape[0]
    turned = lax.dot_general(
        arrived_ref[...], order_ref[...], CONTRACT_ROWS, preferred_element_type=F32
    )

    sub = lax.broadcasted_iota(jnp.int32, (8, LANES), 0)
    block = lax.broadcasted_iota(jnp.int32, (8, LANES), 1) >> log(circles)
    chosen = [(block == b) & ((sub & (per_tile - 1)) == b) for b in range(per_tile)]
    halves = 8 // per_tile
    in_half = [(sub >> log(per_tile)) == h for h in range(halves)]
    step = LANES // packs
    spread = []
    for k in range(slots // 8):
        pieces = [None] * outputs
        for l in range(packs):
            for j in range(total // LANES):
                at = l * step + 8 * k
                v = turned[at : at + 8, j * LANES : (j + 1) * LANES]
                rolled = [v] + [pltpu.roll(v, circles * d, 1) for d in range(1, per_tile)]
                for i in range(per_tile):
                    a = jnp.zeros((8, LANES), F32)
                    for b in range(per_tile):
                        a = jnp.where(chosen[b], rolled[(b - i) % per_tile], a)
                    group_lev, part = divmod(j * per_tile + i, 2)
                    pieces[(group_lev * packs + l) * 2 + part] = jnp.concatenate(
                        [jnp.where(in_half[h], a, 0.0) for h in range(halves)], axis=1
                    )
        spread.append(jnp.concatenate(pieces, axis=0).astype(BF16))

    wide = 2 * LANES
    lane = lax.broadcasted_iota(jnp.int32, (8, wide), 1)
    limits = [limits_ref[8 * k : 8 * k + 8] for k in range(slots // 8)]
    limits = [jnp.concatenate([m, m], axis=1) for m in limits]
    copies = []
    for n in range(0, top_wave, wide):
        sums = [
            jnp.dot(
                spread[k],
                legendre_ref[8 * k * circles : 8 * (k + 1) * circles, n : n + wide],
                preferred_element_type=F32,
            )
            for k in range(slots // 8)
        ]
        keep = [lane + n >= m for m in limits]
        for o in range(outputs):
            out_ref[o, :, n : n + wide] = jnp.concatenate(
                [jnp.where(keep[k], sums[k][8 * o : 8 * o + 8], 0.0) for k in range(slots // 8)],
                axis=0,
            ).astype(BF16)
        columns = (slice(None), slice(None), pl.ds(n, wide))
        copies.append(
            pltpu.make_async_copy(
                out_ref.at[columns], out_hbm.at[columns], sems.at[n // wide]
            )
        )
        copies[-1].start()
    for copy in copies:
        copy.wait()


def other_neighbours(lat, lev):
    inner = [(i, i + 1) for i in range(1, lat - 1, 2)]
    inner += [(j, i) for i, j in inner]
    pairs = [(i * lev + l, j * lev + l) for i, j in inner for l in range(lev)]
    return pairs + [(i * lev + l, i * lev + (l ^ 1)) for i in (0, lat - 1) for l in range(lev)]


def body(
    grid_field, send_blocks, donor_index, tile_choice, kernel_tiles, circle_len, slot_wave, legendre
):
    levels, blocks, _ = grid_field.shape
    send_count = send_blocks.shape[2]
    slots, circles, top_wave = legendre.shape
    lat, lev = lax.axis_size("lat"), lax.axis_size("lev")
    devices = lat * lev
    coarse = PTS // LANES
    own = blocks // coarse
    tiles = slot_wave.shape[0] // LANES
    waves = slot_wave.reshape(tiles, LANES)

    def like(x):
        return jax.ShapeDtypeStruct(x.shape, x.dtype)

    def in_hbm(x):
        return pltpu.with_memory_space_constraint(x, pltpu.HBM)

    halo = jax.ShapeDtypeStruct((send_count, levels * LANES), BF16)
    donors, kinds = donor_index.T, tile_choice.T
    to_far, to_near, field, lengths, waves, donors, kinds, kernels = pl.pallas_call(
        outgoing_kernel,
        out_shape=(
            halo, halo, like(grid_field), jax.ShapeDtypeStruct((2 * own, LANES), jnp.int32),
            like(waves), like(donors), like(kinds), like(kernel_tiles),
        ),
        in_specs=[HBM] * 7, out_specs=(VMEM,) * 8,
        scratch_shapes=[
            pltpu.VMEM(send_blocks.shape, jnp.int32),
            pltpu.SMEM(circle_len.shape, jnp.int32),
            pltpu.SemaphoreType.DMA((7,)),
        ],
        compiler_params=params(4), name="outgoing",
    )(
        *map(in_hbm, (send_blocks, grid_field, circle_len, waves, donors, kinds, kernel_tiles))
    )
    near = lax.ppermute(to_near, "lat", [(i, i ^ 1) for i in range(lat)])
    far = lax.ppermute(to_far, ("lat", "lev"), other_neighbours(lat, lev))

    direct = levels == 2 and 2 * own == 8 and 4 * circles == LANES and slots % 8 == 0
    direct = direct and 2 * slots <= LANES and lev & (lev - 1) == 0
    total = devices * 2 * own if direct else 16
    entries = own * tiles * (LANES + coarse) * 2 * LANES
    choice = jax.ShapeDtypeStruct((blocks, kernel_tiles.shape[0] * send_count), BF16)
    arrival = jax.ShapeDtypeStruct((blocks, levels * LANES), F32)
    fine, wide, limits, far_choice, near_choice, own_part, order = pl.pallas_call(
        functools.partial(table_kernel, lat=lat, lev=lev),
        out_shape=(
            jax.ShapeDtypeStruct((own, tiles, LANES, 2 * LANES), BF16),
            jax.ShapeDtypeStruct((own, tiles, levels * coarse // 2, 2 * LANES), F32),
            jax.ShapeDtypeStruct((slots, LANES), jnp.int32),
            choice,
            choice,
            arrival,
            jax.ShapeDtypeStruct((total, total), BF16),
        ),
        in_specs=[VMEM] * 6 + [HBM], out_specs=(VMEM,) * 7,
        scratch_shapes=[
            pltpu.SMEM(slot_wave.shape, jnp.int32),
            pltpu.SemaphoreType.DMA,
        ],
        compiler_params=params(32), name="tables",
        cost_estimate=pl.CostEstimate(flops=8 * entries, bytes_accessed=3 * entries, transcendentals=0),
    )(lengths, waves, field, donors, kinds, kernels, in_hbm(slot_wave))

    rows = levels * 2 * own
    packs = 1
    while rows % (16 * packs) == 0 and 2 * packs * slots <= LANES:
        packs *= 2
    arrival = pl.pallas_call(
        far_kernel, out_shape=arrival, in_specs=[VMEM] * 4, out_specs=VMEM,
        compiler_params=params(8), name="far_part",
    )(far, far_choice, kernels, own_part)
    coeffs = pl.pallas_call(
        functools.partial(transform_kernel, top_wave=top_wave),
        out_shape=jax.ShapeDtypeStruct((devices, rows // packs, LANES), BF16),
        in_specs=[VMEM] * 8, out_specs=VMEM,
        scratch_shapes=[
            pltpu.VMEM((own, levels * coarse, LANES), BF16),
            pltpu.VMEM((tiles, rows, LANES), F32),
        ],
        compiler_params=params(40), name="transform",
    )(lengths, waves, near, near_choice, arrival, kernels, fine, wide)
    arrived = lax.all_to_all(coeffs, ("lat", "lev"), 0, 0, tiled=True)

    outputs = lev * levels * 2
    height = rows // packs
    if direct:
        spectra = pl.pallas_call(
            functools.partial(legendre_kernel, packs=packs),
            out_shape=jax.ShapeDtypeStruct((outputs, slots, top_wave), BF16),
            in_specs=[VMEM] * 4, out_specs=HBM,
            scratch_shapes=[
                pltpu.VMEM((outputs, slots, top_wave), BF16),
                pltpu.SemaphoreType.DMA((top_wave // (2 * LANES),)),
            ],
            compiler_params=params(32), name="legendre",
        )(
            limits,
            arrived.reshape(devices * height, LANES),
            order,
            legendre.reshape(slots * circles, top_wave),
        )
        return spectra.reshape(outputs // 2, 2, slots, top_wave)

    gathered = arrived.reshape(lat, lev, height, packs, LANES // packs)[..., :slots]
    gathered = gathered.swapaxes(2, 3).reshape(lat, lev, levels, 2, own, slots)
    gathered = gathered.transpose(1, 2, 3, 0, 4, 5).reshape(outputs // 2, 2, circles, slots)
    spectra = jnp.einsum("lcgs,sgn->lcsn", gathered, legendre, preferred_element_type=F32)
    first_slot = (lax.axis_index("lat") * lev + lax.axis_index("lev")) * slots
    mine = lax.dynamic_slice_in_dim(slot_wave, first_slot, slots)
    allowed = jnp.arange(top_wave, dtype=jnp.int32)[None, :] >= mine[:, None]
    return jnp.where(allowed[None, None], spectra, 0.0).astype(BF16)


def solution(mesh):
    return jax.shard_map(
        body,
        mesh=mesh,
        in_specs=(
            P("lev", "lat", None),
            P("lat", None, None),
            P("lat", None),
            P("lat", None),
            P(),
            P(),
            P(),
            P(("lat", "lev"), None, None),
        ),
        out_specs=P(None, None, ("lat", "lev"), None),
        check_vma=False,
    )
```

```python
import functools
import math

import jax
import jax.numpy as jnp
from jax import lax
from jax.experimental import pallas as pl
from jax.experimental.pallas import tpu as pltpu
from jax.sharding import PartitionSpec as P

PTS = 5120
LANES = 128
BF16 = jnp.bfloat16
F32 = jnp.float32
VMEM = pl.BlockSpec(memory_space=pltpu.VMEM)
HBM = pl.BlockSpec(memory_space=pltpu.HBM)
CONTRACT_ROWS = (((0,), (0,)), ((), ()))


def params(mebibytes):
    return pltpu.CompilerParams(vmem_limit_bytes=mebibytes << 20)


def one_hot(condition):
    return jnp.where(condition, 1.0, 0.0).astype(BF16)


def side_by_side(field_ref):
    return jnp.concatenate([field_ref[l] for l in range(field_ref.shape[0])], axis=1)


def outgoing_kernel(
    send_hbm, field_hbm, length_hbm, wave_hbm, donor_hbm, tile_hbm, kernels_hbm,
    far_ref, near_ref, field_ref, lengths_ref, wave_ref, donor_ref, tile_ref, kernels_ref,
    send_ref, length_ref, sems,
):
    pairs = (
        (send_hbm, send_ref), (field_hbm, field_ref), (length_hbm, length_ref), (wave_hbm, wave_ref),
        (donor_hbm, donor_ref), (tile_hbm, tile_ref), (kernels_hbm, kernels_ref),
    )
    copies = [pltpu.make_async_copy(*pair, sems.at[i]) for i, pair in enumerate(pairs)]
    for copy in copies:
        copy.start()
    band = lax.axis_index("lat")
    even = lax.rem(band, 2) == 0
    blocks, count = field_ref.shape[1], send_ref.shape[2]
    rows = lax.broadcasted_iota(jnp.int32, (blocks, count), 0)
    copies[0].wait()
    below, above = send_ref[0, 0:1, :], send_ref[0, 1:2, :]
    far_hot = jnp.transpose(jnp.where(rows == jnp.where(even, below, above), 1.0, 0.0)).astype(BF16)
    near_hot = jnp.transpose(jnp.where(rows == jnp.where(even, above, below), 1.0, 0.0)).astype(BF16)
    copies[1].wait()
    own = side_by_side(field_ref)
    for ref, hot in ((far_ref, far_hot), (near_ref, near_hot)):
        picked = jnp.dot(hot, own, preferred_element_type=F32)
        ref[...] = picked.astype(BF16)
    copies[2].wait()
    circles = lengths_ref.shape[0] // 2
    for i in range(2 * circles):
        length = length_ref[band * circles + i % circles]
        lengths_ref[i : i + 1] = jnp.full((1, LANES), length, jnp.int32)
    for copy in copies[3:]:
        copy.wait()


SINE = (0.07761395, -0.59827207, 2.55007494, -5.16770998, 3.14159264)
COSINE = (0.21953804, -1.33180992, 4.05840238, -4.93479245, 0.99999995)


def turn(steps, waves, length, inverse):
    phase = steps * waves
    rest = phase - jnp.floor(phase * inverse + 0.5) * length
    f = rest * inverse
    x = f * f
    s, c = SINE[0], COSINE[0]
    for p, q in zip(SINE[1:], COSINE[1:]):
        s, c = s * x + p, c * x + q
    s = s * f
    twice = s + s
    return 1.0 - twice * s, twice * c


def log(n):
    return n.bit_length() - 1


def times(a, b):
    return a[0] * b[0] - a[1] * b[1], a[0] * b[1] + a[1] * b[0]


def folded_order(array, coarse):
    half, count = coarse // 2, coarse // 8
    assert coarse % 8 == 0 and half % 8 == 4
    sub = lax.broadcasted_iota(jnp.int32, (8, array.shape[1]), 0)

    def reverse(v):
        v = pltpu.roll(v, 4, 0)
        for h in (2, 1):
            v = jnp.where((sub & h) == 0, pltpu.roll(v, 8 - h, 0), pltpu.roll(v, h, 0))
        return v

    out = []
    for begin in range(0, array.shape[0], coarse):
        rows = [array[begin + 8 * i : begin + 8 * i + 8] for i in range(count)]
        swapped = {i: pltpu.roll(rows[i], 4, 0) for i in range(half // 8, count)}
        for i in range(count):
            q = (8 * i + half) // 8
            if 8 * i + 8 <= half:
                out.append(jnp.where(sub < 4, swapped[q], swapped[q + 1]))
            elif 8 * i < half:
                out.append(jnp.where(sub < 4, swapped[q], reverse(rows[count - 1 - i])))
            else:
                out.append(reverse(rows[count - 1 - i]))
    return jnp.concatenate(out, axis=0)


def table_kernel(
    lengths_ref, wave_ref, field_ref, donor_ref, tile_ref, kernels_ref, slot_hbm,
    fine_ref, coarse_ref, limits_ref, far_choice_ref, near_choice_ref, arrival_ref, order_ref,
    slot_ref, sem, *, lat, lev,
):
    circles, tiles = fine_ref.shape[:2]
    levels, blocks, _ = field_ref.shape
    coarse = blocks // circles
    half = coarse // 2
    fetch = pltpu.make_async_copy(slot_hbm, slot_ref, sem)
    fetch.start()
    row = lax.broadcasted_iota(jnp.int32, (8, LANES), 0)
    near_step = (row + LANES // 2 * (coarse - 1)).astype(F32)
    far_step = (row * LANES + LANES // 2).astype(F32)
    hop_step = jnp.where((row & 1) == 0, 8, 8 * LANES).astype(F32)
    group = 4 if circles % 4 == 0 else 1

    def stepped(base, hop, groups):
        out = [base, times(base, hop)]
        twice = hop[0] + hop[0]
        while len(out) < groups:
            out.append(tuple(twice * x - y for x, y in zip(out[-1], out[-2])))
        return [jnp.concatenate(part, axis=0) for part in zip(*out[:groups])]

    def lengths_of(first):
        each = [
            jnp.broadcast_to(lengths_ref[pl.ds(first + i, 1)], (8, LANES)) for i in range(group)
        ]
        mixed = each[0]
        for i in range(1, group):
            mixed = jnp.where(row >= 2 * i, each[i], mixed)
        return [(x.astype(F32), 1.0 / x.astype(F32)) for x in (*each, mixed)]

    def table(first, t, scales):
        waves = jnp.broadcast_to(wave_ref[pl.ds(t, 1), :], (8, LANES)).astype(F32)
        hops = turn(hop_step, waves, *scales[group])
        for i in range(group):
            near_hop, far_hop = (
                tuple(jnp.broadcast_to(x[k : k + 1], (8, LANES)) for x in hops)
                for k in (2 * i, 2 * i + 1)
            )
            fine = stepped(turn(near_step, waves, *scales[i]), near_hop, LANES // 8)
            fine_ref[first + i, t] = jnp.concatenate(fine, axis=1).astype(BF16)
            wide = stepped(turn(far_step, waves, *scales[i]), far_hop, -(-half // 8))
            coarse_ref[first + i, t] = jnp.concatenate(
                [jnp.concatenate([part[:half]] * levels, axis=0) for part in wide], axis=1
            )

    def looped(index, _):
        first = index // tiles * group
        table(first, lax.rem(index, tiles), lengths_of(first))
        return 0

    listed = jnp.concatenate(
        [donor_ref[...], tile_ref[...], jnp.zeros((4, blocks), jnp.int32)], axis=0
    )
    columns = folded_order(jnp.transpose(listed.astype(F32)), coarse)
    own = side_by_side(field_ref)
    kinds = kernels_ref.shape[0]
    count = far_choice_ref.shape[1] // kinds
    even = lax.rem(lax.axis_index("lat"), 2) == 0
    lane = lax.broadcasted_iota(jnp.int32, (blocks, blocks), 1).astype(F32)
    entry = lax.broadcasted_iota(jnp.int32, far_choice_ref.shape, 1).astype(F32)
    far_choice, near_choice, picked, kind = [], [], [], []
    for k in range(2):
        donor = columns[:, k : k + 1]
        tile = columns[:, 2 + k : 3 + k]
        place = donor - float(blocks)
        above = place >= float(count)
        code = jnp.where(above, place - float(count), place) + float(count) * tile
        code = jnp.where(place >= 0.0, code, -1.0)
        is_far = jnp.logical_xor(above, even)
        far_choice.append(jnp.where(entry == jnp.where(is_far, code, -1.0), 1.0, 0.0))
        near_choice.append(jnp.where(entry == jnp.where(is_far, -1.0, code), 1.0, 0.0))
        picked.append(
            jnp.dot(one_hot(lane == donor), own, preferred_element_type=F32).astype(BF16)
        )
        kind.append(jnp.broadcast_to(tile, (blocks, LANES)))
    far_choice_ref[...] = (far_choice[0] + far_choice[1]).astype(BF16)
    near_choice_ref[...] = (near_choice[0] + near_choice[1]).astype(BF16)
    stacked = jnp.concatenate([kernels_ref[k] for k in range(kinds)], axis=1)
    for l in range(levels):
        total = None
        for k in range(2):
            every = jnp.dot(
                picked[k][:, l * LANES : (l + 1) * LANES], stacked, preferred_element_type=F32
            )
            value = every[:, :LANES]
            for q in range(1, kinds):
                value = jnp.where(kind[k] == float(q), every[:, q * LANES : (q + 1) * LANES], value)
            total = value if k == 0 else total + value
        arrival_ref[:, l * LANES : (l + 1) * LANES] = total

    if circles * tiles <= 64:
        for first in range(0, circles, group):
            scales = lengths_of(first)
            for t in range(tiles):
                table(first, t, scales)
    else:
        lax.fori_loop(0, circles // group * tiles, looped, 0)

    fetch.wait()
    slots = limits_ref.shape[0]
    first = (lax.axis_index("lat") * lev + lax.axis_index("lev")) * slots
    for s in range(slots):
        limits_ref[s : s + 1] = jnp.full((1, LANES), slot_ref[first + s], jnp.int32)

    total = order_ref.shape[0]
    if total == lat * lev * 2 * circles:
        at = lax.broadcasted_iota(jnp.int32, (8, total), 1)
        outer = (at >> log(circles)) & (lat - 1)
        group = at >> log(lat * circles)
        source = (outer << log(circles * 2 * lev)) | (group << log(circles)) | (at & (circles - 1))
        row = lax.broadcasted_iota(jnp.int32, (total, total), 0)
        order_ref[...] = one_hot(row == source[0:1])
    else:
        order_ref[...] = jnp.zeros(order_ref.shape, BF16)


def fold(parts):
    row = lax.broadcasted_iota(jnp.int32, (8, LANES), 0)
    for half in (4, 2, 1):
        low = (row & half) == 0
        count = len(parts) // 2
        parts = [
            jnp.where(low, a, pltpu.roll(b, half, 0)) + jnp.where(low, pltpu.roll(a, 8 - half, 0), b)
            for a, b in zip(parts[:count], parts[count:])
        ]
    return parts[0]


def from_halo(halo, kernels_ref, choice):
    kinds = kernels_ref.shape[0]
    count, levels = halo.shape[0], halo.shape[1] // LANES
    stacked = jnp.concatenate([kernels_ref[k] for k in range(kinds)], axis=1)
    rows = jnp.concatenate(
        [halo[:, l * LANES : (l + 1) * LANES] for l in range(levels)], axis=0
    )
    every = jnp.dot(rows, stacked, preferred_element_type=F32)
    every = jnp.concatenate(
        [
            jnp.concatenate(
                [every[l * count : (l + 1) * count, q * LANES : (q + 1) * LANES] for q in range(kinds)],
                axis=0,
            )
            for l in range(levels)
        ],
        axis=1,
    )
    high = every.astype(BF16)
    low = (every - high.astype(F32)).astype(BF16)
    return jnp.dot(choice, high, preferred_element_type=F32) + jnp.dot(
        choice, low, preferred_element_type=F32
    )


def far_kernel(far_ref, choice_ref, kernels_ref, own_ref, arrival_ref):
    band = lax.axis_index("lat")
    at_end = (band == 0) | (band == lax.axis_size("lat") - 1)
    far = far_ref[...]
    far = jnp.where(at_end, jnp.zeros_like(far), far)
    arrival_ref[...] = own_ref[...] + from_halo(far, kernels_ref, choice_ref[...])


def transform_kernel(
    lengths_ref, wave_ref, near_ref, choice_ref, arrival_ref, kernels_ref, fine_ref,
    coarse_ref, out_ref, points_ref, coeff_ref, *, top_wave,
):
    blocks = arrival_ref.shape[0]
    levels = arrival_ref.shape[1] // LANES
    circles, tiles = fine_ref.shape[:2]
    coarse = blocks // circles
    half = coarse // 2
    arrival = arrival_ref[...] + from_halo(near_ref[...], kernels_ref, choice_ref[...])

    distance = lax.broadcasted_iota(jnp.int32, (coarse, LANES), 0)
    row = jnp.where(distance < half, distance + half, coarse - 1 - distance)
    position = row * LANES + lax.broadcasted_iota(jnp.int32, (coarse, LANES), 1)
    unrolled = circles * tiles <= 64
    points = []
    for g in range(circles):
        inside = position < jnp.broadcast_to(lengths_ref[g : g + 1], (coarse, LANES))
        sums, differences = [], []
        for l in range(levels):
            rows = slice(g * coarse, (g + 1) * coarse)
            part = arrival[rows, l * LANES : (l + 1) * LANES]
            part = jnp.where(inside, part * part, 0.0)
            sums.append(part[:half] + part[half:])
            differences.append(part[:half] - part[half:])
        points.append(jnp.concatenate(sums + differences, axis=0).astype(BF16))
        if not unrolled:
            points_ref[g] = points[g]

    height = 2 * circles
    lengths = lengths_ref[...]
    sine = lax.broadcasted_iota(jnp.int32, (height, LANES), 0) >= circles
    sub = lax.broadcasted_iota(jnp.int32, (8, LANES), 0)

    def level_sum(value, l):
        first, last = l * half, (l + 1) * half
        total = None
        for at in range(first // 8 * 8, last, 8):
            piece = value[at : at + 8]
            if at < first:
                piece = jnp.where(sub >= first - at, piece, 0.0)
            if at + 8 > last:
                piece = jnp.where(sub < last - at, piece, 0.0)
            total = piece if total is None else total + piece
        return total

    def tile(t):
        sums = [([], []) for _ in range(levels)]
        for g in range(circles):
            rows = points[g] if unrolled else points_ref[g]
            turned = jnp.dot(rows, fine_ref[g, t], preferred_element_type=F32)
            both, apart = turned[: levels * half], turned[levels * half :]
            c, s = coarse_ref[g, t, :, :LANES], coarse_ref[g, t, :, LANES:]
            real = both[:, :LANES] * c - apart[:, LANES:] * s
            imag = both[:, LANES:] * c + apart[:, :LANES] * s
            for l in range(levels):
                sums[l][0].append(level_sum(real, l))
                sums[l][1].append(level_sum(imag, l))
        waves = jnp.broadcast_to(wave_ref[pl.ds(t, 1), :], (height, LANES))
        live = (waves >= 1) & (waves < top_wave) & (2 * waves < lengths)
        found = []
        for l in range(levels):
            ordered = sums[l][0] + sums[l][1]
            rows = [fold(ordered[i : i + 8]) for i in range(0, height, 8)]
            rows = jnp.concatenate(rows, axis=0)
            found.append(jnp.where(live, jnp.where(sine, -rows, rows), 0.0))
        return jnp.concatenate(found, axis=0)

    def stored(t, _):
        coeff_ref[t] = tile(t)
        return 0

    devices, chunk_rows, _ = out_ref.shape
    width = tiles * LANES // devices
    packs = coeff_ref.shape[1] // chunk_rows
    step = LANES // packs
    lane = lax.broadcasted_iota(jnp.int32, (chunk_rows, LANES), 1)
    if unrolled:
        coeffs = [tile(t) for t in range(tiles)]
    else:
        lax.fori_loop(0, tiles, stored, 0)
        coeffs = [coeff_ref.at[t] for t in range(tiles)]
    for d in range(devices):
        t, shift = divmod(d * width, LANES)
        chunk = jnp.zeros((chunk_rows, LANES), F32)
        for p in range(packs):
            rows = slice(p * chunk_rows, (p + 1) * chunk_rows)
            at = p * step
            value = pltpu.roll(coeffs[t][rows], (at - shift) % LANES, 1)
            if shift + width > LANES:
                after = pltpu.roll(coeffs[t + 1][rows], (at - shift) % LANES, 1)
                value = jnp.where(lane < at + LANES - shift, value, after)
            chunk = value if p == 0 else jnp.where(lane < at, chunk, value)
        out_ref[d] = chunk.astype(BF16)


def legendre_kernel(limits_ref, arrived_ref, order_ref, legendre_ref, out_hbm, out_ref, sems, *, packs):
    outputs, slots, top_wave = out_ref.shape
    circles = legendre_ref.shape[0] // slots
    per_tile = LANES // circles
    total = arrived_ref.shape[0]
    turned = lax.dot_general(
        arrived_ref[...], order_ref[...], CONTRACT_ROWS, preferred_element_type=F32
    )

    sub = lax.broadcasted_iota(jnp.int32, (8, LANES), 0)
    block = lax.broadcasted_iota(jnp.int32, (8, LANES), 1) >> log(circles)
    chosen = [(block == b) & ((sub & (per_tile - 1)) == b) for b in range(per_tile)]
    halves = 8 // per_tile
    in_half = [(sub >> log(per_tile)) == h for h in range(halves)]
    step = LANES // packs
    spread = []
    for k in range(slots // 8):
        pieces = [None] * outputs
        for l in range(packs):
            for j in range(total // LANES):
                at = l * step + 8 * k
                v = turned[at : at + 8, j * LANES : (j + 1) * LANES]
                rolled = [v] + [pltpu.roll(v, circles * d, 1) for d in range(1, per_tile)]
                for i in range(per_tile):
                    a = jnp.zeros((8, LANES), F32)
                    for b in range(per_tile):
                        a = jnp.where(chosen[b], rolled[(b - i) % per_tile], a)
                    group_lev, part = divmod(j * per_tile + i, 2)
                    pieces[(group_lev * packs + l) * 2 + part] = jnp.concatenate(
                        [jnp.where(in_half[h], a, 0.0) for h in range(halves)], axis=1
                    )
        spread.append(jnp.concatenate(pieces, axis=0).astype(BF16))

    wide = 2 * LANES
    lane = lax.broadcasted_iota(jnp.int32, (8, wide), 1)
    limits = [limits_ref[8 * k : 8 * k + 8] for k in range(slots // 8)]
    limits = [jnp.concatenate([m, m], axis=1) for m in limits]
    copies = []
    for n in range(0, top_wave, wide):
        sums = [
            jnp.dot(
                spread[k],
                legendre_ref[8 * k * circles : 8 * (k + 1) * circles, n : n + wide],
                preferred_element_type=F32,
            )
            for k in range(slots // 8)
        ]
        keep = [lane + n >= m for m in limits]
        for o in range(outputs):
            out_ref[o, :, n : n + wide] = jnp.concatenate(
                [jnp.where(keep[k], sums[k][8 * o : 8 * o + 8], 0.0) for k in range(slots // 8)],
                axis=0,
            ).astype(BF16)
        columns = (slice(None), slice(None), pl.ds(n, wide))
        copies.append(
            pltpu.make_async_copy(
                out_ref.at[columns], out_hbm.at[columns], sems.at[n // wide]
            )
        )
        copies[-1].start()
    for copy in copies:
        copy.wait()


def other_neighbours(lat, lev):
    inner = [(i, i + 1) for i in range(1, lat - 1, 2)]
    inner += [(j, i) for i, j in inner]
    pairs = [(i * lev + l, j * lev + l) for i, j in inner for l in range(lev)]
    return pairs + [(i * lev + l, i * lev + (l ^ 1)) for i in (0, lat - 1) for l in range(lev)]


def body(
    grid_field, send_blocks, donor_index, tile_choice, kernel_tiles, circle_len, slot_wave, legendre
):
    levels, blocks, _ = grid_field.shape
    send_count = send_blocks.shape[2]
    slots, circles, top_wave = legendre.shape
    lat, lev = lax.axis_size("lat"), lax.axis_size("lev")
    devices = lat * lev
    coarse = PTS // LANES
    own = blocks // coarse
    tiles = slot_wave.shape[0] // LANES
    waves = slot_wave.reshape(tiles, LANES)

    def like(x):
        return jax.ShapeDtypeStruct(x.shape, x.dtype)

    def in_hbm(x):
        return pltpu.with_memory_space_constraint(x, pltpu.HBM)

    halo = jax.ShapeDtypeStruct((send_count, levels * LANES), BF16)
    donors, kinds = donor_index.T, tile_choice.T
    to_far, to_near, field, lengths, waves, donors, kinds, kernels = pl.pallas_call(
        outgoing_kernel,
        out_shape=(
            halo, halo, like(grid_field), jax.ShapeDtypeStruct((2 * own, LANES), jnp.int32),
            like(waves), like(donors), like(kinds), like(kernel_tiles),
        ),
        in_specs=[HBM] * 7, out_specs=(VMEM,) * 8,
        scratch_shapes=[
            pltpu.VMEM(send_blocks.shape, jnp.int32),
            pltpu.SMEM(circle_len.shape, jnp.int32),
            pltpu.SemaphoreType.DMA((7,)),
        ],
        compiler_params=params(4), name="outgoing",
    )(
        *map(in_hbm, (send_blocks, grid_field, circle_len, waves, donors, kinds, kernel_tiles))
    )
    near = lax.ppermute(to_near, "lat", [(i, i ^ 1) for i in range(lat)])
    far = lax.ppermute(to_far, ("lat", "lev"), other_neighbours(lat, lev))

    direct = levels == 2 and 2 * own == 8 and 4 * circles == LANES and slots % 8 == 0
    direct = direct and 2 * slots <= LANES and lev & (lev - 1) == 0
    total = devices * 2 * own if direct else 16
    entries = own * tiles * (LANES + coarse) * 2 * LANES
    choice = jax.ShapeDtypeStruct((blocks, kernel_tiles.shape[0] * send_count), BF16)
    arrival = jax.ShapeDtypeStruct((blocks, levels * LANES), F32)
    fine, wide, limits, far_choice, near_choice, own_part, order = pl.pallas_call(
        functools.partial(table_kernel, lat=lat, lev=lev),
        out_shape=(
            jax.ShapeDtypeStruct((own, tiles, LANES, 2 * LANES), BF16),
            jax.ShapeDtypeStruct((own, tiles, levels * coarse // 2, 2 * LANES), F32),
            jax.ShapeDtypeStruct((slots, LANES), jnp.int32),
            choice,
            choice,
            arrival,
            jax.ShapeDtypeStruct((total, total), BF16),
        ),
        in_specs=[VMEM] * 6 + [HBM], out_specs=(VMEM,) * 7,
        scratch_shapes=[
            pltpu.SMEM(slot_wave.shape, jnp.int32),
            pltpu.SemaphoreType.DMA,
        ],
        compiler_params=params(32), name="tables",
        cost_estimate=pl.CostEstimate(flops=8 * entries, bytes_accessed=3 * entries, transcendentals=0),
    )(lengths, waves, field, donors, kinds, kernels, in_hbm(slot_wave))

    rows = levels * 2 * own
    packs = 1
    while rows % (16 * packs) == 0 and 2 * packs * slots <= LANES:
        packs *= 2
    arrival = pl.pallas_call(
        far_kernel, out_shape=arrival, in_specs=[VMEM] * 4, out_specs=VMEM,
        compiler_params=params(8), name="far_part",
    )(far, far_choice, kernels, own_part)
    coeffs = pl.pallas_call(
        functools.partial(transform_kernel, top_wave=top_wave),
        out_shape=jax.ShapeDtypeStruct((devices, rows // packs, LANES), BF16),
        in_specs=[VMEM] * 8, out_specs=VMEM,
        scratch_shapes=[
            pltpu.VMEM((own, levels * coarse, LANES), BF16),
            pltpu.VMEM((tiles, rows, LANES), F32),
        ],
        compiler_params=params(40), name="transform",
    )(lengths, waves, near, near_choice, arrival, kernels, fine, wide)
    arrived = lax.all_to_all(coeffs, ("lat", "lev"), 0, 0, tiled=True)

    outputs = lev * levels * 2
    height = rows // packs
    if direct:
        spectra = pl.pallas_call(
            functools.partial(legendre_kernel, packs=packs),
            out_shape=jax.ShapeDtypeStruct((outputs, slots, top_wave), BF16),
            in_specs=[VMEM] * 4, out_specs=HBM,
            scratch_shapes=[
                pltpu.VMEM((outputs, slots, top_wave), BF16),
                pltpu.SemaphoreType.DMA((top_wave // (2 * LANES),)),
            ],
            compiler_params=params(32), name="legendre",
        )(
            limits,
            arrived.reshape(devices * height, LANES),
            order,
            legendre.reshape(slots * circles, top_wave),
        )
        return spectra.reshape(outputs // 2, 2, slots, top_wave)

    gathered = arrived.reshape(lat, lev, height, packs, LANES // packs)[..., :slots]
    gathered = gathered.swapaxes(2, 3).reshape(lat, lev, levels, 2, own, slots)
    gathered = gathered.transpose(1, 2, 3, 0, 4, 5).reshape(outputs // 2, 2, circles, slots)
    spectra = jnp.einsum("lcgs,sgn->lcsn", gathered, legendre, preferred_element_type=F32)
    first_slot = (lax.axis_index("lat") * lev + lax.axis_index("lev")) * slots
    mine = lax.dynamic_slice_in_dim(slot_wave, first_slot, slots)
    allowed = jnp.arange(top_wave, dtype=jnp.int32)[None, :] >= mine[:, None]
    return jnp.where(allowed[None, None], spectra, 0.0).astype(BF16)


def solution(mesh):
    return jax.shard_map(
        body,
        mesh=mesh,
        in_specs=(
            P("lev", "lat", None),
            P("lat", None, None),
            P("lat", None),
            P("lat", None),
            P(),
            P(),
            P(),
            P(("lat", "lev"), None, None),
        ),
        out_specs=P(None, None, ("lat", "lev"), None),
        check_vma=False,
    )
```

```python
import functools
import math

import jax
import jax.numpy as jnp
from jax import lax
from jax.experimental import pallas as pl
from jax.experimental.pallas import tpu as pltpu
from jax.sharding import PartitionSpec as P

PTS = 5120
LANES = 128
BF16 = jnp.bfloat16
F32 = jnp.float32
VMEM = pl.BlockSpec(memory_space=pltpu.VMEM)
HBM = pl.BlockSpec(memory_space=pltpu.HBM)
CONTRACT_ROWS = (((0,), (0,)), ((), ()))


def params(mebibytes):
    return pltpu.CompilerParams(vmem_limit_bytes=mebibytes << 20)


def one_hot(condition):
    return jnp.where(condition, 1.0, 0.0).astype(BF16)


def side_by_side(field_ref):
    return jnp.concatenate([field_ref[l] for l in range(field_ref.shape[0])], axis=1)


def outgoing_kernel(
    send_hbm, field_hbm, length_hbm, wave_hbm, donor_hbm, tile_hbm, kernels_hbm,
    far_ref, near_ref, field_ref, lengths_ref, wave_ref, donor_ref, tile_ref, kernels_ref,
    send_ref, length_ref, sems,
):
    pairs = (
        (send_hbm, send_ref), (field_hbm, field_ref), (length_hbm, length_ref), (wave_hbm, wave_ref),
        (donor_hbm, donor_ref), (tile_hbm, tile_ref), (kernels_hbm, kernels_ref),
    )
    copies = [pltpu.make_async_copy(*pair, sems.at[i]) for i, pair in enumerate(pairs)]
    for copy in copies:
        copy.start()
    band = lax.axis_index("lat")
    even = lax.rem(band, 2) == 0
    blocks, count = field_ref.shape[1], send_ref.shape[2]
    rows = lax.broadcasted_iota(jnp.int32, (blocks, count), 0)
    copies[0].wait()
    below, above = send_ref[0, 0:1, :], send_ref[0, 1:2, :]
    far_hot = jnp.transpose(jnp.where(rows == jnp.where(even, below, above), 1.0, 0.0)).astype(BF16)
    near_hot = jnp.transpose(jnp.where(rows == jnp.where(even, above, below), 1.0, 0.0)).astype(BF16)
    copies[1].wait()
    own = side_by_side(field_ref)
    for ref, hot in ((far_ref, far_hot), (near_ref, near_hot)):
        picked = jnp.dot(hot, own, preferred_element_type=F32)
        ref[...] = picked.astype(BF16)
    copies[2].wait()
    circles = lengths_ref.shape[0] // 2
    for i in range(2 * circles):
        length = length_ref[band * circles + i % circles]
        lengths_ref[i : i + 1] = jnp.full((1, LANES), length, jnp.int32)
    for copy in copies[3:]:
        copy.wait()


SINE = (0.07761395, -0.59827207, 2.55007494, -5.16770998, 3.14159264)
COSINE = (0.21953804, -1.33180992, 4.05840238, -4.93479245, 0.99999995)


def turn(steps, waves, length, inverse):
    phase = steps * waves
    rest = phase - jnp.floor(phase * inverse + 0.5) * length
    f = rest * inverse
    x = f * f
    s, c = SINE[0], COSINE[0]
    for p, q in zip(SINE[1:], COSINE[1:]):
        s, c = s * x + p, c * x + q
    s = s * f
    twice = s + s
    return 1.0 - twice * s, twice * c


def log(n):
    return n.bit_length() - 1


def times(a, b):
    return a[0] * b[0] - a[1] * b[1], a[0] * b[1] + a[1] * b[0]


def folded_order(array, coarse):
    half, count = coarse // 2, coarse // 8
    assert coarse % 8 == 0 and half % 8 == 4
    sub = lax.broadcasted_iota(jnp.int32, (8, array.shape[1]), 0)

    def reverse(v):
        v = pltpu.roll(v, 4, 0)
        for h in (2, 1):
            v = jnp.where((sub & h) == 0, pltpu.roll(v, 8 - h, 0), pltpu.roll(v, h, 0))
        return v

    out = []
    for begin in range(0, array.shape[0], coarse):
        rows = [array[begin + 8 * i : begin + 8 * i + 8] for i in range(count)]
        swapped = {i: pltpu.roll(rows[i], 4, 0) for i in range(half // 8, count)}
        for i in range(count):
            q = (8 * i + half) // 8
            if 8 * i + 8 <= half:
                out.append(jnp.where(sub < 4, swapped[q], swapped[q + 1]))
            elif 8 * i < half:
                out.append(jnp.where(sub < 4, swapped[q], reverse(rows[count - 1 - i])))
            else:
                out.append(reverse(rows[count - 1 - i]))
    return jnp.concatenate(out, axis=0)


def table_kernel(
    lengths_ref, wave_ref, field_ref, donor_ref, tile_ref, kernels_ref, slot_hbm,
    fine_ref, coarse_ref, limits_ref, far_choice_ref, near_choice_ref, arrival_ref, order_ref,
    slot_ref, sem, *, lat, lev,
):
    circles, tiles = fine_ref.shape[:2]
    levels, blocks, _ = field_ref.shape
    coarse = blocks // circles
    half = coarse // 2
    fetch = pltpu.make_async_copy(slot_hbm, slot_ref, sem)
    fetch.start()
    row = lax.broadcasted_iota(jnp.int32, (8, LANES), 0)
    near_step = (row + LANES // 2 * (coarse - 1)).astype(F32)
    far_step = (row * LANES + LANES // 2).astype(F32)
    hop_step = jnp.where((row & 1) == 0, 8, 8 * LANES).astype(F32)
    group = 4 if circles % 4 == 0 else 1

    def stepped(base, hop, groups):
        out = [base, times(base, hop)]
        twice = hop[0] + hop[0]
        while len(out) < groups:
            out.append(tuple(twice * x - y for x, y in zip(out[-1], out[-2])))
        return [jnp.concatenate(part, axis=0) for part in zip(*out[:groups])]

    def lengths_of(first):
        each = [
            jnp.broadcast_to(lengths_ref[pl.ds(first + i, 1)], (8, LANES)) for i in range(group)
        ]
        mixed = each[0]
        for i in range(1, group):
            mixed = jnp.where(row >= 2 * i, each[i], mixed)
        return [(x.astype(F32), 1.0 / x.astype(F32)) for x in (*each, mixed)]

    def table(first, t, scales):
        waves = jnp.broadcast_to(wave_ref[pl.ds(t, 1), :], (8, LANES)).astype(F32)
        hops = turn(hop_step, waves, *scales[group])
        for i in range(group):
            near_hop, far_hop = (
                tuple(jnp.broadcast_to(x[k : k + 1], (8, LANES)) for x in hops)
                for k in (2 * i, 2 * i + 1)
            )
            fine = stepped(turn(near_step, waves, *scales[i]), near_hop, LANES // 8)
            fine_ref[first + i, t] = jnp.concatenate(fine, axis=1).astype(BF16)
            wide = stepped(turn(far_step, waves, *scales[i]), far_hop, -(-half // 8))
            coarse_ref[first + i, t] = jnp.concatenate(
                [jnp.concatenate([part[:half]] * levels, axis=0) for part in wide], axis=1
            )

    def looped(index, _):
        first = index // tiles * group
        table(first, lax.rem(index, tiles), lengths_of(first))
        return 0

    listed = jnp.concatenate(
        [donor_ref[...], tile_ref[...], jnp.zeros((4, blocks), jnp.int32)], axis=0
    )
    columns = folded_order(jnp.transpose(listed.astype(F32)), coarse)
    own = side_by_side(field_ref)
    kinds = kernels_ref.shape[0]
    count = far_choice_ref.shape[1] // kinds
    even = lax.rem(lax.axis_index("lat"), 2) == 0
    lane = lax.broadcasted_iota(jnp.int32, (blocks, blocks), 1).astype(F32)
    entry = lax.broadcasted_iota(jnp.int32, far_choice_ref.shape, 1).astype(F32)
    far_choice, near_choice, picked, kind = [], [], [], []
    for k in range(2):
        donor = columns[:, k : k + 1]
        tile = columns[:, 2 + k : 3 + k]
        place = donor - float(blocks)
        above = place >= float(count)
        code = jnp.where(above, place - float(count), place) + float(count) * tile
        code = jnp.where(place >= 0.0, code, -1.0)
        is_far = jnp.logical_xor(above, even)
        far_choice.append(jnp.where(entry == jnp.where(is_far, code, -1.0), 1.0, 0.0))
        near_choice.append(jnp.where(entry == jnp.where(is_far, -1.0, code), 1.0, 0.0))
        picked.append(
            jnp.dot(one_hot(lane == donor), own, preferred_element_type=F32).astype(BF16)
        )
        kind.append(jnp.broadcast_to(tile, (blocks, LANES)))
    far_choice_ref[...] = (far_choice[0] + far_choice[1]).astype(BF16)
    near_choice_ref[...] = (near_choice[0] + near_choice[1]).astype(BF16)
    stacked = jnp.concatenate([kernels_ref[k] for k in range(kinds)], axis=1)
    for l in range(levels):
        total = None
        for k in range(2):
            every = jnp.dot(
                picked[k][:, l * LANES : (l + 1) * LANES], stacked, preferred_element_type=F32
            )
            value = every[:, :LANES]
            for q in range(1, kinds):
                value = jnp.where(kind[k] == float(q), every[:, q * LANES : (q + 1) * LANES], value)
            total = value if k == 0 else total + value
        arrival_ref[:, l * LANES : (l + 1) * LANES] = total

    if circles * tiles <= 64:
        for first in range(0, circles, group):
            scales = lengths_of(first)
            for t in range(tiles):
                table(first, t, scales)
    else:
        lax.fori_loop(0, circles // group * tiles, looped, 0)

    fetch.wait()
    slots = limits_ref.shape[0]
    first = (lax.axis_index("lat") * lev + lax.axis_index("lev")) * slots
    for s in range(slots):
        limits_ref[s : s + 1] = jnp.full((1, LANES), slot_ref[first + s], jnp.int32)

    total = order_ref.shape[0]
    if total == lat * lev * 2 * circles:
        at = lax.broadcasted_iota(jnp.int32, (8, total), 1)
        outer = (at >> log(circles)) & (lat - 1)
        group = at >> log(lat * circles)
        source = (outer << log(circles * 2 * lev)) | (group << log(circles)) | (at & (circles - 1))
        row = lax.broadcasted_iota(jnp.int32, (total, total), 0)
        order_ref[...] = one_hot(row == source[0:1])
    else:
        order_ref[...] = jnp.zeros(order_ref.shape, BF16)


def fold(parts):
    row = lax.broadcasted_iota(jnp.int32, (8, LANES), 0)
    for half in (4, 2, 1):
        low = (row & half) == 0
        count = len(parts) // 2
        parts = [
            jnp.where(low, a, pltpu.roll(b, half, 0)) + jnp.where(low, pltpu.roll(a, 8 - half, 0), b)
            for a, b in zip(parts[:count], parts[count:])
        ]
    return parts[0]


def from_halo(halo, kernels_ref, choice):
    kinds = kernels_ref.shape[0]
    count, levels = halo.shape[0], halo.shape[1] // LANES
    stacked = jnp.concatenate([kernels_ref[k] for k in range(kinds)], axis=1)
    rows = jnp.concatenate(
        [halo[:, l * LANES : (l + 1) * LANES] for l in range(levels)], axis=0
    )
    every = jnp.dot(rows, stacked, preferred_element_type=F32)
    every = jnp.concatenate(
        [
            jnp.concatenate(
                [every[l * count : (l + 1) * count, q * LANES : (q + 1) * LANES] for q in range(kinds)],
                axis=0,
            )
            for l in range(levels)
        ],
        axis=1,
    )
    high = every.astype(BF16)
    low = (every - high.astype(F32)).astype(BF16)
    return jnp.dot(choice, high, preferred_element_type=F32) + jnp.dot(
        choice, low, preferred_element_type=F32
    )


def far_kernel(far_ref, choice_ref, kernels_ref, own_ref, arrival_ref):
    band = lax.axis_index("lat")
    at_end = (band == 0) | (band == lax.axis_size("lat") - 1)
    far = far_ref[...]
    far = jnp.where(at_end, jnp.zeros_like(far), far)
    arrival_ref[...] = own_ref[...] + from_halo(far, kernels_ref, choice_ref[...])


def transform_kernel(
    lengths_ref, wave_ref, near_ref, choice_ref, arrival_ref, kernels_ref, fine_ref,
    coarse_ref, out_ref, points_ref, coeff_ref, *, top_wave,
):
    blocks = arrival_ref.shape[0]
    levels = arrival_ref.shape[1] // LANES
    circles, tiles = fine_ref.shape[:2]
    coarse = blocks // circles
    half = coarse // 2
    arrival = arrival_ref[...] + from_halo(near_ref[...], kernels_ref, choice_ref[...])

    distance = lax.broadcasted_iota(jnp.int32, (coarse, LANES), 0)
    row = jnp.where(distance < half, distance + half, coarse - 1 - distance)
    position = row * LANES + lax.broadcasted_iota(jnp.int32, (coarse, LANES), 1)
    unrolled = circles * tiles <= 64
    points = []
    for g in range(circles):
        inside = position < jnp.broadcast_to(lengths_ref[g : g + 1], (coarse, LANES))
        sums, differences = [], []
        for l in range(levels):
            rows = slice(g * coarse, (g + 1) * coarse)
            part = arrival[rows, l * LANES : (l + 1) * LANES]
            part = jnp.where(inside, part * part, 0.0)
            sums.append(part[:half] + part[half:])
            differences.append(part[:half] - part[half:])
        points.append(jnp.concatenate(sums + differences, axis=0).astype(BF16))
        if not unrolled:
            points_ref[g] = points[g]

    height = 2 * circles
    lengths = lengths_ref[...]
    sine = lax.broadcasted_iota(jnp.int32, (height, LANES), 0) >= circles
    sub = lax.broadcasted_iota(jnp.int32, (8, LANES), 0)

    def level_sum(value, l):
        first, last = l * half, (l + 1) * half
        total = None
        for at in range(first // 8 * 8, last, 8):
            piece = value[at : at + 8]
            if at < first:
                piece = jnp.where(sub >= first - at, piece, 0.0)
            if at + 8 > last:
                piece = jnp.where(sub < last - at, piece, 0.0)
            total = piece if total is None else total + piece
        return total

    def tile(t):
        sums = [([], []) for _ in range(levels)]
        for g in range(circles):
            rows = points[g] if unrolled else points_ref[g]
            turned = jnp.dot(rows, fine_ref[g, t], preferred_element_type=F32)
            both, apart = turned[: levels * half], turned[levels * half :]
            c, s = coarse_ref[g, t, :, :LANES], coarse_ref[g, t, :, LANES:]
            real = both[:, :LANES] * c - apart[:, LANES:] * s
            imag = both[:, LANES:] * c + apart[:, :LANES] * s
            for l in range(levels):
                sums[l][0].append(level_sum(real, l))
                sums[l][1].append(level_sum(imag, l))
        waves = jnp.broadcast_to(wave_ref[pl.ds(t, 1), :], (height, LANES))
        live = (waves >= 1) & (waves < top_wave) & (2 * waves < lengths)
        found = []
        for l in range(levels):
            ordered = sums[l][0] + sums[l][1]
            rows = [fold(ordered[i : i + 8]) for i in range(0, height, 8)]
            rows = jnp.concatenate(rows, axis=0)
            found.append(jnp.where(live, jnp.where(sine, -rows, rows), 0.0))
        return jnp.concatenate(found, axis=0)

    def stored(t, _):
        coeff_ref[t] = tile(t)
        return 0

    devices, chunk_rows, _ = out_ref.shape
    width = tiles * LANES // devices
    packs = coeff_ref.shape[1] // chunk_rows
    step = LANES // packs
    lane = lax.broadcasted_iota(jnp.int32, (chunk_rows, LANES), 1)
    if unrolled:
        coeffs = [tile(t) for t in range(tiles)]
    else:
        lax.fori_loop(0, tiles, stored, 0)
        coeffs = [coeff_ref.at[t] for t in range(tiles)]
    for d in range(devices):
        t, shift = divmod(d * width, LANES)
        chunk = jnp.zeros((chunk_rows, LANES), F32)
        for p in range(packs):
            rows = slice(p * chunk_rows, (p + 1) * chunk_rows)
            at = p * step
            value = pltpu.roll(coeffs[t][rows], (at - shift) % LANES, 1)
            if shift + width > LANES:
                after = pltpu.roll(coeffs[t + 1][rows], (at - shift) % LANES, 1)
                value = jnp.where(lane < at + LANES - shift, value, after)
            chunk = value if p == 0 else jnp.where(lane < at, chunk, value)
        out_ref[d] = chunk.astype(BF16)


def legendre_kernel(limits_ref, arrived_ref, order_ref, legendre_ref, out_hbm, out_ref, sems, *, packs):
    outputs, slots, top_wave = out_ref.shape
    circles = legendre_ref.shape[0] // slots
    per_tile = LANES // circles
    total = arrived_ref.shape[0]
    turned = lax.dot_general(
        arrived_ref[...], order_ref[...], CONTRACT_ROWS, preferred_element_type=F32
    )

    sub = lax.broadcasted_iota(jnp.int32, (8, LANES), 0)
    block = lax.broadcasted_iota(jnp.int32, (8, LANES), 1) >> log(circles)
    chosen = [(block == b) & ((sub & (per_tile - 1)) == b) for b in range(per_tile)]
    halves = 8 // per_tile
    in_half = [(sub >> log(per_tile)) == h for h in range(halves)]
    step = LANES // packs
    spread = []
    for k in range(slots // 8):
        pieces = [None] * outputs
        for l in range(packs):
            for j in range(total // LANES):
                at = l * step + 8 * k
                v = turned[at : at + 8, j * LANES : (j + 1) * LANES]
                rolled = [v] + [pltpu.roll(v, circles * d, 1) for d in range(1, per_tile)]
                for i in range(per_tile):
                    a = jnp.zeros((8, LANES), F32)
                    for b in range(per_tile):
                        a = jnp.where(chosen[b], rolled[(b - i) % per_tile], a)
                    group_lev, part = divmod(j * per_tile + i, 2)
                    pieces[(group_lev * packs + l) * 2 + part] = jnp.concatenate(
                        [jnp.where(in_half[h], a, 0.0) for h in range(halves)], axis=1
                    )
        spread.append(jnp.concatenate(pieces, axis=0).astype(BF16))

    wide = 2 * LANES
    lane = lax.broadcasted_iota(jnp.int32, (8, wide), 1)
    limits = [limits_ref[8 * k : 8 * k + 8] for k in range(slots // 8)]
    limits = [jnp.concatenate([m, m], axis=1) for m in limits]
    def products(n):
        return [
            jnp.dot(
                spread[k],
                legendre_ref[8 * k * circles : 8 * (k + 1) * circles, n : n + wide],
                preferred_element_type=F32,
            )
            for k in range(slots // 8)
        ]

    copies = []
    later = products(0)
    for n in range(0, top_wave, wide):
        sums, later = later, products(n + wide) if n + wide < top_wave else None
        keep = [lane + n >= m for m in limits]
        for o in range(outputs):
            out_ref[o, :, n : n + wide] = jnp.concatenate(
                [jnp.where(keep[k], sums[k][8 * o : 8 * o + 8], 0.0) for k in range(slots // 8)],
                axis=0,
            ).astype(BF16)
        columns = (slice(None), slice(None), pl.ds(n, wide))
        copies.append(
            pltpu.make_async_copy(
                out_ref.at[columns], out_hbm.at[columns], sems.at[n // wide]
            )
        )
        copies[-1].start()
    for copy in copies:
        copy.wait()


def other_neighbours(lat, lev):
    inner = [(i, i + 1) for i in range(1, lat - 1, 2)]
    inner += [(j, i) for i, j in inner]
    pairs = [(i * lev + l, j * lev + l) for i, j in inner for l in range(lev)]
    return pairs + [(i * lev + l, i * lev + (l ^ 1)) for i in (0, lat - 1) for l in range(lev)]


def body(
    grid_field, send_blocks, donor_index, tile_choice, kernel_tiles, circle_len, slot_wave, legendre
):
    levels, blocks, _ = grid_field.shape
    send_count = send_blocks.shape[2]
    slots, circles, top_wave = legendre.shape
    lat, lev = lax.axis_size("lat"), lax.axis_size("lev")
    devices = lat * lev
    coarse = PTS // LANES
    own = blocks // coarse
    tiles = slot_wave.shape[0] // LANES
    waves = slot_wave.reshape(tiles, LANES)

    def like(x):
        return jax.ShapeDtypeStruct(x.shape, x.dtype)

    def in_hbm(x):
        return pltpu.with_memory_space_constraint(x, pltpu.HBM)

    halo = jax.ShapeDtypeStruct((send_count, levels * LANES), BF16)
    donors, kinds = donor_index.T, tile_choice.T
    to_far, to_near, field, lengths, waves, donors, kinds, kernels = pl.pallas_call(
        outgoing_kernel,
        out_shape=(
            halo, halo, like(grid_field), jax.ShapeDtypeStruct((2 * own, LANES), jnp.int32),
            like(waves), like(donors), like(kinds), like(kernel_tiles),
        ),
        in_specs=[HBM] * 7, out_specs=(VMEM,) * 8,
        scratch_shapes=[
            pltpu.VMEM(send_blocks.shape, jnp.int32),
            pltpu.SMEM(circle_len.shape, jnp.int32),
            pltpu.SemaphoreType.DMA((7,)),
        ],
        compiler_params=params(4), name="outgoing",
    )(
        *map(in_hbm, (send_blocks, grid_field, circle_len, waves, donors, kinds, kernel_tiles))
    )
    near = lax.ppermute(to_near, "lat", [(i, i ^ 1) for i in range(lat)])
    far = lax.ppermute(to_far, ("lat", "lev"), other_neighbours(lat, lev))

    direct = levels == 2 and 2 * own == 8 and 4 * circles == LANES and slots % 8 == 0
    direct = direct and 2 * slots <= LANES and lev & (lev - 1) == 0
    total = devices * 2 * own if direct else 16
    entries = own * tiles * (LANES + coarse) * 2 * LANES
    choice = jax.ShapeDtypeStruct((blocks, kernel_tiles.shape[0] * send_count), BF16)
    arrival = jax.ShapeDtypeStruct((blocks, levels * LANES), F32)
    fine, wide, limits, far_choice, near_choice, own_part, order = pl.pallas_call(
        functools.partial(table_kernel, lat=lat, lev=lev),
        out_shape=(
            jax.ShapeDtypeStruct((own, tiles, LANES, 2 * LANES), BF16),
            jax.ShapeDtypeStruct((own, tiles, levels * coarse // 2, 2 * LANES), F32),
            jax.ShapeDtypeStruct((slots, LANES), jnp.int32),
            choice,
            choice,
            arrival,
            jax.ShapeDtypeStruct((total, total), BF16),
        ),
        in_specs=[VMEM] * 6 + [HBM], out_specs=(VMEM,) * 7,
        scratch_shapes=[
            pltpu.SMEM(slot_wave.shape, jnp.int32),
            pltpu.SemaphoreType.DMA,
        ],
        compiler_params=params(32), name="tables",
        cost_estimate=pl.CostEstimate(flops=8 * entries, bytes_accessed=3 * entries, transcendentals=0),
    )(lengths, waves, field, donors, kinds, kernels, in_hbm(slot_wave))

    rows = levels * 2 * own
    packs = 1
    while rows % (16 * packs) == 0 and 2 * packs * slots <= LANES:
        packs *= 2
    arrival = pl.pallas_call(
        far_kernel, out_shape=arrival, in_specs=[VMEM] * 4, out_specs=VMEM,
        compiler_params=params(8), name="far_part",
    )(far, far_choice, kernels, own_part)
    coeffs = pl.pallas_call(
        functools.partial(transform_kernel, top_wave=top_wave),
        out_shape=jax.ShapeDtypeStruct((devices, rows // packs, LANES), BF16),
        in_specs=[VMEM] * 8, out_specs=VMEM,
        scratch_shapes=[
            pltpu.VMEM((own, levels * coarse, LANES), BF16),
            pltpu.VMEM((tiles, rows, LANES), F32),
        ],
        compiler_params=params(40), name="transform",
    )(lengths, waves, near, near_choice, arrival, kernels, fine, wide)
    arrived = lax.all_to_all(coeffs, ("lat", "lev"), 0, 0, tiled=True)

    outputs = lev * levels * 2
    height = rows // packs
    if direct:
        spectra = pl.pallas_call(
            functools.partial(legendre_kernel, packs=packs),
            out_shape=jax.ShapeDtypeStruct((outputs, slots, top_wave), BF16),
            in_specs=[VMEM] * 4, out_specs=HBM,
            scratch_shapes=[
                pltpu.VMEM((outputs, slots, top_wave), BF16),
                pltpu.SemaphoreType.DMA((top_wave // (2 * LANES),)),
            ],
            compiler_params=params(32), name="legendre",
        )(
            limits,
            arrived.reshape(devices * height, LANES),
            order,
            legendre.reshape(slots * circles, top_wave),
        )
        return spectra.reshape(outputs // 2, 2, slots, top_wave)

    gathered = arrived.reshape(lat, lev, height, packs, LANES // packs)[..., :slots]
    gathered = gathered.swapaxes(2, 3).reshape(lat, lev, levels, 2, own, slots)
    gathered = gathered.transpose(1, 2, 3, 0, 4, 5).reshape(outputs // 2, 2, circles, slots)
    spectra = jnp.einsum("lcgs,sgn->lcsn", gathered, legendre, preferred_element_type=F32)
    first_slot = (lax.axis_index("lat") * lev + lax.axis_index("lev")) * slots
    mine = lax.dynamic_slice_in_dim(slot_wave, first_slot, slots)
    allowed = jnp.arange(top_wave, dtype=jnp.int32)[None, :] >= mine[:, None]
    return jnp.where(allowed[None, None], spectra, 0.0).astype(BF16)


def solution(mesh):
    return jax.shard_map(
        body,
        mesh=mesh,
        in_specs=(
            P("lev", "lat", None),
            P("lat", None, None),
            P("lat", None),
            P("lat", None),
            P(),
            P(),
            P(),
            P(("lat", "lev"), None, None),
        ),
        out_specs=P(None, None, ("lat", "lev"), None),
        check_vma=False,
    )
```
